512 devices in a mesh: grp: 32 (over x, y), tp: 16 (over z, core).
Axes of the slice: x: 4, y: 8, z: 8, core: 2. Of those that a mesh axis runs over, the one named last changes fastest.
Arguments:
- activations: bfloat16 [8192, 8192], P('grp', 'tp'), may hold values from -6 to 6
- kv_weight: bfloat16 [8192, 2048], P(None, 'tp'), may hold values from -0.0625 to 0.0625
- store_down: bfloat16 [32, 8192, 128], P(None, ('tp', 'grp')), may hold values from -0.0625 to 0.0625
- store_up: bfloat16 [32, 128, 2048], P(None, 'grp', 'tp'), may hold values from -0.375 to 0.375
- block_home: int32 [32], replicated, may hold values from 0 to 31, each once
- group_variants: int32 [32, 4], replicated, may hold values from 0 to 15, as said below
- row_variant: int32 [8192, 1], P('grp'), may hold values from 0 to 3; in each aligned block of 256 rows (0 to 255, 256 to 511, ...) at most 192 rows name the same one
Outputs:
- kv_out: bfloat16 [8192, 2048], P('grp', 'tp')
The draws below stay inside these ranges and needn't reach their ends.
Inputs may be any that keep to these rules, and one draw needn't show every extreme that they name: `group_variants`: each row lists 4 different variants; every variant is listed by some group. `row_variant`: among the tokens of one group no position is named by more than 192 tokens.
All inputs are finite; a program needn't handle non-finite values.
Results may differ from the reference program's by a relative error of at most 0.014.
Values may be sent and summed in bfloat16 or wider, within the bound.
A program may use at most 64 MiB of HBM per device.

```python
import math
import jax
import jax.numpy as jnp
import numpy as np
from jax import lax

D = 8192
KVW = 2048
R = 256
NV = 16
PIECES = 2
VPG = 4
TOK_DEV = 256
CAP = 192
RB = 128
NBLK = 32
GROUPS = 32
TOKENS = 8192


def draw_group_variants(key, part):
    key = jax.random.fold_in(key, 11)
    key_rank, key_noise, key_order = jax.random.split(key, 3)
    popularity = jax.random.permutation(key_rank, NV)
    noise = jax.random.randint(key_noise, (GROUPS, NV), 0, 1024)
    score = noise // (popularity[None, :] + 1)
    order = jax.random.permutation(key_order, NV)
    placed = jnp.argsort(order, stable=True)
    group_ids = jnp.arange(GROUPS, dtype=jnp.int32)[:, None]
    columns = jnp.arange(NV, dtype=jnp.int32)[None, :]
    covered = jnp.logical_and(group_ids < NV // VPG, placed[None, :] // VPG == group_ids)
    score = score + covered.astype(jnp.int32) * 4096
    score = score * NV + columns
    _, picked = lax.top_k(score, VPG)
    return picked.astype(jnp.int32)


def levels(rng, shape, cuts, low, top_value):
    loudness = 1.0
    for dim, blocks in cuts:
        heights = jax.random.uniform(jax.random.fold_in(jax.random.fold_in(rng, 6), dim), (blocks,), jnp.float32, low / len(cuts), top_value / len(cuts))
        loudness = loudness * jnp.repeat(jnp.exp(heights), shape[dim] // blocks).reshape((-1,) + (1,) * (len(shape) - 1 - dim))
    return loudness


def routed_block(rng, own, number, rows, count, top, most, skew):
    sequence = jax.random.permutation(rng, count)
    packed, common = load_shares(count, rows * top, most, skew, True), load_shares(count, rows * top, most, skew, False)
    places = jnp.arange(count)

    def named(lengths, rotation):
        used = int((lengths > 0).sum())
        fixed = max(1, used // 4)
        passed = fixed + (places - fixed + rotation * (used - fixed)) % max(1, count - fixed)
        return jnp.zeros((count,), jnp.int32).at[sequence[jnp.where(places < fixed, places, passed)]].set(jnp.asarray(lengths, jnp.int32))

    lengths = jnp.where(number % 4 == 0, named(packed, number // 4), named(common, number - number // 4 - 1))
    mixed = jax.random.permutation(jax.random.fold_in(own, 3), count)
    source_of, sink = mixed[0:count // 2 * 2:2], mixed[1:count // 2 * 2:2]
    margin = jnp.minimum(lengths[source_of] - 1, most - lengths[sink]) // 2
    margin = jnp.where((source_of == sequence[0]) | (sink == sequence[0]) | (lengths[sink] == 0), 0, jnp.maximum(margin, 0))
    passed = jax.random.randint(jax.random.fold_in(own, 4), (count // 2,), 0, 1 << 20) % (margin + 1)
    lengths = lengths.at[source_of].add(-passed).at[sink].add(passed)
    members = jnp.searchsorted(jnp.cumsum(lengths), jnp.arange(rows * top), side="right").astype(jnp.int32)
    listing = members.reshape(top, rows).T
    listing = listing[jax.random.permutation(jax.random.fold_in(own, 1), rows)]
    rotation = jax.random.randint(jax.random.fold_in(own, 2), (rows, 1), 0, top)
    return jnp.take_along_axis(listing, (jnp.arange(top)[None, :] + rotation) % top, axis=1)


def load_shares(count, total, limit, slope, full):
    loads = [(1 << 20) // math.isqrt(grade ** slope) + 1 for grade in range(1, count + 1)]
    largest = limit if full else min(limit, max(-(-total // count), total * loads[0] // sum(loads)))
    least = 1 if total - largest >= count - 1 else 0
    counts, surplus = [largest] + [least] * (count - 1), total - largest - least * (count - 1)
    while surplus > 0:
        free = [i for i in range(1, count) if counts[i] < largest] or [i for i in range(1, count) if counts[i] < limit]
        whole, remaining = sum([loads[i] for i in free]), surplus
        for i in free:
            more = min(limit - counts[i], max(1, remaining * loads[i] // whole), surplus)
            counts[i] = counts[i] + more
            surplus = surplus - more
    return np.array(counts)


def gaussian(key, extent, width, most, cuts=(), kind=jnp.bfloat16):
    level = levels(key, extent, cuts, -0.22, 0.18) if cuts else 1.0
    drawn = jax.random.normal(key, extent, jnp.float32) * width * level
    return jnp.minimum(jnp.maximum(drawn, -most), most).astype(kind)


def setup_inputs(seed: int = 0) -> dict:
    key_list = jax.random.split(jax.random.key(seed), 8)
    activations = gaussian(key_list[0], (TOKENS, D), 1.0, 6.0, ((0, 32), (1, 16)))
    kv_weight = gaussian(key_list[1], (D, KVW), D ** -0.5, 0.0625, ((1, 16),))
    store_down = gaussian(key_list[2], (NBLK, D, RB), D ** -0.5, 0.0625, ((1, 512),))
    store_up = gaussian(key_list[3], (NBLK, RB, KVW), R ** -0.5, 0.375, ((1, 32), (2, 16)))
    block_home = jax.random.permutation(key_list[4], NBLK).astype(jnp.int32)
    group_variants = draw_group_variants(jax.random.fold_in(key_list[7], 71), 0)
    row_variant_keys = jax.random.split(jax.random.fold_in(key_list[6], 1), TOKENS // TOK_DEV)
    row_variant_turns = jax.random.permutation(jax.random.fold_in(key_list[6], 3), TOKENS // TOK_DEV)
    row_variant = jax.vmap(lambda own, number: routed_block(jax.random.fold_in(key_list[6], 2), own, number, TOK_DEV, VPG, 1, CAP, 2))(row_variant_keys, row_variant_turns).reshape((TOKENS, 1))
    return dict(activations=activations, kv_weight=kv_weight, store_down=store_down, store_up=store_up, block_home=block_home, group_variants=group_variants, row_variant=row_variant)


def reference(activations, kv_weight, store_down, store_up, block_home, group_variants, row_variant):
    block_ids = jnp.arange(NV, dtype=jnp.int32)[:, None] * PIECES + jnp.arange(PIECES, dtype=jnp.int32)[None, :]
    slot_table = block_home[block_ids]
    down_table = store_down[slot_table]
    up_table = store_up[slot_table]

    def one_group(group_number):
        group_rows = lax.dynamic_slice_in_dim(activations, group_number * TOK_DEV, TOK_DEV, 0)
        chosen = lax.dynamic_slice_in_dim(row_variant, group_number * TOK_DEV, TOK_DEV, 0)[:, 0]
        listed = group_variants[group_number]
        down_need = down_table[listed]
        up_need = up_table[listed].reshape(VPG, R, KVW)
        base_out = jnp.dot(group_rows, kv_weight, preferred_element_type=jnp.float32)
        shrunk_all = jnp.einsum("td,vpdr->tvpr", group_rows.astype(jnp.float32), down_need.astype(jnp.float32))
        shrunk_all = shrunk_all.reshape(TOK_DEV, VPG, R)
        picker = (chosen[:, None] == jnp.arange(VPG, dtype=jnp.int32)[None, :]).astype(jnp.float32)
        shrunk = jnp.sum(shrunk_all * picker[:, :, None], axis=1)
        shrunk_bf = shrunk.astype(jnp.bfloat16)
        expanded = jnp.einsum("tr,vrk->tvk", shrunk_bf.astype(jnp.float32), up_need.astype(jnp.float32))
        delta_out = jnp.sum(expanded * picker[:, :, None], axis=1)
        return (base_out + delta_out).astype(jnp.bfloat16)

    result = lax.map(one_group, jnp.arange(GROUPS, dtype=jnp.int32))
    return result.reshape(TOKENS, KVW)
```

```python
import functools

import jax
import jax.numpy as jnp
from jax import lax
from jax.experimental import pallas as pl
from jax.experimental.pallas import tpu as pltpu
from jax.sharding import PartitionSpec as P

PIECES = 2
VPG = 4
SLOTS = PIECES * VPG
MESH = pl.DeviceIdType.MESH
F32 = jnp.float32
BF16 = jnp.bfloat16


class Ring:
    def __init__(self, buf, pieces, peers, send, recv):
        self.buf, self.pieces, self.peers = buf, pieces, peers
        self.send, self.recv = send, recv
        self.n = buf.shape[0]
        self.half = self.n // 2
        self.size = buf.shape[1] // pieces

    def events(self):
        for hop in range(1, self.half):
            for index in range(self.pieces):
                yield hop, index
        yield self.half, 0

    def cut(self, way, hop, index):
        if hop == self.half:
            size = self.buf.shape[1] // 2
            return pl.ds(way * size, size)
        piece = index if way == 0 else self.pieces - 1 - index
        return pl.ds(piece * self.size, self.size)

    def slot(self, way, hop):
        return hop % self.n if way == 0 else (self.n - hop) % self.n

    def copy(self, way, hop, index):
        cut = self.cut(way, hop, index)
        return pltpu.make_async_remote_copy(
            src_ref=self.buf.at[self.slot(way, hop - 1), cut],
            dst_ref=self.buf.at[self.slot(way, hop), cut],
            send_sem=self.send.at[way, hop - 1, index],
            recv_sem=self.recv.at[way, hop - 1, index],
            device_id=self.peers[way],
            device_id_type=MESH,
        )

    def start(self):
        for index in range(self.pieces):
            for way in range(2):
                self.copy(way, 1, index).start()

    def advance(self, hop, index):
        for way in range(2):
            self.copy(way, hop, index).wait_recv()
            if hop + 1 < self.half or (hop + 1 == self.half and index == 0):
                self.copy(way, hop + 1, index).start()

    def finish(self):
        for hop, index in self.events():
            for way in range(2):
                self.copy(way, hop, index).wait_send()


def kernel(
    nx, ny, nz,
    act, weight, down, up, home, served, var, out,
    abuf, wbuf, ybuf, ubuf, sel, xsend, xrelay, xrecv, usend, urecv, uother,
    acc, sums, sums_in, whole, parts, parts_in, shrunk, swap, swap_in, table, homes, lists, var_row, var_wide,
    chooser, opener,
    local_sem, z_send, z_recv, y_send, y_recv, u_send, u_recv, x_send, x_recv, v_send, v_recv,
    pair_send, pair_recv, a_send, a_recv, b_send, b_recv,
):
    grp, tp = lax.axis_index("grp"), lax.axis_index("tp")
    x, y = grp // ny, lax.rem(grp, ny)
    z, core = tp // 2, lax.rem(tp, 2)
    tokens = out.shape[0]
    cols = out.shape[1]
    groups = nx * ny
    far = 1 - 2 * core

    def at_x(step):
        return (lax.rem(x + step + nx, nx) * ny + y, tp)

    def at_y(step):
        return (x * ny + lax.rem(y + step + ny, ny), tp)

    def at_z(step):
        return (grp, lax.rem(z + step + nz, nz) * 2 + core)

    other = (grp, z * 2 + 1 - core)

    local = [
        pltpu.make_async_copy(home, homes, local_sem.at[4]),
        pltpu.make_async_copy(served, lists, local_sem.at[5]),
        pltpu.make_async_copy(down, ybuf.at[0], local_sem.at[1]),
        pltpu.make_async_copy(act, abuf.at[0], local_sem.at[0]),
        pltpu.make_async_copy(up, ubuf.at[0], local_sem.at[2]),
        pltpu.make_async_copy(var, var_row, local_sem.at[6]),
        pltpu.make_async_copy(weight.at[:, core], wbuf.at[:, :, pl.ds(0, cols)], local_sem.at[3]),
    ]
    for copy in local:
        copy.start()

    barrier = pltpu.get_barrier_semaphore()
    partners = [other, at_y(1), at_y(-1)] + [at_x(e) for e in range(1, nx)] + [at_z(e) for e in range(1, nz)]
    for partner in partners:
        pl.semaphore_signal(barrier, inc=1, device_id=partner, device_id_type=MESH)

    local[0].wait()
    local[1].wait()

    def fill(k, carry):
        owner = lax.rem(x + k // SLOTS, nx) * ny + y
        j = lax.rem(k, SLOTS)
        table[k] = homes[lists[j // PIECES, owner] * PIECES + lax.rem(j, PIECES)]
        return carry

    lax.fori_loop(0, nx * SLOTS, fill, 0)
    up_rows = up.shape[0] * up.shape[1]
    rank = xrecv.shape[3]

    def set_up():
        shape = chooser.shape
        line = lax.broadcasted_iota(jnp.int32, shape, 0)

        def pick(k, rows):
            return jnp.where((line >> 2) == k, table[k], rows)

        rows = lax.fori_loop(0, nx * SLOTS, pick, jnp.zeros(shape, jnp.int32), unroll=4)
        wanted = rows * 4 + (line & 3)
        chooser[...] = (wanted == lax.broadcasted_iota(jnp.int32, shape, 1)).astype(F32).astype(BF16)
        row = lax.broadcasted_iota(jnp.int32, opener.shape, 0)
        column = lax.broadcasted_iota(jnp.int32, opener.shape, 1)
        hit = (row == ((column >> 4) << 2) + (column & 3)) & (((column >> 2) & 1) == core)
        opener[...] = hit.astype(F32).astype(BF16)
        local[5].wait()
        for i in range(0, tokens, cols):
            size = min(cols, tokens - i)
            row = jnp.broadcast_to(var_row[:, pl.ds(i, size)], (cols, size))
            var_wide[pl.ds(i, size), :] = row.T

    pl.semaphore_wait(barrier, len(partners))

    zring = Ring(abuf, 2, (at_z(1), at_z(-1)), z_send, z_recv)
    yring = Ring(ybuf, 2, (at_y(1), at_y(-1)), y_send, y_recv)
    uring = Ring(ubuf, 1, (at_y(1), at_y(-1)), u_send, u_recv)

    def pair(index, src, dst):
        return pltpu.make_async_remote_copy(
            src_ref=src, dst_ref=dst, send_sem=pair_send.at[index], recv_sem=pair_recv.at[index],
            device_id=other, device_id_type=MESH,
        )

    local[2].wait()
    yring.start()
    local[3].wait()
    zring.start()
    weights = pair(0, weight.at[:, 1 - core], wbuf.at[:, :, pl.ds(cols, cols)])
    weights.start()

    def behind(d):
        return lax.rem(y - d + ny, ny)

    def hand(kind, d):
        mine = x * ny + behind(d)
        passed = lax.rem(x - far + nx, nx) * ny + behind(d)
        straight = d == ny // 2
        src, dst, peer = (
            (xsend.at[d, pl.ds(SLOTS, SLOTS)], xrecv.at[:, mine], at_x(1)),
            (xsend.at[d, pl.ds(3 * SLOTS, SLOTS)], xrecv.at[:, mine], at_x(-1)),
            (
                xsend.at[d, pl.ds(2 * SLOTS, SLOTS)],
                xrecv.at[:, mine] if straight else xrelay.at[d],
                at_x(2) if straight else at_x(far),
            ),
            (xrelay.at[d], xrecv.at[:, passed], at_x(far)),
        )[kind]
        return pltpu.make_async_remote_copy(
            src_ref=src, dst_ref=dst, send_sem=x_send.at[kind, d], recv_sem=x_recv.at[kind, d],
            device_id=peer, device_id_type=MESH,
        )

    def choose(d):
        sel[...] = ybuf[d]
        for e, kind in ((2, 2), (1, 0), (3, 1), (0, None)):

            def take(j, carry):
                xsend[d, e * SLOTS + j] = sel[table[e * SLOTS + j]]
                return carry

            lax.fori_loop(0, SLOTS, take, 0, unroll=True)
            if kind is not None:
                hand(kind, d).start()
        xrecv[:, x * ny + behind(d)] = xsend[d, pl.ds(0, SLOTS)]

    def relay(d):
        if d != ny // 2:
            hand(2, d).wait_recv()
            hand(3, d).start()

    def hand_up(e):
        return pltpu.make_async_remote_copy(
            src_ref=usend.at[e], dst_ref=urecv.at[:, x], send_sem=v_send.at[e - 1], recv_sem=v_recv.at[e - 1],
            device_id=at_x(e), device_id_type=MESH,
        )

    def choose_up(d):
        chosen = jnp.dot(chooser[...], ubuf[d].reshape(up_rows, cols), preferred_element_type=F32)
        chosen = chosen.astype(BF16).reshape(nx, 2, 16, cols)
        for e in range(nx):
            usend[e, :, behind(d)] = chosen[e]

    def multiply(slot, cut):
        home_z = lax.rem(z - slot + nz, nz)
        acc[cut, :] += jnp.dot(abuf[slot, cut, :], wbuf[home_z], preferred_element_type=F32)

    def z_step(event):
        zring.advance(*event)
        hop, index = event
        for way in range(2):
            multiply(zring.slot(way, hop), zring.cut(way, hop, index))

    z_events, y_events, u_events = (list(ring.events()) for ring in (zring, yring, uring))
    choose(0)
    set_up()

    def u_step(event):
        uring.advance(*event)
        for d in sorted({uring.slot(0, event[0]), uring.slot(1, event[0])}):
            choose_up(d)

    waiting = [0]
    last_y = len(y_events) - 1
    for number, (hop, index) in enumerate(y_events):
        yring.advance(hop, index)
        if number == max(last_y - 2, 0):
            local[4].wait()
            uring.start()
        if hop == yring.half or index == 1:
            ready = sorted({yring.slot(0, hop), yring.slot(1, hop)})
            for d in ready:
                choose(d)
            for d in waiting:
                relay(d)
            waiting = ready
        if number == 1:
            local[6].wait()
            weights.wait_recv()
            acc[...] = jnp.dot(abuf[0], wbuf[z], preferred_element_type=F32)
        if number % 2 == 1 and number // 2 < len(z_events) - 4:
            z_step(z_events[number // 2])
    for event in z_events[min(len(y_events) // 2, len(z_events) - 4):-3]:
        z_step(event)
    choose_up(0)
    u_step(u_events[0])

    for d in range(ny):
        for kind in (0, 1, 2 if d == ny // 2 else 3):
            hand(kind, d).wait_recv()
    depth = act.shape[1]
    mine = abuf[0]
    total = jnp.zeros((tokens, PIECES * rank), F32)
    who = jnp.concatenate([var_wide[:, pl.ds(0, rank)]] * PIECES, axis=1)
    for v in range(VPG):
        factor = jnp.concatenate([xrecv[v * PIECES + p].reshape(depth, rank) for p in range(PIECES)], axis=1)
        total = jnp.where(who == v, jnp.dot(mine, factor, preferred_element_type=F32), total)
    for p in range(PIECES):
        sums[p] = total[:, p * rank:(p + 1) * rank]
    first = pair(1, sums.at[1 - core], sums_in)
    first.start()
    if len(u_events) > 2:
        u_step(u_events[1])
    first.wait_recv()
    total = sums[core] + sums_in[...]
    whole[...] = total.reshape(nz, tokens // nz, rank)
    parts[...] = total.astype(BF16).reshape(nz, tokens // nz, rank)

    def scatter(e):
        return pltpu.make_async_remote_copy(
            src_ref=parts.at[lax.rem(z + e, nz)], dst_ref=parts_in.at[e - 1],
            send_sem=a_send.at[e - 1], recv_sem=a_recv.at[e - 1], device_id=at_z(e), device_id_type=MESH,
        )

    def spread(e):
        return pltpu.make_async_remote_copy(
            src_ref=shrunk.at[z], dst_ref=shrunk.at[z],
            send_sem=b_send.at[e - 1], recv_sem=b_recv.at[e - 1], device_id=at_z(e), device_id_type=MESH,
        )

    for e in range(1, nz):
        scatter(e).start()
    z_step(z_events[-3])
    for event in u_events[2 if len(u_events) > 2 else 1:]:
        u_step(event)
    for e in range(1, nx):
        hand_up(e).start()
    urecv[:, x] = usend[0]
    total = whole[z]
    for e in range(1, nz):
        scatter(e).wait_recv()
        total += parts_in[e - 1].astype(F32)
    shrunk[z] = total.astype(BF16)
    for e in range(1, nz):
        spread(e).start()

    for e in range(1, nx):
        hand_up(e).wait_recv()
    ups = pair(2, urecv, uother)
    ups.start()
    for event in z_events[-2:]:
        z_step(event)
    ups.wait_recv()

    wide = groups * 16
    for e in range(1, nz):
        spread(e).wait_recv()
    opened = jnp.dot(shrunk[...].reshape(tokens, rank), opener[...], preferred_element_type=F32)
    total = acc[...]
    who = jnp.concatenate([var_wide[:, pl.ds(0, min(cols, wide))]] * max(wide // cols, 1), axis=1)
    which = (lax.broadcasted_iota(jnp.int32, (1, wide), 1) >> 3) & 1
    for h in range(2):
        part = jnp.where(who == which + 2 * h, opened, 0.0).astype(BF16)
        factor = jnp.concatenate([urecv[h].reshape(wide, cols), uother[h].reshape(wide, cols)], axis=1)
        total += jnp.dot(part, factor, preferred_element_type=F32)
    mine, theirs = total[:, :cols], total[:, cols:]
    swap[...] = theirs
    last = pair(3, swap, swap_in)
    last.start()
    last.wait_recv()
    out[...] = (mine + swap_in[...]).astype(BF16)

    for ring in (zring, yring, uring):
        ring.finish()
    for e in range(1, nx):
        hand_up(e).wait_send()
    for d in range(ny):
        for kind in range(3 if d == ny // 2 else 4):
            hand(kind, d).wait_send()
    for e in range(1, nz):
        scatter(e).wait_send()
        spread(e).wait_send()
    for copy in (weights, first, ups, last):
        copy.wait_send()


def on_device(nx, ny, nz, act, weight, down, up, home, served, var):
    tokens, depth = act.shape
    cols = weight.shape[1]
    blocks, rank = down.shape[0], down.shape[2]
    groups = nx * ny
    served, var = served.T, var.T
    up = up.reshape(blocks * 4 // 16, 16, cols)
    weight = weight.reshape(nz, 2, depth, cols)
    hbm = pl.BlockSpec(memory_space=pl.ANY)
    vmem = pl.BlockSpec(memory_space=pltpu.VMEM)
    dma = pltpu.SemaphoreType.DMA
    share = tokens // nz
    scratch = [
        pltpu.VMEM((nz, tokens, depth), BF16),
        pltpu.VMEM((nz, depth, 2 * cols), BF16),
        pltpu.VMEM((ny,) + down.shape, BF16),
        pltpu.VMEM((ny,) + up.shape, BF16),
        pltpu.VMEM(down.shape, BF16),
        pltpu.VMEM((ny, nx * SLOTS, 16, rank), BF16),
        pltpu.VMEM((ny, SLOTS, 16, rank), BF16),
        pltpu.VMEM((SLOTS, groups, 16, rank), BF16),
        pltpu.VMEM((nx, 2, ny, 16, cols), BF16),
        pltpu.VMEM((2, nx, ny, 16, cols), BF16),
        pltpu.VMEM((2, nx, ny, 16, cols), BF16),
        pltpu.VMEM((tokens, 2 * cols), F32),
        pltpu.VMEM((2, tokens, rank), F32),
        pltpu.VMEM((tokens, rank), F32),
        pltpu.VMEM((nz, share, rank), F32),
        pltpu.VMEM((nz, share, rank), BF16),
        pltpu.VMEM((nz - 1, share, rank), BF16),
        pltpu.VMEM((nz, share, rank), BF16),
        pltpu.VMEM((tokens, cols), F32),
        pltpu.VMEM((tokens, cols), F32),
        pltpu.SMEM((nx * SLOTS,), jnp.int32),
        pltpu.SMEM(home.shape, jnp.int32),
        pltpu.SMEM(served.shape, jnp.int32),
        pltpu.VMEM(var.shape, jnp.int32),
        pltpu.VMEM((tokens, cols), jnp.int32),
        pltpu.VMEM((nx * SLOTS * 4, blocks * 4), BF16),
        pltpu.VMEM((rank, groups * 16), BF16),
        dma((7,)),
        dma((2, nz // 2, 2)), dma((2, nz // 2, 2)),
        dma((2, ny // 2, 2)), dma((2, ny // 2, 2)),
        dma((2, ny // 2, 1)), dma((2, ny // 2, 1)),
        dma((4, ny)), dma((4, ny)),
        dma((nx - 1,)), dma((nx - 1,)),
        dma((4,)), dma((4,)),
        dma((nz - 1,)), dma((nz - 1,)),
        dma((nz - 1,)), dma((nz - 1,)),
    ]
    return pl.pallas_call(
        functools.partial(kernel, nx, ny, nz),
        out_shape=jax.ShapeDtypeStruct((tokens, cols), BF16),
        in_specs=[hbm] * 7,
        out_specs=vmem,
        scratch_shapes=scratch,
        compiler_params=pltpu.CompilerParams(
            collective_id=0, has_side_effects=True, vmem_limit_bytes=56 * 1024 * 1024
        ),
    )(act, weight, down, up, home, served, var)


def solution(mesh):
    nx = 4
    ny, nz = mesh.shape["grp"] // nx, mesh.shape["tp"] // 2
    in_specs = (
        P("grp", "tp"),
        P(None, "tp"),
        P(None, ("tp", "grp"), None),
        P(None, "grp", "tp"),
        P(),
        P(),
        P("grp", None),
    )
    return jax.shard_map(
        functools.partial(on_device, nx, ny, nz),
        mesh=mesh, in_specs=in_specs, out_specs=P("grp", "tp"), check_vma=False,
    )
```

```python
import functools

import jax
import jax.numpy as jnp
from jax import lax
from jax.experimental import pallas as pl
from jax.experimental.pallas import tpu as pltpu
from jax.sharding import PartitionSpec as P

PIECES = 2
VPG = 4
SLOTS = PIECES * VPG
MESH = pl.DeviceIdType.MESH
F32 = jnp.float32
BF16 = jnp.bfloat16


class Ring:
    def __init__(self, buf, pieces, peers, send, recv):
        self.buf, self.pieces, self.peers = buf, pieces, peers
        self.send, self.recv = send, recv
        self.n = buf.shape[0]
        self.half = self.n // 2
        self.size = buf.shape[1] // pieces

    def events(self):
        for hop in range(1, self.half):
            for index in range(self.pieces):
                yield hop, index
        yield self.half, 0

    def cut(self, way, hop, index):
        if hop == self.half:
            size = self.buf.shape[1] // 2
            return pl.ds(way * size, size)
        piece = index if way == 0 else self.pieces - 1 - index
        return pl.ds(piece * self.size, self.size)

    def slot(self, way, hop):
        return hop % self.n if way == 0 else (self.n - hop) % self.n

    def copy(self, way, hop, index):
        cut = self.cut(way, hop, index)
        return pltpu.make_async_remote_copy(
            src_ref=self.buf.at[self.slot(way, hop - 1), cut],
            dst_ref=self.buf.at[self.slot(way, hop), cut],
            send_sem=self.send.at[way, hop - 1, index],
            recv_sem=self.recv.at[way, hop - 1, index],
            device_id=self.peers[way],
            device_id_type=MESH,
        )

    def start(self):
        for index in range(self.pieces):
            for way in range(2):
                self.copy(way, 1, index).start()

    def advance(self, hop, index):
        for way in range(2):
            self.copy(way, hop, index).wait_recv()
            if hop + 1 < self.half or (hop + 1 == self.half and index == 0):
                self.copy(way, hop + 1, index).start()

    def finish(self):
        for hop, index in self.events():
            for way in range(2):
                self.copy(way, hop, index).wait_send()


def kernel(
    nx, ny, nz,
    act, weight, down, up, home, served, var, out,
    abuf, wmine, wother, ybuf, ubuf, sel, xsend, xrelay, xrecv, usend, urecv,
    acc, sums, sums_in, whole, parts, parts_in, shrunk, swap_in, table, homes, lists, var_row, var_wide,
    chooser, opener,
    local_sem, z_send, z_recv, y_send, y_recv, u_send, u_recv, x_send, x_recv, v_send, v_recv,
    pair_send, pair_recv, a_send, a_recv, b_send, b_recv,
):
    grp, tp = lax.axis_index("grp"), lax.axis_index("tp")
    x, y = grp // ny, lax.rem(grp, ny)
    z, core = tp // 2, lax.rem(tp, 2)
    tokens = out.shape[0]
    cols = out.shape[1]
    groups = nx * ny
    far = 1 - 2 * core

    def at_x(step):
        return (lax.rem(x + step + nx, nx) * ny + y, tp)

    def at_y(step):
        return (x * ny + lax.rem(y + step + ny, ny), tp)

    def at_z(step, side=0):
        return (grp, lax.rem(z + step + nz, nz) * 2 + (core if side == 0 else 1 - core))

    other = (grp, z * 2 + 1 - core)

    local = [
        pltpu.make_async_copy(home, homes, local_sem.at[4]),
        pltpu.make_async_copy(served, lists, local_sem.at[5]),
        pltpu.make_async_copy(down, ybuf.at[0], local_sem.at[1]),
        pltpu.make_async_copy(act, abuf.at[0], local_sem.at[0]),
        pltpu.make_async_copy(up, ubuf.at[0], local_sem.at[2]),
        pltpu.make_async_copy(var, var_row, local_sem.at[6]),
        pltpu.make_async_copy(weight.at[:, core], wmine, local_sem.at[3]),
    ]
    for copy in local:
        copy.start()

    barrier = pltpu.get_barrier_semaphore()
    partners = [other] + [at_y(e) for e in range(1, ny)] + [at_x(e) for e in range(1, nx)]
    partners += [at_z(e, side) for side in range(2) for e in range(1, nz)]
    for partner in partners:
        pl.semaphore_signal(barrier, inc=1, device_id=partner, device_id_type=MESH)

    local[0].wait()
    local[1].wait()

    def fill(k, carry):
        owner = lax.rem(x + k // SLOTS, nx) * ny + y
        j = lax.rem(k, SLOTS)
        table[k] = homes[lists[j // PIECES, owner] * PIECES + lax.rem(j, PIECES)]
        return carry

    lax.fori_loop(0, nx * SLOTS, fill, 0)
    up_rows = up.shape[0] * up.shape[1]
    rank = xrecv.shape[-1]
    depth = act.shape[1]
    share = tokens // nz

    def set_up():
        shape = chooser.shape
        line = lax.broadcasted_iota(jnp.int32, shape, 0)

        def pick(k, rows):
            return jnp.where((line >> 2) == k, table[k], rows)

        rows = lax.fori_loop(0, nx * SLOTS, pick, jnp.zeros(shape, jnp.int32), unroll=4)
        wanted = rows * 4 + (line & 3)
        chooser[...] = (wanted == lax.broadcasted_iota(jnp.int32, shape, 1)).astype(F32).astype(BF16)
        row = lax.broadcasted_iota(jnp.int32, opener.shape, 0)
        column = lax.broadcasted_iota(jnp.int32, opener.shape, 1)
        piece = (column >> 2) & 1
        hit = row == piece * rank + ((column >> 4) << 2) + (column & 3)
        opener[...] = hit.astype(F32).astype(BF16)
        local[5].wait()
        for i in range(0, tokens, cols):
            size = min(cols, tokens - i)
            row = jnp.broadcast_to(var_row[:, pl.ds(i, size)], (cols, size))
            var_wide[pl.ds(i, size), :] = row.T

    pl.semaphore_wait(barrier, len(partners))

    zring = Ring(abuf, 2, (at_z(1), at_z(-1)), z_send, z_recv)
    yring = Ring(ybuf, 2, (at_y(1), at_y(-1)), y_send, y_recv)

    def pair(index, src, dst):
        return pltpu.make_async_remote_copy(
            src_ref=src, dst_ref=dst, send_sem=pair_send.at[index], recv_sem=pair_recv.at[index],
            device_id=other, device_id_type=MESH,
        )

    local[2].wait()
    yring.start()
    local[3].wait()
    zring.start()
    weights = pair(0, weight.at[:, 1 - core], wother)
    weights.start()

    def behind(d):
        return lax.rem(y - d + ny, ny)

    def hand(kind, d):
        mine = x * ny + behind(d)
        passed = lax.rem(x - far + nx, nx) * ny + behind(d)
        straight = d == ny // 2
        src, dst, peer = (
            (xsend.at[d, pl.ds(SLOTS, SLOTS)], xrecv.at[mine], at_x(1)),
            (xsend.at[d, pl.ds(3 * SLOTS, SLOTS)], xrecv.at[mine], at_x(-1)),
            (
                xsend.at[d, pl.ds(2 * SLOTS, SLOTS)],
                xrecv.at[mine] if straight else xrelay.at[d],
                at_x(2) if straight else at_x(far),
            ),
            (xrelay.at[d], xrecv.at[passed], at_x(far)),
        )[kind]
        return pltpu.make_async_remote_copy(
            src_ref=src, dst_ref=dst, send_sem=x_send.at[kind, d], recv_sem=x_recv.at[kind, d],
            device_id=peer, device_id_type=MESH,
        )

    def choose(d):
        sel[...] = ybuf[d]
        for e, kind in ((2, 2), (1, 0), (3, 1), (0, None)):

            def take(j, carry):
                xsend[d, e * SLOTS + j] = sel[table[e * SLOTS + j]]
                return carry

            lax.fori_loop(0, SLOTS, take, 0, unroll=True)
            if kind is not None:
                hand(kind, d).start()
        xrecv[x * ny + behind(d)] = xsend[d, pl.ds(0, SLOTS)]

    def relay(d):
        if d != ny // 2:
            hand(2, d).wait_recv()
            hand(3, d).start()

    def spread_up(e):
        return pltpu.make_async_remote_copy(
            src_ref=ubuf.at[0], dst_ref=ubuf.at[e], send_sem=u_send.at[e - 1], recv_sem=u_recv.at[e - 1],
            device_id=at_y(e), device_id_type=MESH,
        )

    def hand_up(e):
        return pltpu.make_async_remote_copy(
            src_ref=usend.at[e], dst_ref=urecv.at[x], send_sem=v_send.at[e - 1], recv_sem=v_recv.at[e - 1],
            device_id=at_x(e), device_id_type=MESH,
        )

    def choose_up():
        blocks = jnp.concatenate([ubuf[d].reshape(up_rows, cols) for d in range(ny)], axis=1)
        chosen = jnp.dot(chooser[...], blocks, preferred_element_type=F32).astype(BF16)
        for d in range(ny):
            some = chosen[:, d * cols:(d + 1) * cols].reshape(nx, 2, 16, cols)
            for e in range(nx):
                usend[e, :, behind(d)] = some[e]

    def multiply(slot, cut):
        place = lax.rem(z - slot + nz, nz)
        both = jnp.concatenate([wmine[place], wother[place]], axis=1)
        return jnp.dot(abuf[slot, cut, :], both, preferred_element_type=F32)

    def z_multiply(event):
        hop, index = event
        for way in range(2):
            cut = zring.cut(way, hop, index)
            acc[cut, :] += multiply(zring.slot(way, hop), cut)

    z_events, y_events = (list(ring.events()) for ring in (zring, yring))
    choose(0)
    set_up()

    waiting = [0]
    last_y = len(y_events) - 1
    early = min(len(y_events) // 2, len(z_events) - 4)
    for number, (hop, index) in enumerate(y_events):
        yring.advance(hop, index)
        if number == max(last_y - 2, 0):
            local[4].wait()
            for e in range(1, ny):
                spread_up(e).start()
        if hop == yring.half or index == 1:
            ready = sorted({yring.slot(0, hop), yring.slot(1, hop)})
            for d in ready:
                choose(d)
            for d in waiting:
                relay(d)
            waiting = ready
        if number % 2 == 1 and number // 2 < early:
            zring.advance(*z_events[number // 2])
    for event in z_events[early:-3]:
        zring.advance(*event)
    local[6].wait()
    weights.wait_recv()
    acc[...] = multiply(0, pl.ds(0, tokens))
    z_multiply(z_events[0])

    for d in range(ny):
        for kind in (0, 1, 2 if d == ny // 2 else 3):
            hand(kind, d).wait_recv()
    mine = abuf[0]
    total = jnp.zeros((tokens, PIECES * rank), F32)
    who = jnp.concatenate([var_wide[:, pl.ds(0, rank)]] * PIECES, axis=1)
    for v in range(VPG):
        factor = jnp.concatenate([xrecv[:, v * PIECES + p].reshape(depth, rank) for p in range(PIECES)], axis=1)
        total = jnp.where(who == v, jnp.dot(mine, factor, preferred_element_type=F32), total)
    for p in range(PIECES):
        sums[p] = total[:, p * rank:(p + 1) * rank]
    first = pair(1, sums.at[1 - core], sums_in)
    first.start()
    zring.advance(*z_events[-3])
    for event in z_events[1:-4]:
        z_multiply(event)
    first.wait_recv()
    total = sums[core] + sums_in[...]
    whole[...] = total.reshape(nz, share, rank)
    parts[...] = total.astype(BF16).reshape(nz, share, rank)

    def scatter(e):
        return pltpu.make_async_remote_copy(
            src_ref=parts.at[lax.rem(z + e, nz)], dst_ref=parts_in.at[e - 1],
            send_sem=a_send.at[e - 1], recv_sem=a_recv.at[e - 1], device_id=at_z(e), device_id_type=MESH,
        )

    def spread(e, side):
        return pltpu.make_async_remote_copy(
            src_ref=shrunk.at[core, z], dst_ref=shrunk.at[core, z],
            send_sem=b_send.at[side, e], recv_sem=b_recv.at[side, e],
            device_id=at_z(e, side), device_id_type=MESH,
        )

    targets = [(e, side) for e in range(1, nz) for side in range(2)] + [(0, 1)]

    for e in range(1, nz):
        scatter(e).start()
    for e in range(1, ny):
        spread_up(e).wait_recv()
    choose_up()
    for e in range(1, nx):
        hand_up(e).start()
    urecv[x] = usend[0]
    total = whole[z]
    for e in range(1, nz):
        scatter(e).wait_recv()
        total += parts_in[e - 1].astype(F32)
    shrunk[core, z] = total.astype(BF16)
    for target in targets:
        spread(*target).start()

    zring.advance(*z_events[-2])
    for event in z_events[-4:-1]:
        z_multiply(event)
    zring.advance(*z_events[-1])
    z_multiply(z_events[-1])
    last = pair(2, acc.at[:, pl.ds(cols, cols)], swap_in)
    last.start()

    wide = groups * 16
    for e in range(1, nx):
        hand_up(e).wait_recv()
    for target in targets:
        spread(*target).wait_recv()
    both = jnp.concatenate([shrunk[p].reshape(tokens, rank) for p in range(PIECES)], axis=1)
    opened = jnp.dot(both, opener[...], preferred_element_type=F32)
    total = acc[:, pl.ds(0, cols)]
    who = jnp.concatenate([var_wide[:, pl.ds(0, min(cols, wide))]] * max(wide // cols, 1), axis=1)
    which = (lax.broadcasted_iota(jnp.int32, (1, wide), 1) >> 3) & 1
    for h in range(2):
        part = jnp.where(who == which + 2 * h, opened, 0.0).astype(BF16)
        total += jnp.dot(part, urecv[:, h].reshape(wide, cols), preferred_element_type=F32)
    last.wait_recv()
    out[...] = (total + swap_in[...]).astype(BF16)

    for e in range(1, ny):
        spread_up(e).wait_send()
    for ring in (zring, yring):
        ring.finish()
    for e in range(1, nx):
        hand_up(e).wait_send()
    for d in range(ny):
        for kind in range(3 if d == ny // 2 else 4):
            hand(kind, d).wait_send()
    for e in range(1, nz):
        scatter(e).wait_send()
    for target in targets:
        spread(*target).wait_send()
    for copy in (weights, first, last):
        copy.wait_send()


def on_device(nx, ny, nz, act, weight, down, up, home, served, var):
    tokens, depth = act.shape
    cols = weight.shape[1]
    blocks, rank = down.shape[0], down.shape[2]
    groups = nx * ny
    served, var = served.T, var.T
    up = up.reshape(blocks * 4 // 16, 16, cols)
    weight = weight.reshape(nz, 2, depth, cols)
    hbm = pl.BlockSpec(memory_space=pl.ANY)
    vmem = pl.BlockSpec(memory_space=pltpu.VMEM)
    dma = pltpu.SemaphoreType.DMA
    share = tokens // nz
    scratch = [
        pltpu.VMEM((nz, tokens, depth), BF16),
        pltpu.VMEM((nz, depth, cols), BF16),
        pltpu.VMEM((nz, depth, cols), BF16),
        pltpu.VMEM((ny,) + down.shape, BF16),
        pltpu.VMEM((ny,) + up.shape, BF16),
        pltpu.VMEM(down.shape, BF16),
        pltpu.VMEM((ny, nx * SLOTS, 16, rank), BF16),
        pltpu.VMEM((ny, SLOTS, 16, rank), BF16),
        pltpu.VMEM((groups, SLOTS, 16, rank), BF16),
        pltpu.VMEM((nx, 2, ny, 16, cols), BF16),
        pltpu.VMEM((nx, 2, ny, 16, cols), BF16),
        pltpu.VMEM((tokens, 2 * cols), F32),
        pltpu.VMEM((2, tokens, rank), F32),
        pltpu.VMEM((tokens, rank), F32),
        pltpu.VMEM((nz, share, rank), F32),
        pltpu.VMEM((nz, share, rank), BF16),
        pltpu.VMEM((nz - 1, share, rank), BF16),
        pltpu.VMEM((PIECES, nz, share, rank), BF16),
        pltpu.VMEM((tokens, cols), F32),
        pltpu.SMEM((nx * SLOTS,), jnp.int32),
        pltpu.SMEM(home.shape, jnp.int32),
        pltpu.SMEM(served.shape, jnp.int32),
        pltpu.VMEM(var.shape, jnp.int32),
        pltpu.VMEM((tokens, cols), jnp.int32),
        pltpu.VMEM((nx * SLOTS * 4, blocks * 4), BF16),
        pltpu.VMEM((PIECES * rank, groups * 16), BF16),
        dma((7,)),
        dma((2, nz // 2, 2)), dma((2, nz // 2, 2)),
        dma((2, ny // 2, 2)), dma((2, ny // 2, 2)),
        dma((ny - 1,)), dma((ny - 1,)),
        dma((4, ny)), dma((4, ny)),
        dma((nx - 1,)), dma((nx - 1,)),
        dma((3,)), dma((3,)),
        dma((nz - 1,)), dma((nz - 1,)),
        dma((2, nz)), dma((2, nz)),
    ]
    return pl.pallas_call(
        functools.partial(kernel, nx, ny, nz),
        out_shape=jax.ShapeDtypeStruct((tokens, cols), BF16),
        in_specs=[hbm] * 7,
        out_specs=vmem,
        scratch_shapes=scratch,
        compiler_params=pltpu.CompilerParams(
            collective_id=0, has_side_effects=True, vmem_limit_bytes=56 * 1024 * 1024
        ),
    )(act, weight, down, up, home, served, var)


def solution(mesh):
    nx = 4
    ny, nz = mesh.shape["grp"] // nx, mesh.shape["tp"] // 2
    in_specs = (
        P("grp", "tp"),
        P(None, "tp"),
        P(None, ("tp", "grp"), None),
        P(None, "grp", "tp"),
        P(),
        P(),
        P("grp", None),
    )
    return jax.shard_map(
        functools.partial(on_device, nx, ny, nz),
        mesh=mesh, in_specs=in_specs, out_specs=P("grp", "tp"), check_vma=False,
    )
```

```python
import functools

import jax
import jax.numpy as jnp
from jax import lax
from jax.experimental import pallas as pl
from jax.experimental.pallas import tpu as pltpu
from jax.sharding import PartitionSpec as P

PIECES = 2
VPG = 4
SLOTS = PIECES * VPG
MESH = pl.DeviceIdType.MESH
F32 = jnp.float32
BF16 = jnp.bfloat16


class Ring:
    def __init__(self, buf, pieces, peers, send, recv):
        self.buf, self.pieces, self.peers = buf, pieces, peers
        self.send, self.recv = send, recv
        self.n = buf.shape[0]
        self.half = self.n // 2
        self.size = buf.shape[1] // pieces

    def events(self):
        for hop in range(1, self.half):
            for index in range(self.pieces):
                yield hop, index
        yield self.half, 0

    def cut(self, way, hop, index):
        if hop == self.half:
            size = self.buf.shape[1] // 2
            return pl.ds(way * size, size)
        piece = index if way == 0 else self.pieces - 1 - index
        return pl.ds(piece * self.size, self.size)

    def slot(self, way, hop):
        return hop % self.n if way == 0 else (self.n - hop) % self.n

    def copy(self, way, hop, index):
        cut = self.cut(way, hop, index)
        return pltpu.make_async_remote_copy(
            src_ref=self.buf.at[self.slot(way, hop - 1), cut],
            dst_ref=self.buf.at[self.slot(way, hop), cut],
            send_sem=self.send,
            recv_sem=self.recv.at[way, hop - 1, index],
            device_id=self.peers[way],
            device_id_type=MESH,
        )

    def start(self):
        for index in range(self.pieces):
            for way in range(2):
                self.copy(way, 1, index).start()

    def advance(self, hop, index):
        for way in range(2):
            self.copy(way, hop, index).wait_recv()
            if hop + 1 < self.half or (hop + 1 == self.half and index == 0):
                self.copy(way, hop + 1, index).start()


def loop(first, end, body):
    def step(k, carry):
        body(k)
        return carry

    lax.fori_loop(first, end, step, 0)


def kernel(
    nx, ny, nz,
    act, weight, down, up, home, served, var, out,
    abuf, wmine, wother, ybuf, ubuf, sel, xsend, xrelay, xrecv, usend, urecv,
    acc, sums, sums_in, whole, parts, parts_in, shrunk, swap_in, table, homes, lists, var_row, var_wide,
    chooser, opener,
    permuted, local_sem, z_recv, y_recv, relay_recv, sent, got, pair_send, pair_recv,
):
    grp, tp = lax.axis_index("grp"), lax.axis_index("tp")
    x, y = grp // ny, lax.rem(grp, ny)
    z, core = tp // 2, lax.rem(tp, 2)
    tokens = out.shape[0]
    cols = out.shape[1]
    groups = nx * ny
    far = 1 - 2 * core

    def at_x(step):
        return (lax.rem(x + step + nx, nx) * ny + y, tp)

    def at_y(step):
        return (x * ny + lax.rem(y + step + ny, ny), tp)

    def at_z(step, side=0):
        return (grp, lax.rem(z + step + nz, nz) * 2 + (core if side == 0 else 1 - core))

    other = (grp, z * 2 + 1 - core)

    local = [
        pltpu.make_async_copy(home, homes, local_sem.at[4]),
        pltpu.make_async_copy(served, lists, local_sem.at[5]),
        pltpu.make_async_copy(down, ybuf.at[0], local_sem.at[1]),
        pltpu.make_async_copy(act, abuf.at[0], local_sem.at[0]),
        pltpu.make_async_copy(up, ubuf.at[0], local_sem.at[2]),
        pltpu.make_async_copy(var, var_row, local_sem.at[6]),
        pltpu.make_async_copy(weight.at[:, core], wmine, local_sem.at[3]),
    ]
    for copy in local:
        copy.start()

    barrier = pltpu.get_barrier_semaphore()

    def greet(partner):
        pl.semaphore_signal(barrier, inc=1, device_id=partner, device_id_type=MESH)

    greet(other)
    loop(1, ny, lambda e: greet(at_y(e)))
    loop(1, nx, lambda e: greet(at_x(e)))
    loop(1, nz, lambda e: [greet(at_z(e, side)) for side in range(2)])

    local[0].wait()
    local[1].wait()

    def fill(k, carry):
        owner = lax.rem(x + k // SLOTS, nx) * ny + y
        j = lax.rem(k, SLOTS)
        table[k] = homes[lists[j // PIECES, owner] * PIECES + lax.rem(j, PIECES)]
        return carry

    lax.fori_loop(0, nx * SLOTS, fill, 0)
    up_rows = up.shape[0] * up.shape[1]
    rank = xrecv.shape[-1]
    depth = act.shape[1]
    share = tokens // nz

    def set_up():
        shape = chooser.shape
        line = lax.broadcasted_iota(jnp.int32, shape, 0)

        def pick(k, rows):
            return jnp.where((line >> 2) == k, table[k], rows)

        rows = lax.fori_loop(0, nx * SLOTS, pick, jnp.zeros(shape, jnp.int32), unroll=4)
        wanted = rows * 4 + (line & 3)
        chooser[...] = (wanted == lax.broadcasted_iota(jnp.int32, shape, 1)).astype(F32).astype(BF16)
        row = lax.broadcasted_iota(jnp.int32, opener.shape, 0)
        column = lax.broadcasted_iota(jnp.int32, opener.shape, 1)
        piece = (column >> 2) & 1
        hit = row == piece * rank + ((column >> 4) << 2) + (column & 3)
        opener[...] = hit.astype(F32).astype(BF16)
        for e in range(nx):
            width = ny * 16
            row = lax.broadcasted_iota(jnp.int32, (depth, width), 0)
            column = lax.broadcasted_iota(jnp.int32, (depth, width), 1)
            place = column >> 4
            behind_y = jnp.where((place & 1) == 1, (place + 1) >> 1, ny - (place >> 1))
            from_group = lax.rem(x + nx - e, nx) * ny + ((y - behind_y) & (ny - 1))
            hit = (row >> 4 == from_group) & ((row & 15) == (column & 15))
            columns = jnp.dot(abuf[0], hit.astype(F32).astype(BF16), preferred_element_type=F32)
            permuted[:, e * width:(e + 1) * width] = columns.astype(BF16)
        local[5].wait()
        for i in range(0, tokens, cols):
            size = min(cols, tokens - i)
            row = jnp.broadcast_to(var_row[:, pl.ds(i, size)], (cols, size))
            var_wide[pl.ds(i, size), :] = row.T

    pl.semaphore_wait(barrier, ny + nx + 2 * nz - 3)

    zring = Ring(abuf, 2, (at_z(1), at_z(-1)), sent.at[0], z_recv)
    yring = Ring(ybuf, 2, (at_y(1), at_y(-1)), sent.at[1], y_recv)

    def pair(index, src, dst):
        return pltpu.make_async_remote_copy(
            src_ref=src, dst_ref=dst, send_sem=pair_send.at[index], recv_sem=pair_recv.at[index],
            device_id=other, device_id_type=MESH,
        )

    local[2].wait()
    yring.start()
    local[3].wait()
    zring.start()
    weights = pair(0, weight.at[:, 1 - core], wother)
    weights.start()

    def behind(d):
        return lax.rem(y - d + ny, ny)

    def remote(src, dst, send, recv, peer):
        return pltpu.make_async_remote_copy(
            src_ref=src, dst_ref=dst, send_sem=send, recv_sem=recv, device_id=peer, device_id_type=MESH
        )

    def all_sent(kind, ref):
        remote(ref, ref, sent.at[kind], got.at[0], other).wait_send()

    def all_got(kind, ref):
        remote(ref, ref, sent.at[0], got.at[kind], other).wait_recv()

    groups_of_places = [(0, 1)] + [(2 * k - 1, 2) for k in range(1, ny // 2)] + [(ny - 1, 1)]

    def chunk(place):
        return (place + 1) // 2 if place % 2 else (ny - place // 2) % ny

    def hand(e, number):
        places = pl.ds(*groups_of_places[number])
        if e == 2 and number != len(groups_of_places) - 1:
            return remote(xsend.at[2, places], xrelay.at[places], sent.at[2], relay_recv.at[number], at_x(far))
        return remote(xsend.at[e, places], xrecv.at[e, places], sent.at[2], got.at[1], at_x(e))

    def choose(number):
        first, count = groups_of_places[number]
        for place in range(first, first + count):
            sel[place - first] = ybuf[chunk(place)]
        for e in (2, 1, 3, 0):

            def take(j):
                slot = table[e * SLOTS + j]
                for k in range(count):
                    if e == 0:
                        xrecv[0, first + k, j] = sel[k, slot]
                    else:
                        xsend[e, first + k, j] = sel[k, slot]

            loop(0, SLOTS, take)
            if e:
                hand(e, number).start()

    def relay(number):
        if number != len(groups_of_places) - 1:
            hand(2, number).wait_recv()
            places = pl.ds(*groups_of_places[number])
            remote(xrelay.at[places], xrecv.at[2, places], sent.at[3], got.at[1], at_x(far)).start()

    def spread_up(e):
        return remote(ubuf.at[0], ubuf.at[e], sent.at[4], got.at[2], at_y(e))

    def hand_up(e):
        return remote(usend.at[e], urecv.at[x], sent.at[5], got.at[3], at_x(e))

    def choose_up():
        blocks = jnp.concatenate([ubuf[d].reshape(up_rows, cols) for d in range(ny)], axis=1)
        chosen = jnp.dot(chooser[...], blocks, preferred_element_type=F32).astype(BF16)
        for d in range(ny):
            some = chosen[:, d * cols:(d + 1) * cols].reshape(nx, 2, 16, cols)
            for e in range(nx):
                usend[e, :, behind(d)] = some[e]

    def multiply(slot):
        place = lax.rem(z - slot + nz, nz)
        both = jnp.concatenate([wmine[place], wother[place]], axis=1)
        return jnp.dot(abuf[slot], both, preferred_element_type=F32)

    def multiply_pair(hop):
        def add(k):
            acc[...] += multiply(hop + k * (nz - 2 * hop))

        loop(0, 2, add)

    z_events, y_events = (list(ring.events()) for ring in (zring, yring))
    choose(0)
    set_up()

    last_y = len(y_events) - 1
    for number, (hop, index) in enumerate(y_events):
        yring.advance(hop, index)
        if number == max(last_y - 2, 0):
            local[4].wait()
            loop(1, ny, lambda e: spread_up(e).start())
        if hop == yring.half or index == 1:
            choose(hop)
            relay(hop - 1)
        if number % 2 == 1 and number // 2 < len(z_events) - 4:
            zring.advance(*z_events[number // 2])
    for event in z_events[min(len(y_events) // 2, len(z_events) - 4):-3]:
        zring.advance(*event)
    local[6].wait()
    weights.wait_recv()
    acc[...] = multiply(0)
    multiply_pair(1)

    all_got(1, xrecv.at[pl.ds(1, nx - 1)])
    mine = permuted[...]
    total = jnp.zeros((tokens, PIECES * rank), F32)
    who = jnp.concatenate([var_wide[:, pl.ds(0, rank)]] * PIECES, axis=1)
    for v in range(VPG):
        factor = jnp.concatenate([xrecv[:, :, v * PIECES + p].reshape(depth, rank) for p in range(PIECES)], axis=1)
        total = jnp.where(who == v, jnp.dot(mine, factor, preferred_element_type=F32), total)
    for p in range(PIECES):
        sums[p] = total[:, p * rank:(p + 1) * rank]
    first = pair(1, sums.at[1 - core], sums_in)
    first.start()
    zring.advance(*z_events[-3])
    for hop in range(2, nz // 2 - 1):
        multiply_pair(hop)
    first.wait_recv()
    total = sums[core] + sums_in[...]
    whole[...] = total.reshape(nz, share, rank)
    parts[...] = total.astype(BF16).reshape(nz, share, rank)

    def scatter(e):
        return remote(parts.at[lax.rem(z + e, nz)], parts_in.at[e - 1], sent.at[6], got.at[4], at_z(e))

    def spread(e, side):
        shard = shrunk.at[core * nz + z]
        return remote(shard, shard, sent.at[7], got.at[5], at_z(e, side))

    loop(1, nz, lambda e: scatter(e).start())
    all_got(2, ubuf.at[pl.ds(1, ny - 1)])
    choose_up()
    loop(1, nx, lambda e: hand_up(e).start())
    urecv[x] = usend[0]
    all_got(4, parts_in)
    shrunk[core * nz + z] = (whole[z] + jnp.sum(parts_in[...].astype(F32), axis=0)).astype(BF16)
    loop(1, nz, lambda e: [spread(e, side).start() for side in range(2)])
    spread(0, 1).start()

    zring.advance(*z_events[-2])
    multiply_pair(nz // 2 - 1)
    zring.advance(*z_events[-1])
    acc[...] += multiply(nz // 2)
    last = pair(2, acc.at[:, pl.ds(cols, cols)], swap_in)
    last.start()

    all_sent(0, abuf.at[pl.ds(0, nz - 1)])
    all_sent(1, ybuf.at[pl.ds(0, ny - 1)])
    all_sent(2, xsend.at[pl.ds(1, nx - 1)])
    all_sent(3, xrelay)
    all_sent(4, ubuf.at[pl.ds(0, ny - 1)])
    all_sent(5, usend.at[pl.ds(1, nx - 1)])
    all_sent(6, parts.at[pl.ds(0, nz - 1)])
    weights.wait_send()
    first.wait_send()
    all_got(3, urecv.at[pl.ds(0, nx - 1)])
    all_got(5, shrunk.at[pl.ds(0, 2 * nz - 1)])
    wide = groups * 16
    both = jnp.concatenate([shrunk[pl.ds(p * nz, nz)].reshape(tokens, rank) for p in range(PIECES)], axis=1)
    opened = jnp.dot(both, opener[...], preferred_element_type=F32)
    total = acc[:, pl.ds(0, cols)]
    who = jnp.concatenate([var_wide[:, pl.ds(0, min(cols, wide))]] * max(wide // cols, 1), axis=1)
    which = (lax.broadcasted_iota(jnp.int32, (1, wide), 1) >> 3) & 1
    for h in range(2):
        part = jnp.where(who == which + 2 * h, opened, 0.0).astype(BF16)
        total += jnp.dot(part, urecv[:, h].reshape(wide, cols), preferred_element_type=F32)
    last.wait_recv()
    out[...] = (total + swap_in[...]).astype(BF16)

    all_sent(7, shrunk.at[pl.ds(0, 2 * nz - 1)])
    last.wait_send()


def on_device(nx, ny, nz, act, weight, down, up, home, served, var):
    tokens, depth = act.shape
    cols = weight.shape[1]
    blocks, rank = down.shape[0], down.shape[2]
    groups = nx * ny
    served, var = served.T, var.T
    up = up.reshape(blocks * 4 // 16, 16, cols)
    weight = weight.reshape(nz, 2, depth, cols)
    hbm = pl.BlockSpec(memory_space=pl.ANY)
    vmem = pl.BlockSpec(memory_space=pltpu.VMEM)
    dma = pltpu.SemaphoreType.DMA
    share = tokens // nz
    scratch = [
        pltpu.VMEM((nz, tokens, depth), BF16),
        pltpu.VMEM((nz, depth, cols), BF16),
        pltpu.VMEM((nz, depth, cols), BF16),
        pltpu.VMEM((ny,) + down.shape, BF16),
        pltpu.VMEM((ny,) + up.shape, BF16),
        pltpu.VMEM((2,) + down.shape, BF16),
        pltpu.VMEM((nx, ny, SLOTS, 16, rank), BF16),
        pltpu.VMEM((ny - 1, SLOTS, 16, rank), BF16),
        pltpu.VMEM((nx, ny, SLOTS, 16, rank), BF16),
        pltpu.VMEM((nx, 2, ny, 16, cols), BF16),
        pltpu.VMEM((nx, 2, ny, 16, cols), BF16),
        pltpu.VMEM((tokens, 2 * cols), F32),
        pltpu.VMEM((2, tokens, rank), F32),
        pltpu.VMEM((tokens, rank), F32),
        pltpu.VMEM((nz, share, rank), F32),
        pltpu.VMEM((nz, share, rank), BF16),
        pltpu.VMEM((nz - 1, share, rank), BF16),
        pltpu.VMEM((PIECES * nz, share, rank), BF16),
        pltpu.VMEM((tokens, cols), F32),
        pltpu.SMEM((nx * SLOTS,), jnp.int32),
        pltpu.SMEM(home.shape, jnp.int32),
        pltpu.SMEM(served.shape, jnp.int32),
        pltpu.VMEM(var.shape, jnp.int32),
        pltpu.VMEM((tokens, cols), jnp.int32),
        pltpu.VMEM((nx * SLOTS * 4, blocks * 4), BF16),
        pltpu.VMEM((PIECES * rank, groups * 16), BF16),
        pltpu.VMEM((tokens, depth), BF16),
        dma((7,)),
        dma((2, nz // 2, 2)), dma((2, ny // 2, 2)), dma((ny // 2,)),
        dma((8,)), dma((6,)), dma((3,)), dma((3,)),
    ]
    return pl.pallas_call(
        functools.partial(kernel, nx, ny, nz),
        out_shape=jax.ShapeDtypeStruct((tokens, cols), BF16),
        in_specs=[hbm] * 7,
        out_specs=vmem,
        scratch_shapes=scratch,
        compiler_params=pltpu.CompilerParams(
            collective_id=0, has_side_effects=True, vmem_limit_bytes=56 * 1024 * 1024
        ),
    )(act, weight, down, up, home, served, var)


def solution(mesh):
    nx = 4
    ny, nz = mesh.shape["grp"] // nx, mesh.shape["tp"] // 2
    in_specs = (
        P("grp", "tp"),
        P(None, "tp"),
        P(None, ("tp", "grp"), None),
        P(None, "grp", "tp"),
        P(),
        P(),
        P("grp", None),
    )
    return jax.shard_map(
        functools.partial(on_device, nx, ny, nz),
        mesh=mesh, in_specs=in_specs, out_specs=P("grp", "tp"), check_vma=False,
    )
```

```python
import functools

import jax
import jax.numpy as jnp
from jax import lax
from jax.experimental import pallas as pl
from jax.experimental.pallas import tpu as pltpu
from jax.sharding import PartitionSpec as P

PIECES = 2
VPG = 4
SLOTS = PIECES * VPG
MESH = pl.DeviceIdType.MESH
F32 = jnp.float32
BF16 = jnp.bfloat16


class Ring:
    def __init__(self, buf, pieces, peers, send, recv):
        self.buf, self.pieces, self.peers = buf, pieces, peers
        self.send, self.recv = send, recv
        self.n = buf.shape[0]
        self.half = self.n // 2
        self.size = buf.shape[1] // pieces

    def events(self):
        for hop in range(1, self.half):
            for index in range(self.pieces):
                yield hop, index
        yield self.half, 0

    def cut(self, way, hop, index):
        if hop == self.half:
            size = self.buf.shape[1] // 2
            return pl.ds(way * size, size)
        piece = index if way == 0 else self.pieces - 1 - index
        return pl.ds(piece * self.size, self.size)

    def slot(self, way, hop):
        return hop % self.n if way == 0 else (self.n - hop) % self.n

    def copy(self, way, hop, index):
        cut = self.cut(way, hop, index)
        return pltpu.make_async_remote_copy(
            src_ref=self.buf.at[self.slot(way, hop - 1), cut],
            dst_ref=self.buf.at[self.slot(way, hop), cut],
            send_sem=self.send,
            recv_sem=self.recv.at[way, hop - 1, index],
            device_id=self.peers[way],
            device_id_type=MESH,
        )

    def start(self):
        for index in range(self.pieces):
            for way in range(2):
                self.copy(way, 1, index).start()

    def advance(self, hop, index):
        for way in range(2):
            self.copy(way, hop, index).wait_recv()
            if hop + 1 < self.half or (hop + 1 == self.half and index == 0):
                self.copy(way, hop + 1, index).start()


def loop(first, end, body):
    def step(k, carry):
        body(k)
        return carry

    lax.fori_loop(first, end, step, 0)


def kernel(
    nx, ny, nz,
    act, weight, down, up, home, served, var, out,
    abuf, wmine, wother, ybuf, sel, xsend, xrelay, xrecv,
    acc, sums, sums_in, whole, parts, parts_in, shrunk, swap_in, table, homes, lists, var_row, var_wide,
    chooser, opener,
    permuted, local_sem, z_recv, y_recv, relay_recv, sent, got, pair_send, pair_recv,
):
    grp, tp = lax.axis_index("grp"), lax.axis_index("tp")
    x, y = grp // ny, lax.rem(grp, ny)
    z, core = tp // 2, lax.rem(tp, 2)
    tokens = out.shape[0]
    cols = out.shape[1]
    groups = nx * ny
    blocks = down.shape[0]
    far = 1 - 2 * core

    def at_x(step):
        return (lax.rem(x + step + nx, nx) * ny + y, tp)

    def at_y(step):
        return (x * ny + lax.rem(y + step + ny, ny), tp)

    def at_z(step, side=0):
        return (grp, lax.rem(z + step + nz, nz) * 2 + (core if side == 0 else 1 - core))

    other = (grp, z * 2 + 1 - core)

    local = [
        pltpu.make_async_copy(home, homes, local_sem.at[4]),
        pltpu.make_async_copy(served, lists, local_sem.at[5]),
        pltpu.make_async_copy(down, ybuf.at[0, pl.ds(0, blocks)], local_sem.at[1]),
        pltpu.make_async_copy(act, abuf.at[0], local_sem.at[0]),
        pltpu.make_async_copy(up, ybuf.at[0, pl.ds(blocks, up.shape[0])], local_sem.at[2]),
        pltpu.make_async_copy(var, var_row, local_sem.at[6]),
        pltpu.make_async_copy(weight.at[:, core], wmine, local_sem.at[3]),
    ]
    for copy in local:
        copy.start()

    barrier = pltpu.get_barrier_semaphore()

    def greet(partner):
        pl.semaphore_signal(barrier, inc=1, device_id=partner, device_id_type=MESH)

    greet(other)
    greet(at_y(1))
    greet(at_y(-1))
    loop(1, nx, lambda e: greet(at_x(e)))
    loop(1, nz, lambda e: [greet(at_z(e, side)) for side in range(2)])

    local[0].wait()
    local[1].wait()

    def fill(k, carry):
        owner = lax.rem(x + k // SLOTS, nx) * ny + y
        j = lax.rem(k, SLOTS)
        table[k] = homes[lists[j // PIECES, owner] * PIECES + lax.rem(j, PIECES)]
        return carry

    lax.fori_loop(0, nx * SLOTS, fill, 0)
    up_rows = up.shape[0] * up.shape[1]
    rank = xrecv.shape[-1]
    depth = act.shape[1]
    share = tokens // nz

    def set_up_choice():
        shape = chooser.shape
        line = lax.broadcasted_iota(jnp.int32, shape, 0)

        def pick(k, rows):
            return jnp.where((line >> 2) == k, table[k], rows)

        rows = lax.fori_loop(0, nx * SLOTS, pick, jnp.zeros(shape, jnp.int32), unroll=4)
        wanted = rows * 4 + (line & 3)
        chooser[...] = (wanted == lax.broadcasted_iota(jnp.int32, shape, 1)).astype(F32).astype(BF16)

    def set_up():
        width = ny * 16
        place = lax.broadcasted_iota(jnp.int32, (1, width), 1) >> 4
        behind_y = jnp.where((place & 1) == 1, (place + 1) >> 1, ny - (place >> 1))
        for e in range(nx):
            columns = pl.ds(e * width, width)
            from_group = lax.rem(x + nx - e, nx) * ny + ((y - behind_y) & (ny - 1))
            row = lax.broadcasted_iota(jnp.int32, (depth, width), 0)
            column = lax.broadcasted_iota(jnp.int32, (depth, width), 1)
            hit = row == from_group * 16 + (column & 15)
            moved = jnp.dot(abuf[0], hit.astype(F32).astype(BF16), preferred_element_type=F32)
            permuted[:, columns] = moved.astype(BF16)
            row = lax.broadcasted_iota(jnp.int32, (PIECES * rank, width), 0)
            column = lax.broadcasted_iota(jnp.int32, (PIECES * rank, width), 1)
            hit = row == ((column >> 2) & 1) * rank + from_group * 4 + (column & 3)
            opener[:, columns] = hit.astype(F32).astype(BF16)
        local[5].wait()
        for i in range(0, tokens, cols):
            size = min(cols, tokens - i)
            row = jnp.broadcast_to(var_row[:, pl.ds(i, size)], (cols, size))
            var_wide[pl.ds(i, size), :] = row.T

    pl.semaphore_wait(barrier, nx + 2 * nz)

    zring = Ring(abuf, 2, (at_z(1), at_z(-1)), sent.at[0], z_recv)
    yring = Ring(ybuf, 2, (at_y(1), at_y(-1)), sent.at[1], y_recv)

    def pair(index, src, dst):
        return pltpu.make_async_remote_copy(
            src_ref=src, dst_ref=dst, send_sem=pair_send.at[index], recv_sem=pair_recv.at[index],
            device_id=other, device_id_type=MESH,
        )

    local[2].wait()
    local[4].wait()
    yring.start()
    local[3].wait()
    zring.start()
    weights = pair(0, weight.at[:, 1 - core], wother)

    def behind(d):
        return lax.rem(y - d + ny, ny)

    def remote(src, dst, send, recv, peer):
        return pltpu.make_async_remote_copy(
            src_ref=src, dst_ref=dst, send_sem=send, recv_sem=recv, device_id=peer, device_id_type=MESH
        )

    def all_sent(kind, ref):
        remote(ref, ref, sent.at[kind], got.at[0], other).wait_send()

    def all_got(kind, ref):
        remote(ref, ref, sent.at[0], got.at[kind], other).wait_recv()

    groups_of_places = [(0, 1)] + [(2 * k - 1, 2) for k in range(1, ny // 2)] + [(ny - 1, 1)]

    def chunk(place):
        return (place + 1) // 2 if place % 2 else (ny - place // 2) % ny

    def hand(e, number):
        places = pl.ds(*groups_of_places[number])
        if e == 2 and number != len(groups_of_places) - 1:
            return remote(xsend.at[2, places], xrelay.at[places], sent.at[2], relay_recv.at[number], at_x(far))
        return remote(xsend.at[e, places], xrecv.at[e, places], sent.at[2], got.at[1], at_x(e))

    def choose(number):
        first, count = groups_of_places[number]
        chunks = [chunk(first + k) for k in range(count)]
        ups = [ybuf[d, pl.ds(blocks, up.shape[0])].reshape(up_rows, cols) for d in chunks]
        chosen = jnp.dot(chooser[...], jnp.concatenate(ups, axis=1), preferred_element_type=F32).astype(BF16)
        for k in range(count):
            sel[k] = ybuf[chunks[k], pl.ds(0, blocks)]
        for e in (2, 1, 3, 0):

            def take(j):
                slot = table[e * SLOTS + j]
                for k in range(count):
                    if e == 0:
                        xrecv[0, first + k, j] = sel[k, slot]
                    else:
                        xsend[e, first + k, j] = sel[k, slot]

            loop(0, SLOTS, take)
            for k in range(count):
                rows = chosen[e * SLOTS * 4:(e + 1) * SLOTS * 4, k * cols:(k + 1) * cols].reshape(2, 16, cols)
                if e == 0:
                    xrecv[0, first + k, pl.ds(SLOTS, 2)] = rows
                else:
                    xsend[e, first + k, pl.ds(SLOTS, 2)] = rows
            if e:
                hand(e, number).start()

    def relay(number):
        if number != len(groups_of_places) - 1:
            hand(2, number).wait_recv()
            places = pl.ds(*groups_of_places[number])
            remote(xrelay.at[places], xrecv.at[2, places], sent.at[3], got.at[1], at_x(far)).start()

    def multiply(slot):
        place = lax.rem(z - slot + nz, nz)
        both = jnp.concatenate([wmine[place], wother[place]], axis=1)
        return jnp.dot(abuf[slot], both, preferred_element_type=F32)

    def multiply_pair(hop):
        def add(k):
            acc[...] += multiply(hop + k * (nz - 2 * hop))

        loop(0, 2, add)

    z_events, y_events = (list(ring.events()) for ring in (zring, yring))
    set_up_choice()
    choose(0)
    set_up()

    last_y = len(y_events) - 1
    for number, (hop, index) in enumerate(y_events):
        yring.advance(hop, index)
        if number == min(1, last_y):
            weights.start()
        if hop == yring.half or index == 1:
            choose(hop)
            relay(hop - 1)
        if number % 2 == 1 and number // 2 < len(z_events) - 4:
            zring.advance(*z_events[number // 2])
    for event in z_events[min(len(y_events) // 2, len(z_events) - 4):-3]:
        zring.advance(*event)
    local[6].wait()
    weights.wait_recv()
    acc[...] = multiply(0)
    multiply_pair(1)

    all_got(1, xrecv.at[pl.ds(1, nx - 1)])
    mine = permuted[...]
    total = jnp.zeros((tokens, PIECES * rank), F32)
    who = jnp.concatenate([var_wide[:, pl.ds(0, rank)]] * PIECES, axis=1)
    for v in range(VPG):
        factor = jnp.concatenate([xrecv[:, :, v * PIECES + p].reshape(depth, rank) for p in range(PIECES)], axis=1)
        total = jnp.where(who == v, jnp.dot(mine, factor, preferred_element_type=F32), total)
    for p in range(PIECES):
        sums[p] = total[:, p * rank:(p + 1) * rank]
    first = pair(1, sums.at[1 - core], sums_in)
    first.start()
    zring.advance(*z_events[-3])
    for hop in range(2, nz // 2 - 1):
        multiply_pair(hop)
    first.wait_recv()
    total = sums[core] + sums_in[...]
    whole[...] = total.reshape(nz, share, rank)
    parts[...] = total.astype(BF16).reshape(nz, share, rank)

    def scatter(e):
        return remote(parts.at[lax.rem(z + e, nz)], parts_in.at[e - 1], sent.at[4], got.at[2], at_z(e))

    def spread(e, side):
        shard = shrunk.at[core * nz + z]
        return remote(shard, shard, sent.at[5], got.at[3], at_z(e, side))

    loop(1, nz, lambda e: scatter(e).start())
    all_got(2, parts_in)
    shrunk[core * nz + z] = (whole[z] + jnp.sum(parts_in[...].astype(F32), axis=0)).astype(BF16)
    loop(1, nz, lambda e: [spread(e, side).start() for side in range(2)])
    spread(0, 1).start()

    zring.advance(*z_events[-2])
    multiply_pair(nz // 2 - 1)
    zring.advance(*z_events[-1])
    acc[...] += multiply(nz // 2)
    last = pair(2, acc.at[:, pl.ds(cols, cols)], swap_in)
    last.start()

    all_sent(0, abuf.at[pl.ds(0, nz - 1)])
    all_sent(1, ybuf.at[pl.ds(0, ny - 1)])
    all_sent(2, xsend.at[pl.ds(1, nx - 1)])
    all_sent(3, xrelay)
    all_sent(4, parts.at[pl.ds(0, nz - 1)])
    weights.wait_send()
    first.wait_send()
    all_got(3, shrunk.at[pl.ds(0, 2 * nz - 1)])
    wide = groups * 16
    both = jnp.concatenate([shrunk[pl.ds(p * nz, nz)].reshape(tokens, rank) for p in range(PIECES)], axis=1)
    opened = jnp.dot(both, opener[...], preferred_element_type=F32)
    total = acc[:, pl.ds(0, cols)]
    who = jnp.concatenate([var_wide[:, pl.ds(0, min(cols, wide))]] * max(wide // cols, 1), axis=1)
    which = (lax.broadcasted_iota(jnp.int32, (1, wide), 1) >> 3) & 1
    for h in range(2):
        part = jnp.where(who == which + 2 * h, opened, 0.0).astype(BF16)
        total += jnp.dot(part, xrecv[:, :, SLOTS + h].reshape(wide, cols), preferred_element_type=F32)
    last.wait_recv()
    out[...] = (total + swap_in[...]).astype(BF16)

    all_sent(5, shrunk.at[pl.ds(0, 2 * nz - 1)])
    last.wait_send()


def on_device(nx, ny, nz, act, weight, down, up, home, served, var):
    tokens, depth = act.shape
    cols = weight.shape[1]
    blocks, rank = down.shape[0], down.shape[2]
    groups = nx * ny
    served, var = served.T, var.T
    up = up.reshape(blocks * 4 // 16, 16, cols)
    weight = weight.reshape(nz, 2, depth, cols)
    hbm = pl.BlockSpec(memory_space=pl.ANY)
    vmem = pl.BlockSpec(memory_space=pltpu.VMEM)
    dma = pltpu.SemaphoreType.DMA
    share = tokens // nz
    scratch = [
        pltpu.VMEM((nz, tokens, depth), BF16),
        pltpu.VMEM((nz, depth, cols), BF16),
        pltpu.VMEM((nz, depth, cols), BF16),
        pltpu.VMEM((ny, blocks + up.shape[0], 16, rank), BF16),
        pltpu.VMEM((2,) + down.shape, BF16),
        pltpu.VMEM((nx, ny, SLOTS + 2, 16, rank), BF16),
        pltpu.VMEM((ny - 1, SLOTS + 2, 16, rank), BF16),
        pltpu.VMEM((nx, ny, SLOTS + 2, 16, rank), BF16),
        pltpu.VMEM((tokens, 2 * cols), F32),
        pltpu.VMEM((2, tokens, rank), F32),
        pltpu.VMEM((tokens, rank), F32),
        pltpu.VMEM((nz, share, rank), F32),
        pltpu.VMEM((nz, share, rank), BF16),
        pltpu.VMEM((nz - 1, share, rank), BF16),
        pltpu.VMEM((PIECES * nz, share, rank), BF16),
        pltpu.VMEM((tokens, cols), F32),
        pltpu.SMEM((nx * SLOTS,), jnp.int32),
        pltpu.SMEM(home.shape, jnp.int32),
        pltpu.SMEM(served.shape, jnp.int32),
        pltpu.VMEM(var.shape, jnp.int32),
        pltpu.VMEM((tokens, cols), jnp.int32),
        pltpu.VMEM((nx * SLOTS * 4, blocks * 4), BF16),
        pltpu.VMEM((PIECES * rank, groups * 16), BF16),
        pltpu.VMEM((tokens, depth), BF16),
        dma((7,)),
        dma((2, nz // 2, 2)), dma((2, ny // 2, 2)), dma((ny // 2,)),
        dma((6,)), dma((4,)), dma((3,)), dma((3,)),
    ]
    return pl.pallas_call(
        functools.partial(kernel, nx, ny, nz),
        out_shape=jax.ShapeDtypeStruct((tokens, cols), BF16),
        in_specs=[hbm] * 7,
        out_specs=vmem,
        scratch_shapes=scratch,
        compiler_params=pltpu.CompilerParams(
            collective_id=0, has_side_effects=True, vmem_limit_bytes=56 * 1024 * 1024
        ),
    )(act, weight, down, up, home, served, var)


def solution(mesh):
    nx = 4
    ny, nz = mesh.shape["grp"] // nx, mesh.shape["tp"] // 2
    in_specs = (
        P("grp", "tp"),
        P(None, "tp"),
        P(None, ("tp", "grp"), None),
        P(None, "grp", "tp"),
        P(),
        P(),
        P("grp", None),
    )
    return jax.shard_map(
        functools.partial(on_device, nx, ny, nz),
        mesh=mesh, in_specs=in_specs, out_specs=P("grp", "tp"), check_vma=False,
    )
```

```python
import functools

import jax
import jax.numpy as jnp
from jax import lax
from jax.experimental import pallas as pl
from jax.experimental.pallas import tpu as pltpu
from jax.sharding import PartitionSpec as P

PIECES = 2
VPG = 4
SLOTS = PIECES * VPG
MESH = pl.DeviceIdType.MESH
F32 = jnp.float32
BF16 = jnp.bfloat16


class Ring:
    def __init__(self, buf, pieces, peers, send, recv):
        self.buf, self.pieces, self.peers = buf, pieces, peers
        self.send, self.recv = send, recv
        self.n = buf.shape[0]
        self.half = self.n // 2
        self.size = buf.shape[1] // pieces

    def events(self):
        for hop in range(1, self.half):
            for index in range(self.pieces):
                yield hop, index
        for index in range(self.pieces // 2):
            yield self.half, index

    def cut(self, way, index):
        piece = index if way == 0 else self.pieces - 1 - index
        return pl.ds(piece * self.size, self.size)

    def slot(self, way, hop):
        return hop % self.n if way == 0 else (self.n - hop) % self.n

    def copy(self, way, hop, index):
        cut = self.cut(way, index)
        return pltpu.make_async_remote_copy(
            src_ref=self.buf.at[self.slot(way, hop - 1), cut],
            dst_ref=self.buf.at[self.slot(way, hop), cut],
            send_sem=self.send,
            recv_sem=self.recv.at[way, hop - 1, index],
            device_id=self.peers[way],
            device_id_type=MESH,
        )

    def start(self):
        for index in range(self.pieces):
            for way in range(2):
                self.copy(way, 1, index).start()

    def advance(self, hop, index):
        for way in range(2):
            self.copy(way, hop, index).wait_recv()
            if hop + 1 < self.half or (hop + 1 == self.half and index < self.pieces // 2):
                self.copy(way, hop + 1, index).start()


def loop(first, end, body):
    def step(k, carry):
        body(k)
        return carry

    lax.fori_loop(first, end, step, 0)


def kernel(
    nx, ny, nz,
    act, weight, down, up, home, served, var, out,
    abuf, wmine, wother, ybuf, sel, xsend, xrelay, xrecv,
    acc, whole, parts, parts_in, shrunk, swap_in, table, homes, lists, var_row, var_wide,
    chooser, opener,
    permuted, local_sem, z_recv, y_recv, relay_recv, sent, got, pair_send, pair_recv,
):
    grp, tp = lax.axis_index("grp"), lax.axis_index("tp")
    x, y = grp // ny, lax.rem(grp, ny)
    z, core = tp // 2, lax.rem(tp, 2)
    tokens = out.shape[0]
    cols = out.shape[1]
    groups = nx * ny
    blocks = down.shape[0]
    far = 1 - 2 * core

    def at_x(step):
        return (lax.rem(x + step + nx, nx) * ny + y, tp)

    def at_y(step):
        return (x * ny + lax.rem(y + step + ny, ny), tp)

    def at_z(step, side=0):
        return (grp, lax.rem(z + step + nz, nz) * 2 + (core if side == 0 else 1 - core))

    other = (grp, z * 2 + 1 - core)

    local = [
        pltpu.make_async_copy(home, homes, local_sem.at[4]),
        pltpu.make_async_copy(served, lists, local_sem.at[5]),
        pltpu.make_async_copy(down, ybuf.at[0, pl.ds(0, blocks)], local_sem.at[1]),
        pltpu.make_async_copy(act, abuf.at[0], local_sem.at[0]),
        pltpu.make_async_copy(up, ybuf.at[0, pl.ds(blocks, up.shape[0])], local_sem.at[2]),
        pltpu.make_async_copy(var, var_row, local_sem.at[6]),
        pltpu.make_async_copy(weight.at[:, core], wmine, local_sem.at[3]),
    ]
    for copy in local:
        copy.start()

    barrier = pltpu.get_barrier_semaphore()

    def greet(partner):
        pl.semaphore_signal(barrier, inc=1, device_id=partner, device_id_type=MESH)

    greet(other)
    greet(at_y(1))
    greet(at_y(-1))
    loop(1, nx, lambda e: greet(at_x(e)))
    loop(1, nz, lambda e: [greet(at_z(e, side)) for side in range(2)])

    local[0].wait()
    local[1].wait()

    def fill(k, carry):
        owner = lax.rem(x + k // SLOTS, nx) * ny + y
        j = lax.rem(k, SLOTS)
        table[k] = homes[lists[j // PIECES, owner] * PIECES + lax.rem(j, PIECES)]
        return carry

    lax.fori_loop(0, nx * SLOTS, fill, 0)
    up_rows = up.shape[0] * up.shape[1]
    rank = xrecv.shape[-1]
    depth = act.shape[1]
    share = tokens // nz

    def set_up_choice():
        shape = chooser.shape
        line = lax.broadcasted_iota(jnp.int32, shape, 0)

        def pick(k, rows):
            return jnp.where((line >> 2) == k, table[k], rows)

        rows = lax.fori_loop(0, nx * SLOTS, pick, jnp.zeros(shape, jnp.int32), unroll=4)
        wanted = rows * 4 + (line & 3)
        chooser[...] = (wanted == lax.broadcasted_iota(jnp.int32, shape, 1)).astype(F32).astype(BF16)

    def sources(e):
        width = ny * 16
        place = lax.broadcasted_iota(jnp.int32, (1, width), 1) >> 4
        behind_y = jnp.where((place & 1) == 1, (place + 1) >> 1, ny - (place >> 1))
        return pl.ds(e * width, width), lax.rem(x + nx - e, nx) * ny + ((y - behind_y) & (ny - 1))

    def set_up():
        for e in range(nx):
            columns, from_group = sources(e)
            width = ny * 16
            row = lax.broadcasted_iota(jnp.int32, (depth, width), 0)
            column = lax.broadcasted_iota(jnp.int32, (depth, width), 1)
            hit = row == from_group * 16 + (column & 15)
            moved = jnp.dot(abuf[0], hit.astype(F32).astype(BF16), preferred_element_type=F32)
            permuted[:, columns] = moved.astype(BF16)

    def set_up_last():
        for e in range(nx):
            columns, from_group = sources(e)
            width = ny * 16
            row = lax.broadcasted_iota(jnp.int32, (PIECES * rank, width), 0)
            column = lax.broadcasted_iota(jnp.int32, (PIECES * rank, width), 1)
            hit = row == ((column >> 2) & 1) * rank + from_group * 4 + (column & 3)
            opener[:, columns] = hit.astype(F32).astype(BF16)

    def set_up_tokens():
        local[5].wait()
        for i in range(0, tokens, cols):
            size = min(cols, tokens - i)
            row = jnp.broadcast_to(var_row[:, pl.ds(i, size)], (cols, size))
            var_wide[pl.ds(i, size), :] = row.T

    pl.semaphore_wait(barrier, nx + 2 * nz)

    zring = Ring(abuf, 2, (at_z(1), at_z(-1)), sent.at[0], z_recv)
    yring = Ring(ybuf, 4, (at_y(1), at_y(-1)), sent.at[1], y_recv)

    def pair(index, src, dst):
        return pltpu.make_async_remote_copy(
            src_ref=src, dst_ref=dst, send_sem=pair_send.at[index], recv_sem=pair_recv.at[index],
            device_id=other, device_id_type=MESH,
        )

    local[2].wait()
    local[4].wait()
    yring.start()
    local[3].wait()
    zring.start()
    weights = pair(0, weight.at[:, 1 - core], wother)

    def behind(d):
        return lax.rem(y - d + ny, ny)

    def remote(src, dst, send, recv, peer):
        return pltpu.make_async_remote_copy(
            src_ref=src, dst_ref=dst, send_sem=send, recv_sem=recv, device_id=peer, device_id_type=MESH
        )

    def all_sent(kind, ref):
        remote(ref, ref, sent.at[kind], got.at[0], other).wait_send()

    def all_got(kind, ref):
        remote(ref, ref, sent.at[0], got.at[kind], other).wait_recv()

    groups_of_places = [(0, 1)] + [(2 * k - 1, 2) for k in range(1, ny // 2)] + [(ny - 1, 1)]

    def chunk(place):
        return (place + 1) // 2 if place % 2 else (ny - place // 2) % ny

    def hand(e, number):
        places = pl.ds(*groups_of_places[number])
        if e == 2 and number != len(groups_of_places) - 1:
            return remote(xsend.at[2, places], xrelay.at[places], sent.at[2], relay_recv.at[number], at_x(far))
        return remote(xsend.at[e, places], xrecv.at[e, places], sent.at[2], got.at[1], at_x(e))

    def choose(number):
        first, count = groups_of_places[number]
        chunks = [chunk(first + k) for k in range(count)]
        ups = [ybuf[d, pl.ds(blocks, up.shape[0])].reshape(up_rows, cols) for d in chunks]
        chosen = jnp.dot(chooser[...], jnp.concatenate(ups, axis=1), preferred_element_type=F32).astype(BF16)
        for k in range(count):
            sel[k] = ybuf[chunks[k], pl.ds(0, blocks)]
        for e in (2, 1, 3, 0):

            def take(j):
                slot = table[e * SLOTS + j]
                for k in range(count):
                    if e == 0:
                        xrecv[0, first + k, j] = sel[k, slot]
                    else:
                        xsend[e, first + k, j] = sel[k, slot]

            for j in range(SLOTS):
                take(j)
            for k in range(count):
                rows = chosen[e * SLOTS * 4:(e + 1) * SLOTS * 4, k * cols:(k + 1) * cols].reshape(2, 16, cols)
                if e == 0:
                    xrecv[0, first + k, pl.ds(SLOTS, 2)] = rows
                else:
                    xsend[e, first + k, pl.ds(SLOTS, 2)] = rows
            if e:
                hand(e, number).start()

    def relay(number):
        if number != len(groups_of_places) - 1:
            hand(2, number).wait_recv()
            places = pl.ds(*groups_of_places[number])
            remote(xrelay.at[places], xrecv.at[2, places], sent.at[3], got.at[1], at_x(far)).start()

    def multiply(slot):
        place = lax.rem(z - slot + nz, nz)
        both = jnp.concatenate([wmine[place], wother[place]], axis=1)
        return jnp.dot(abuf[slot], both, preferred_element_type=F32)

    def multiply_pair(hop):
        def add(k):
            acc[...] += multiply(hop + k * (nz - 2 * hop))

        loop(0, 2, add)

    z_events, y_events = (list(ring.events()) for ring in (zring, yring))
    set_up_choice()
    choose(0)
    set_up()

    for number, (hop, index) in enumerate(y_events):
        yring.advance(hop, index)
        if number + 1 == len(y_events) or y_events[number + 1][0] > hop:
            choose(hop)
            relay(hop - 1)
            if hop == 1:
                weights.start()
        if hop > 1 and index == 1:
            zring.advance(*z_events[hop - 2])
    set_up_tokens()
    for event in z_events[yring.half - 1:-3]:
        zring.advance(*event)

    all_got(1, xrecv.at[pl.ds(1, nx - 1)])
    mine = permuted[...]
    total = jnp.zeros((tokens, PIECES * rank), F32)
    who = jnp.concatenate([var_wide[:, pl.ds(0, rank)]] * PIECES, axis=1)
    for v in range(VPG):
        factor = jnp.concatenate([xrecv[:, :, v * PIECES + p].reshape(depth, rank) for p in range(PIECES)], axis=1)
        total = jnp.where(who == v, jnp.dot(mine, factor, preferred_element_type=F32), total)
    for p in range(PIECES):
        part = total[:, p * rank:(p + 1) * rank]
        parts[p] = part.astype(BF16).reshape(nz, share, rank)
        whole[p] = part.reshape(nz, share, rank)

    def scatter(e, side):
        source = parts.at[core if side == 0 else 1 - core, lax.rem(z + e, nz)]
        return remote(source, parts_in.at[side * nz + e], sent.at[4], got.at[2], at_z(e, side))

    def spread(e, side):
        shard = shrunk.at[core * nz + z]
        return remote(shard, shard, sent.at[5], got.at[3], at_z(e, side))

    loop(1, nz, lambda e: [scatter(e, side).start() for side in range(2)])
    scatter(0, 1).start()
    zring.advance(*z_events[-3])
    set_up_last()
    local[6].wait()
    weights.wait_recv()
    acc[...] = multiply(0)
    multiply_pair(1)
    all_got(2, parts_in.at[pl.ds(1, 2 * nz - 1)])
    others = jnp.sum(parts_in[pl.ds(1, 2 * nz - 1)].astype(F32), axis=0)
    shrunk[core * nz + z] = (whole[core, z] + others).astype(BF16)
    loop(1, nz, lambda e: [spread(e, side).start() for side in range(2)])
    spread(0, 1).start()
    for hop in range(2, nz // 2 - 1):
        multiply_pair(hop)

    zring.advance(*z_events[-2])
    multiply_pair(nz // 2 - 1)
    zring.advance(*z_events[-1])
    acc[...] += multiply(nz // 2)
    last = pair(1, acc.at[:, pl.ds(cols, cols)], swap_in)
    last.start()

    all_sent(0, abuf.at[pl.ds(0, nz - 1)])
    all_sent(1, ybuf.at[pl.ds(0, ny - 1)])
    all_sent(2, xsend.at[pl.ds(1, nx - 1)])
    all_sent(3, xrelay)
    all_sent(4, parts_in.at[pl.ds(1, 2 * nz - 1)])
    weights.wait_send()
    all_got(3, shrunk.at[pl.ds(0, 2 * nz - 1)])
    wide = groups * 16
    both = jnp.concatenate([shrunk[pl.ds(p * nz, nz)].reshape(tokens, rank) for p in range(PIECES)], axis=1)
    opened = jnp.dot(both, opener[...], preferred_element_type=F32)
    total = acc[:, pl.ds(0, cols)]
    who = jnp.concatenate([var_wide[:, pl.ds(0, min(cols, wide))]] * max(wide // cols, 1), axis=1)
    which = (lax.broadcasted_iota(jnp.int32, (1, wide), 1) >> 3) & 1
    for h in range(2):
        part = jnp.where(who == which + 2 * h, opened, 0.0).astype(BF16)
        total += jnp.dot(part, xrecv[:, :, SLOTS + h].reshape(wide, cols), preferred_element_type=F32)
    last.wait_recv()
    out[...] = (total + swap_in[...]).astype(BF16)

    all_sent(5, shrunk.at[pl.ds(0, 2 * nz - 1)])
    last.wait_send()


def on_device(nx, ny, nz, act, weight, down, up, home, served, var):
    tokens, depth = act.shape
    cols = weight.shape[1]
    blocks, rank = down.shape[0], down.shape[2]
    groups = nx * ny
    served, var = served.T, var.T
    up = up.reshape(blocks * 4 // 16, 16, cols)
    weight = weight.reshape(nz, 2, depth, cols)
    hbm = pl.BlockSpec(memory_space=pl.ANY)
    vmem = pl.BlockSpec(memory_space=pltpu.VMEM)
    dma = pltpu.SemaphoreType.DMA
    share = tokens // nz
    scratch = [
        pltpu.VMEM((nz, tokens, depth), BF16),
        pltpu.VMEM((nz, depth, cols), BF16),
        pltpu.VMEM((nz, depth, cols), BF16),
        pltpu.VMEM((ny, blocks + up.shape[0], 16, rank), BF16),
        pltpu.VMEM((2,) + down.shape, BF16),
        pltpu.VMEM((nx, ny, SLOTS + 2, 16, rank), BF16),
        pltpu.VMEM((ny - 1, SLOTS + 2, 16, rank), BF16),
        pltpu.VMEM((nx, ny, SLOTS + 2, 16, rank), BF16),
        pltpu.VMEM((tokens, 2 * cols), F32),
        pltpu.VMEM((PIECES, nz, share, rank), F32),
        pltpu.VMEM((PIECES, nz, share, rank), BF16),
        pltpu.VMEM((2 * nz, share, rank), BF16),
        pltpu.VMEM((PIECES * nz, share, rank), BF16),
        pltpu.VMEM((tokens, cols), F32),
        pltpu.SMEM((nx * SLOTS,), jnp.int32),
        pltpu.SMEM(home.shape, jnp.int32),
        pltpu.SMEM(served.shape, jnp.int32),
        pltpu.VMEM(var.shape, jnp.int32),
        pltpu.VMEM((tokens, cols), jnp.int32),
        pltpu.VMEM((nx * SLOTS * 4, blocks * 4), BF16),
        pltpu.VMEM((PIECES * rank, groups * 16), BF16),
        pltpu.VMEM((tokens, depth), BF16),
        dma((7,)),
        dma((2, nz // 2, 2)), dma((2, ny // 2, 4)), dma((ny // 2,)),
        dma((6,)), dma((4,)), dma((2,)), dma((2,)),
    ]
    return pl.pallas_call(
        functools.partial(kernel, nx, ny, nz),
        out_shape=jax.ShapeDtypeStruct((tokens, cols), BF16),
        in_specs=[hbm] * 7,
        out_specs=vmem,
        scratch_shapes=scratch,
        compiler_params=pltpu.CompilerParams(
            collective_id=0, has_side_effects=True, vmem_limit_bytes=56 * 1024 * 1024
        ),
    )(act, weight, down, up, home, served, var)


def solution(mesh):
    nx = 4
    ny, nz = mesh.shape["grp"] // nx, mesh.shape["tp"] // 2
    in_specs = (
        P("grp", "tp"),
        P(None, "tp"),
        P(None, ("tp", "grp"), None),
        P(None, "grp", "tp"),
        P(),
        P(),
        P("grp", None),
    )
    return jax.shard_map(
        functools.partial(on_device, nx, ny, nz),
        mesh=mesh, in_specs=in_specs, out_specs=P("grp", "tp"), check_vma=False,
    )
```

```python
import functools

import jax
import jax.numpy as jnp
from jax import lax
from jax.experimental import pallas as pl
from jax.experimental.pallas import tpu as pltpu
from jax.sharding import PartitionSpec as P

PIECES = 2
VPG = 4
SLOTS = PIECES * VPG
MESH = pl.DeviceIdType.MESH
F32 = jnp.float32
BF16 = jnp.bfloat16


class Ring:
    def __init__(self, buf, pieces, peers, send, recv):
        self.buf, self.pieces, self.peers = buf, pieces, peers
        self.send, self.recv = send, recv
        self.n = buf.shape[0]
        self.half = self.n // 2
        self.size = buf.shape[1] // pieces

    def events(self):
        for hop in range(1, self.half):
            for index in range(self.pieces):
                yield hop, index
        for index in range(self.pieces // 2):
            yield self.half, index

    def cut(self, way, index):
        piece = index if way == 0 else self.pieces - 1 - index
        return pl.ds(piece * self.size, self.size)

    def slot(self, way, hop):
        return hop % self.n if way == 0 else (self.n - hop) % self.n

    def copy(self, way, hop, index):
        cut = self.cut(way, index)
        return pltpu.make_async_remote_copy(
            src_ref=self.buf.at[self.slot(way, hop - 1), cut],
            dst_ref=self.buf.at[self.slot(way, hop), cut],
            send_sem=self.send,
            recv_sem=self.recv.at[way, hop - 1, index],
            device_id=self.peers[way],
            device_id_type=MESH,
        )

    def start(self):
        for index in range(self.pieces):
            for way in range(2):
                self.copy(way, 1, index).start()

    def advance(self, hop, index):
        for way in range(2):
            self.copy(way, hop, index).wait_recv()
            if hop + 1 < self.half or (hop + 1 == self.half and index < self.pieces // 2):
                self.copy(way, hop + 1, index).start()


def loop(first, end, body):
    def step(k, carry):
        body(k)
        return carry

    lax.fori_loop(first, end, step, 0)


def kernel(
    nx, ny, nz,
    act, weight, down, up, home, served, var, out,
    abuf, wmine, wother, ybuf, ubuf, sel, xsend, xrelay, xrecv, usend, urecv,
    acc, whole, parts, parts_in, shrunk, swap_in, table, homes, lists, var_row, var_wide,
    chooser, opener,
    permuted, local_sem, z_recv, y_recv, u_recv, relay_recv, sent, got, pair_send, pair_recv,
):
    grp, tp = lax.axis_index("grp"), lax.axis_index("tp")
    x, y = grp // ny, lax.rem(grp, ny)
    z, core = tp // 2, lax.rem(tp, 2)
    tokens = out.shape[0]
    cols = out.shape[1]
    groups = nx * ny
    far = 1 - 2 * core

    def at_x(step):
        return (lax.rem(x + step + nx, nx) * ny + y, tp)

    def at_y(step):
        return (x * ny + lax.rem(y + step + ny, ny), tp)

    def at_z(step, side=0):
        return (grp, lax.rem(z + step + nz, nz) * 2 + (core if side == 0 else 1 - core))

    other = (grp, z * 2 + 1 - core)

    local = [
        pltpu.make_async_copy(home, homes, local_sem.at[4]),
        pltpu.make_async_copy(served, lists, local_sem.at[5]),
        pltpu.make_async_copy(down, ybuf.at[0], local_sem.at[1]),
        pltpu.make_async_copy(act, abuf.at[0], local_sem.at[0]),
        pltpu.make_async_copy(up, ubuf.at[0], local_sem.at[2]),
        pltpu.make_async_copy(var, var_row, local_sem.at[6]),
        pltpu.make_async_copy(weight.at[:, core], wmine, local_sem.at[3]),
    ]
    for copy in local:
        copy.start()

    barrier = pltpu.get_barrier_semaphore()

    def greet(partner):
        pl.semaphore_signal(barrier, inc=1, device_id=partner, device_id_type=MESH)

    greet(other)
    greet(at_y(1))
    greet(at_y(-1))
    loop(1, nx, lambda e: greet(at_x(e)))
    loop(1, nz, lambda e: [greet(at_z(e, side)) for side in range(2)])

    local[0].wait()
    local[1].wait()

    def fill(k, carry):
        owner = lax.rem(x + k // SLOTS, nx) * ny + y
        j = lax.rem(k, SLOTS)
        table[k] = homes[lists[j // PIECES, owner] * PIECES + lax.rem(j, PIECES)]
        return carry

    lax.fori_loop(0, nx * SLOTS, fill, 0)
    up_rows = up.shape[0] * up.shape[1]
    rank = xrecv.shape[-1]
    depth = act.shape[1]
    share = tokens // nz

    def set_up_choice():
        shape = chooser.shape
        line = lax.broadcasted_iota(jnp.int32, shape, 0)

        def pick(k, rows):
            return jnp.where((line >> 2) == k, table[k], rows)

        rows = lax.fori_loop(0, nx * SLOTS, pick, jnp.zeros(shape, jnp.int32), unroll=4)
        wanted = rows * 4 + (line & 3)
        chooser[...] = (wanted == lax.broadcasted_iota(jnp.int32, shape, 1)).astype(F32).astype(BF16)

    def sources(e):
        width = ny * 16
        place = lax.broadcasted_iota(jnp.int32, (1, width), 1) >> 4
        behind_y = jnp.where((place & 1) == 1, (place + 1) >> 1, ny - (place >> 1))
        return pl.ds(e * width, width), lax.rem(x + nx - e, nx) * ny + ((y - behind_y) & (ny - 1))

    def set_up():
        for e in range(nx):
            columns, from_group = sources(e)
            width = ny * 16
            row = lax.broadcasted_iota(jnp.int32, (depth, width), 0)
            column = lax.broadcasted_iota(jnp.int32, (depth, width), 1)
            hit = row == from_group * 16 + (column & 15)
            moved = jnp.dot(abuf[0], hit.astype(F32).astype(BF16), preferred_element_type=F32)
            permuted[:, columns] = moved.astype(BF16)

    def set_up_last():
        for e in range(nx):
            columns, from_group = sources(e)
            width = ny * 16
            row = lax.broadcasted_iota(jnp.int32, (PIECES * rank, width), 0)
            column = lax.broadcasted_iota(jnp.int32, (PIECES * rank, width), 1)
            hit = row == ((column >> 2) & 1) * rank + from_group * 4 + (column & 3)
            opener[:, columns] = hit.astype(F32).astype(BF16)

    def set_up_tokens():
        local[5].wait()
        for i in range(0, tokens, cols):
            size = min(cols, tokens - i)
            row = jnp.broadcast_to(var_row[:, pl.ds(i, size)], (cols, size))
            var_wide[pl.ds(i, size), :] = row.T

    pl.semaphore_wait(barrier, nx + 2 * nz)

    zring = Ring(abuf, 2, (at_z(1), at_z(-1)), sent.at[0], z_recv)
    yring = Ring(ybuf, 4, (at_y(1), at_y(-1)), sent.at[1], y_recv)
    uring = Ring(ubuf, 2, (at_y(1), at_y(-1)), sent.at[6], u_recv)

    def pair(index, src, dst):
        return pltpu.make_async_remote_copy(
            src_ref=src, dst_ref=dst, send_sem=pair_send.at[index], recv_sem=pair_recv.at[index],
            device_id=other, device_id_type=MESH,
        )

    local[2].wait()
    yring.start()
    local[3].wait()
    zring.start()
    weights = pair(0, weight.at[:, 1 - core], wother)

    def behind(d):
        return lax.rem(y - d + ny, ny)

    def remote(src, dst, send, recv, peer):
        return pltpu.make_async_remote_copy(
            src_ref=src, dst_ref=dst, send_sem=send, recv_sem=recv, device_id=peer, device_id_type=MESH
        )

    def all_sent(kind, ref):
        remote(ref, ref, sent.at[kind], got.at[0], other).wait_send()

    def all_got(kind, ref):
        remote(ref, ref, sent.at[0], got.at[kind], other).wait_recv()

    groups_of_places = [(0, 1)] + [(2 * k - 1, 2) for k in range(1, ny // 2)] + [(ny - 1, 1)]

    def chunk(place):
        return (place + 1) // 2 if place % 2 else (ny - place // 2) % ny

    def hand(e, number):
        places = pl.ds(*groups_of_places[number])
        if e == 2 and number != len(groups_of_places) - 1:
            return remote(xsend.at[2, places], xrelay.at[places], sent.at[2], relay_recv.at[number], at_x(far))
        return remote(xsend.at[e, places], xrecv.at[e, places], sent.at[2], got.at[1], at_x(e))

    def choose(number):
        first, count = groups_of_places[number]
        chunks = [chunk(first + k) for k in range(count)]
        for k in range(count):
            sel[k] = ybuf[chunks[k]]
        for e in (2, 1, 3, 0):

            def take(j):
                slot = table[e * SLOTS + j]
                for k in range(count):
                    if e == 0:
                        xrecv[0, first + k, j] = sel[k, slot]
                    else:
                        xsend[e, first + k, j] = sel[k, slot]

            for j in range(SLOTS):
                take(j)
            if e:
                hand(e, number).start()

    def choose_up():
        ups = [ubuf[chunk(place)].reshape(up_rows, cols) for place in range(ny)]
        chosen = jnp.dot(chooser[...], jnp.concatenate(ups, axis=1), preferred_element_type=F32).astype(BF16)
        for place in range(ny):
            rows = chosen[:, place * cols:(place + 1) * cols].reshape(nx, 2, 16, cols)
            for e in range(nx):
                usend[e, place] = rows[e]

    def hand_up(e):
        return remote(usend.at[e], urecv.at[e], sent.at[7], got.at[0], at_x(e))

    def relay(number):
        if number != len(groups_of_places) - 1:
            hand(2, number).wait_recv()
            places = pl.ds(*groups_of_places[number])
            remote(xrelay.at[places], xrecv.at[2, places], sent.at[3], got.at[1], at_x(far)).start()

    def multiply(slot):
        place = lax.rem(z - slot + nz, nz)
        both = jnp.concatenate([wmine[place], wother[place]], axis=1)
        return jnp.dot(abuf[slot], both, preferred_element_type=F32)

    def multiply_pair(hop):
        def add(k):
            acc[...] += multiply(hop + k * (nz - 2 * hop))

        loop(0, 2, add)

    z_events, y_events = (list(ring.events()) for ring in (zring, yring))
    choose(0)
    set_up_choice()
    set_up()

    for number, (hop, index) in enumerate(y_events):
        if index == 0 and hop < yring.half:
            zring.advance(*z_events[hop - 1])
        yring.advance(hop, index)
        if number + 1 == len(y_events) or y_events[number + 1][0] > hop:
            choose(hop)
            relay(hop - 1)
            if hop == 1:
                local[4].wait()
                uring.start()
                weights.start()
            else:
                for event in uring.events():
                    if event[0] == hop - 1:
                        uring.advance(*event)
    for event in z_events[yring.half - 1:-3]:
        zring.advance(*event)
    set_up_tokens()

    all_got(1, xrecv.at[pl.ds(1, nx - 1)])
    mine = permuted[...]
    total = jnp.zeros((tokens, PIECES * rank), F32)
    who = jnp.concatenate([var_wide[:, pl.ds(0, rank)]] * PIECES, axis=1)
    for v in range(VPG):
        factor = jnp.concatenate([xrecv[:, :, v * PIECES + p].reshape(depth, rank) for p in range(PIECES)], axis=1)
        total = jnp.where(who == v, jnp.dot(mine, factor, preferred_element_type=F32), total)
    for p in range(PIECES):
        part = total[:, p * rank:(p + 1) * rank]
        parts[p] = part.astype(BF16).reshape(nz, share, rank)
        whole[p] = part.reshape(nz, share, rank)

    def scatter(e, side):
        source = parts.at[core if side == 0 else 1 - core, lax.rem(z + e, nz)]
        return remote(source, parts_in.at[side * nz + e], sent.at[4], got.at[2], at_z(e, side))

    def spread(e, side):
        shard = shrunk.at[core * nz + z]
        return remote(shard, shard, sent.at[5], got.at[3], at_z(e, side))

    loop(1, nz, lambda e: [scatter(e, side).start() for side in range(2)])
    scatter(0, 1).start()
    zring.advance(*z_events[-3])
    for event in uring.events():
        if event[0] == uring.half:
            uring.advance(*event)
    choose_up()
    loop(1, nx, lambda e: hand_up(e).start())
    urecv[0] = usend[0]
    set_up_last()
    local[6].wait()
    weights.wait_recv()
    acc[...] = multiply(0)
    multiply_pair(1)
    all_got(2, parts_in.at[pl.ds(1, 2 * nz - 1)])
    others = jnp.sum(parts_in[pl.ds(1, 2 * nz - 1)].astype(F32), axis=0)
    shrunk[core * nz + z] = (whole[core, z] + others).astype(BF16)
    loop(1, nz, lambda e: [spread(e, side).start() for side in range(2)])
    spread(0, 1).start()
    for hop in range(2, nz // 2 - 1):
        multiply_pair(hop)

    zring.advance(*z_events[-2])
    multiply_pair(nz // 2 - 1)
    zring.advance(*z_events[-1])
    acc[...] += multiply(nz // 2)
    last = pair(1, acc.at[:, pl.ds(cols, cols)], swap_in)
    last.start()

    all_sent(0, abuf.at[pl.ds(0, nz - 1)])
    all_sent(1, ybuf.at[pl.ds(0, ny - 1)])
    all_sent(2, xsend.at[pl.ds(1, nx - 1)])
    all_sent(3, xrelay)
    all_sent(4, parts_in.at[pl.ds(1, 2 * nz - 1)])
    all_sent(6, ubuf.at[pl.ds(0, ny - 1)])
    all_sent(7, usend.at[pl.ds(1, nx - 1)])
    weights.wait_send()
    all_got(0, urecv.at[pl.ds(1, nx - 1)])
    all_got(3, shrunk.at[pl.ds(0, 2 * nz - 1)])
    wide = groups * 16
    both = jnp.concatenate([shrunk[pl.ds(p * nz, nz)].reshape(tokens, rank) for p in range(PIECES)], axis=1)
    opened = jnp.dot(both, opener[...], preferred_element_type=F32)
    total = acc[:, pl.ds(0, cols)]
    who = jnp.concatenate([var_wide[:, pl.ds(0, min(cols, wide))]] * max(wide // cols, 1), axis=1)
    which = (lax.broadcasted_iota(jnp.int32, (1, wide), 1) >> 3) & 1
    for h in range(2):
        part = jnp.where(who == which + 2 * h, opened, 0.0).astype(BF16)
        total += jnp.dot(part, urecv[:, :, h].reshape(wide, cols), preferred_element_type=F32)
    last.wait_recv()
    out[...] = (total + swap_in[...]).astype(BF16)

    all_sent(5, shrunk.at[pl.ds(0, 2 * nz - 1)])
    last.wait_send()


def on_device(nx, ny, nz, act, weight, down, up, home, served, var):
    tokens, depth = act.shape
    cols = weight.shape[1]
    blocks, rank = down.shape[0], down.shape[2]
    groups = nx * ny
    served, var = served.T, var.T
    up = up.reshape(blocks * 4 // 16, 16, cols)
    weight = weight.reshape(nz, 2, depth, cols)
    hbm = pl.BlockSpec(memory_space=pl.ANY)
    vmem = pl.BlockSpec(memory_space=pltpu.VMEM)
    dma = pltpu.SemaphoreType.DMA
    share = tokens // nz
    scratch = [
        pltpu.VMEM((nz, tokens, depth), BF16),
        pltpu.VMEM((nz, depth, cols), BF16),
        pltpu.VMEM((nz, depth, cols), BF16),
        pltpu.VMEM((ny,) + down.shape, BF16),
        pltpu.VMEM((ny,) + up.shape, BF16),
        pltpu.VMEM((2,) + down.shape, BF16),
        pltpu.VMEM((nx, ny, SLOTS, 16, rank), BF16),
        pltpu.VMEM((ny - 1, SLOTS, 16, rank), BF16),
        pltpu.VMEM((nx, ny, SLOTS, 16, rank), BF16),
        pltpu.VMEM((nx, ny, 2, 16, cols), BF16),
        pltpu.VMEM((nx, ny, 2, 16, cols), BF16),
        pltpu.VMEM((tokens, 2 * cols), F32),
        pltpu.VMEM((PIECES, nz, share, rank), F32),
        pltpu.VMEM((PIECES, nz, share, rank), BF16),
        pltpu.VMEM((2 * nz, share, rank), BF16),
        pltpu.VMEM((PIECES * nz, share, rank), BF16),
        pltpu.VMEM((tokens, cols), F32),
        pltpu.SMEM((nx * SLOTS,), jnp.int32),
        pltpu.SMEM(home.shape, jnp.int32),
        pltpu.SMEM(served.shape, jnp.int32),
        pltpu.VMEM(var.shape, jnp.int32),
        pltpu.VMEM((tokens, cols), jnp.int32),
        pltpu.VMEM((nx * SLOTS * 4, blocks * 4), BF16),
        pltpu.VMEM((PIECES * rank, groups * 16), BF16),
        pltpu.VMEM((tokens, depth), BF16),
        dma((7,)),
        dma((2, nz // 2, 2)), dma((2, ny // 2, 4)), dma((2, ny // 2, 2)), dma((ny // 2,)),
        dma((8,)), dma((4,)), dma((2,)), dma((2,)),
    ]
    return pl.pallas_call(
        functools.partial(kernel, nx, ny, nz),
        out_shape=jax.ShapeDtypeStruct((tokens, cols), BF16),
        in_specs=[hbm] * 7,
        out_specs=vmem,
        scratch_shapes=scratch,
        compiler_params=pltpu.CompilerParams(
            collective_id=0, has_side_effects=True, vmem_limit_bytes=56 * 1024 * 1024
        ),
    )(act, weight, down, up, home, served, var)


def solution(mesh):
    nx = 4
    ny, nz = mesh.shape["grp"] // nx, mesh.shape["tp"] // 2
    in_specs = (
        P("grp", "tp"),
        P(None, "tp"),
        P(None, ("tp", "grp"), None),
        P(None, "grp", "tp"),
        P(),
        P(),
        P("grp", None),
    )
    return jax.shard_map(
        functools.partial(on_device, nx, ny, nz),
        mesh=mesh, in_specs=in_specs, out_specs=P("grp", "tp"), check_vma=False,
    )
```

```python
import functools

import jax
import jax.numpy as jnp
from jax import lax
from jax.experimental import pallas as pl
from jax.experimental.pallas import tpu as pltpu
from jax.sharding import PartitionSpec as P

PIECES = 2
VPG = 4
SLOTS = PIECES * VPG
MESH = pl.DeviceIdType.MESH
F32 = jnp.float32
BF16 = jnp.bfloat16


class Ring:
    def __init__(self, buf, pieces, peers, send, recv):
        self.buf, self.pieces, self.peers = buf, pieces, peers
        self.send, self.recv = send, recv
        self.n = buf.shape[0]
        self.half = self.n // 2
        self.size = buf.shape[1] // pieces

    def events(self):
        for hop in range(1, self.half):
            for index in range(self.pieces):
                yield hop, index
        for index in range(self.pieces // 2):
            yield self.half, index

    def cut(self, way, index):
        piece = index if way == 0 else self.pieces - 1 - index
        return pl.ds(piece * self.size, self.size)

    def slot(self, way, hop):
        return hop % self.n if way == 0 else (self.n - hop) % self.n

    def copy(self, way, hop, index):
        cut = self.cut(way, index)
        return pltpu.make_async_remote_copy(
            src_ref=self.buf.at[self.slot(way, hop - 1), cut],
            dst_ref=self.buf.at[self.slot(way, hop), cut],
            send_sem=self.send,
            recv_sem=self.recv.at[way, hop - 1, index],
            device_id=self.peers[way],
            device_id_type=MESH,
        )

    def start(self):
        for index in range(self.pieces):
            for way in range(2):
                self.copy(way, 1, index).start()

    def advance(self, hop, index):
        for way in range(2):
            self.copy(way, hop, index).wait_recv()
            if hop + 1 < self.half or (hop + 1 == self.half and index < self.pieces // 2):
                self.copy(way, hop + 1, index).start()


def loop(first, end, body):
    def step(k, carry):
        body(k)
        return carry

    lax.fori_loop(first, end, step, 0)


def kernel(
    nx, ny, nz,
    act, weight, down, up, home, served, var, out,
    abuf, wmine, wother, ybuf, ubuf, sel, xsend, xrelay, xrecv, usend, urecv, uother,
    acc, sums, sums_in, whole, parts, parts_in, shrunk, swap_in, table, homes, lists, var_row, var_wide,
    chooser, opener,
    permuted, local_sem, z_recv, y_recv, u_recv, relay_recv, sent, got, pair_send, pair_recv,
):
    grp, tp = lax.axis_index("grp"), lax.axis_index("tp")
    x, y = grp // ny, lax.rem(grp, ny)
    z, core = tp // 2, lax.rem(tp, 2)
    tokens = out.shape[0]
    cols = out.shape[1]
    groups = nx * ny
    far = 1 - 2 * core

    def at_x(step):
        return (lax.rem(x + step + nx, nx) * ny + y, tp)

    def at_y(step):
        return (x * ny + lax.rem(y + step + ny, ny), tp)

    def at_z(step):
        return (grp, lax.rem(z + step + nz, nz) * 2 + core)

    other = (grp, z * 2 + 1 - core)

    local = [
        pltpu.make_async_copy(home, homes, local_sem.at[4]),
        pltpu.make_async_copy(served, lists, local_sem.at[5]),
        pltpu.make_async_copy(down, ybuf.at[0], local_sem.at[1]),
        pltpu.make_async_copy(act, abuf.at[0], local_sem.at[0]),
        pltpu.make_async_copy(up, ubuf.at[0], local_sem.at[2]),
        pltpu.make_async_copy(var, var_row, local_sem.at[6]),
        pltpu.make_async_copy(weight.at[:, core], wmine, local_sem.at[3]),
    ]
    for copy in local:
        copy.start()

    barrier = pltpu.get_barrier_semaphore()

    def greet(partner):
        pl.semaphore_signal(barrier, inc=1, device_id=partner, device_id_type=MESH)

    greet(other)
    greet(at_y(1))
    greet(at_y(-1))
    loop(1, nx, lambda e: greet(at_x(e)))
    loop(1, nz, lambda e: greet(at_z(e)))

    local[0].wait()
    local[1].wait()

    def fill(k, carry):
        owner = lax.rem(x + k // SLOTS, nx) * ny + y
        j = lax.rem(k, SLOTS)
        table[k] = homes[lists[j // PIECES, owner] * PIECES + lax.rem(j, PIECES)]
        return carry

    lax.fori_loop(0, nx * SLOTS, fill, 0)
    up_rows = up.shape[0] * up.shape[1]
    rank = xrecv.shape[-1]
    depth = act.shape[1]
    share = tokens // nz

    def set_up_choice():
        shape = chooser.shape
        line = lax.broadcasted_iota(jnp.int32, shape, 0)

        def pick(k, rows):
            return jnp.where((line >> 2) == k, table[k], rows)

        rows = lax.fori_loop(0, nx * SLOTS, pick, jnp.zeros(shape, jnp.int32), unroll=4)
        wanted = rows * 4 + (line & 3)
        chooser[...] = (wanted == lax.broadcasted_iota(jnp.int32, shape, 1)).astype(F32).astype(BF16)

    def sources(e):
        width = ny * 16
        place = lax.broadcasted_iota(jnp.int32, (1, width), 1) >> 4
        behind_y = jnp.where((place & 1) == 1, (place + 1) >> 1, ny - (place >> 1))
        return pl.ds(e * width, width), lax.rem(x + nx - e, nx) * ny + ((y - behind_y) & (ny - 1))

    def set_up():
        for e in range(nx):
            columns, from_group = sources(e)
            width = ny * 16
            row = lax.broadcasted_iota(jnp.int32, (depth, width), 0)
            column = lax.broadcasted_iota(jnp.int32, (depth, width), 1)
            hit = row == from_group * 16 + (column & 15)
            moved = jnp.dot(abuf[0], hit.astype(F32).astype(BF16), preferred_element_type=F32)
            permuted[:, columns] = moved.astype(BF16)

    def set_up_last():
        for e in range(nx):
            columns, from_group = sources(e)
            width = ny * 16
            row = lax.broadcasted_iota(jnp.int32, (rank, width), 0)
            column = lax.broadcasted_iota(jnp.int32, (rank, width), 1)
            hit = (row == from_group * 4 + (column & 3)) & (((column >> 2) & 1) == core)
            opener[:, columns] = hit.astype(F32).astype(BF16)

    def set_up_tokens():
        local[5].wait()
        for i in range(0, tokens, cols):
            size = min(cols, tokens - i)
            row = jnp.broadcast_to(var_row[:, pl.ds(i, size)], (cols, size))
            var_wide[pl.ds(i, size), :] = row.T

    pl.semaphore_wait(barrier, nx + nz + 1)

    zring = Ring(abuf, 4, (at_z(1), at_z(-1)), sent.at[0], z_recv)
    yring = Ring(ybuf, 4, (at_y(1), at_y(-1)), sent.at[1], y_recv)
    uring = Ring(ubuf, 2, (at_y(1), at_y(-1)), sent.at[6], u_recv)

    def pair(index, src, dst):
        return pltpu.make_async_remote_copy(
            src_ref=src, dst_ref=dst, send_sem=pair_send.at[index], recv_sem=pair_recv.at[index],
            device_id=other, device_id_type=MESH,
        )

    local[2].wait()
    yring.start()
    local[3].wait()
    zring.start()
    weights = pair(0, weight.at[:, 1 - core], wother)

    def behind(d):
        return lax.rem(y - d + ny, ny)

    def remote(src, dst, send, recv, peer):
        return pltpu.make_async_remote_copy(
            src_ref=src, dst_ref=dst, send_sem=send, recv_sem=recv, device_id=peer, device_id_type=MESH
        )

    def all_sent(kind, ref):
        remote(ref, ref, sent.at[kind], got.at[0], other).wait_send()

    def all_got(kind, ref):
        remote(ref, ref, sent.at[0], got.at[kind], other).wait_recv()

    groups_of_places = [(0, 1)] + [(2 * k - 1, 2) for k in range(1, ny // 2)] + [(ny - 1, 1)]

    def chunk(place):
        return (place + 1) // 2 if place % 2 else (ny - place // 2) % ny

    def hand(e, number):
        places = pl.ds(*groups_of_places[number])
        if e == 2 and number != len(groups_of_places) - 1:
            return remote(xsend.at[2, places], xrelay.at[places], sent.at[2], relay_recv.at[number], at_x(far))
        return remote(xsend.at[e, places], xrecv.at[e, places], sent.at[2], got.at[1], at_x(e))

    def choose(number):
        first, count = groups_of_places[number]
        chunks = [chunk(first + k) for k in range(count)]
        for k in range(count):
            sel[k] = ybuf[chunks[k]]
        for e in (2, 1, 3, 0):

            def take(j):
                slot = table[e * SLOTS + j]
                for k in range(count):
                    if e == 0:
                        xrecv[0, first + k, j] = sel[k, slot]
                    else:
                        xsend[e, first + k, j] = sel[k, slot]

            for j in range(SLOTS):
                take(j)
            if e:
                hand(e, number).start()

    def choose_up():
        ups = [ubuf[chunk(place)].reshape(up_rows, cols) for place in range(ny)]
        chosen = jnp.dot(chooser[...], jnp.concatenate(ups, axis=1), preferred_element_type=F32).astype(BF16)
        for place in range(ny):
            rows = chosen[:, place * cols:(place + 1) * cols].reshape(nx, 2, 16, cols)
            for e in range(nx):
                usend[e, place] = rows[e]

    def hand_up(e):
        return remote(usend.at[e], urecv.at[e], sent.at[7], got.at[0], at_x(e))

    def relay(number):
        if number != len(groups_of_places) - 1:
            hand(2, number).wait_recv()
            places = pl.ds(*groups_of_places[number])
            remote(xrelay.at[places], xrecv.at[2, places], sent.at[3], got.at[1], at_x(far)).start()

    def multiply(slot):
        place = lax.rem(z - slot + nz, nz)
        both = jnp.concatenate([wmine[place], wother[place]], axis=1)
        return jnp.dot(abuf[slot], both, preferred_element_type=F32)

    def multiply_pair(hop):
        z_step(max(0, len(waiting) - sum(event[0] > hop for event in z_events)))

        def add(k):
            acc[...] += multiply(hop + k * (nz - 2 * hop))

        loop(0, 2, add)

    z_events, y_events = (list(ring.events()) for ring in (zring, yring))
    choose(0)
    set_up_choice()
    set_up()

    waiting = list(z_events)

    def z_step(count):
        for event in waiting[:count]:
            zring.advance(*event)
        del waiting[:count]

    for number, (hop, index) in enumerate(y_events):
        yring.advance(hop, index)
        if number + 1 == len(y_events) or y_events[number + 1][0] > hop:
            choose(hop)
            relay(hop - 1)
            z_step(1)
            if hop == 1:
                local[4].wait()
                uring.start()
                weights.start()
            else:
                for event in uring.events():
                    if event[0] == hop - 1:
                        uring.advance(*event)
        elif index == 1:
            z_step(1)
    z_step(2)
    set_up_tokens()

    all_got(1, xrecv.at[pl.ds(1, nx - 1)])
    mine = permuted[...]
    total = jnp.zeros((tokens, PIECES * rank), F32)
    who = jnp.concatenate([var_wide[:, pl.ds(0, rank)]] * PIECES, axis=1)
    for v in range(VPG):
        factor = jnp.concatenate([xrecv[:, :, v * PIECES + p].reshape(depth, rank) for p in range(PIECES)], axis=1)
        total = jnp.where(who == v, jnp.dot(mine, factor, preferred_element_type=F32), total)
    for p in range(PIECES):
        sums[p] = total[:, p * rank:(p + 1) * rank]
    first = pair(1, sums.at[1 - core], sums_in)
    first.start()
    z_step(1)
    first.wait_recv()
    total = sums[core] + sums_in[...]
    whole[...] = total.reshape(nz, share, rank)
    parts[...] = total.astype(BF16).reshape(nz, share, rank)

    def scatter(e):
        return remote(parts.at[lax.rem(z + e, nz)], parts_in.at[e - 1], sent.at[4], got.at[2], at_z(e))

    def spread(e):
        return remote(shrunk.at[z], shrunk.at[z], sent.at[5], got.at[3], at_z(e))

    loop(1, nz, lambda e: scatter(e).start())
    z_step(1)
    for event in uring.events():
        if event[0] == uring.half:
            uring.advance(*event)
    choose_up()
    loop(1, nx, lambda e: hand_up(e).start())
    urecv[0] = usend[0]
    set_up_last()
    all_got(2, parts_in)
    shrunk[z] = (whole[z] + jnp.sum(parts_in[...].astype(F32), axis=0)).astype(BF16)
    loop(1, nz, lambda e: spread(e).start())
    z_step(1)
    local[6].wait()
    weights.wait_recv()
    acc[...] = multiply(0)
    multiply_pair(1)
    all_got(0, urecv.at[pl.ds(1, nx - 1)])
    ups = pair(2, urecv, uother)
    ups.start()
    for hop in range(2, nz // 2 - 1):
        multiply_pair(hop)
    ups.wait_recv()

    all_got(3, shrunk.at[pl.ds(0, nz - 1)])
    wide = groups * 16
    opened = jnp.dot(shrunk[...].reshape(tokens, rank), opener[...], preferred_element_type=F32)
    who = jnp.concatenate([var_wide[:, pl.ds(0, min(cols, wide))]] * max(wide // cols, 1), axis=1)
    which = (lax.broadcasted_iota(jnp.int32, (1, wide), 1) >> 3) & 1
    for h in range(2):
        part = jnp.where(who == which + 2 * h, opened, 0.0).astype(BF16)
        both = jnp.concatenate([side[:, :, h].reshape(wide, cols) for side in (urecv, uother)], axis=1)
        acc[...] += jnp.dot(part, both, preferred_element_type=F32)

    multiply_pair(nz // 2 - 1)
    all_sent(1, ybuf.at[pl.ds(0, ny - 1)])
    all_sent(2, xsend.at[pl.ds(1, nx - 1)])
    all_sent(3, xrelay)
    all_sent(4, parts_in)
    all_sent(5, shrunk.at[pl.ds(0, nz - 1)])
    all_sent(6, ubuf.at[pl.ds(0, ny - 1)])
    all_sent(7, usend.at[pl.ds(1, nx - 1)])
    weights.wait_send()
    first.wait_send()
    ups.wait_send()
    z_step(len(waiting))
    acc[...] += multiply(nz // 2)
    last = pair(3, acc.at[:, pl.ds(cols, cols)], swap_in)
    last.start()
    all_sent(0, abuf.at[pl.ds(0, nz - 1)])
    last.wait_recv()
    out[...] = (acc[:, pl.ds(0, cols)] + swap_in[...]).astype(BF16)
    last.wait_send()


def on_device(nx, ny, nz, act, weight, down, up, home, served, var):
    tokens, depth = act.shape
    cols = weight.shape[1]
    blocks, rank = down.shape[0], down.shape[2]
    groups = nx * ny
    served, var = served.T, var.T
    up = up.reshape(blocks * 4 // 16, 16, cols)
    weight = weight.reshape(nz, 2, depth, cols)
    hbm = pl.BlockSpec(memory_space=pl.ANY)
    vmem = pl.BlockSpec(memory_space=pltpu.VMEM)
    dma = pltpu.SemaphoreType.DMA
    share = tokens // nz
    scratch = [
        pltpu.VMEM((nz, tokens, depth), BF16),
        pltpu.VMEM((nz, depth, cols), BF16),
        pltpu.VMEM((nz, depth, cols), BF16),
        pltpu.VMEM((ny,) + down.shape, BF16),
        pltpu.VMEM((ny,) + up.shape, BF16),
        pltpu.VMEM((2,) + down.shape, BF16),
        pltpu.VMEM((nx, ny, SLOTS, 16, rank), BF16),
        pltpu.VMEM((ny - 1, SLOTS, 16, rank), BF16),
        pltpu.VMEM((nx, ny, SLOTS, 16, rank), BF16),
        pltpu.VMEM((nx, ny, 2, 16, cols), BF16),
        pltpu.VMEM((nx, ny, 2, 16, cols), BF16),
        pltpu.VMEM((nx, ny, 2, 16, cols), BF16),
        pltpu.VMEM((tokens, 2 * cols), F32),
        pltpu.VMEM((PIECES, tokens, rank), F32),
        pltpu.VMEM((tokens, rank), F32),
        pltpu.VMEM((nz, share, rank), F32),
        pltpu.VMEM((nz, share, rank), BF16),
        pltpu.VMEM((nz - 1, share, rank), BF16),
        pltpu.VMEM((nz, share, rank), BF16),
        pltpu.VMEM((tokens, cols), F32),
        pltpu.SMEM((nx * SLOTS,), jnp.int32),
        pltpu.SMEM(home.shape, jnp.int32),
        pltpu.SMEM(served.shape, jnp.int32),
        pltpu.VMEM(var.shape, jnp.int32),
        pltpu.VMEM((tokens, cols), jnp.int32),
        pltpu.VMEM((nx * SLOTS * 4, blocks * 4), BF16),
        pltpu.VMEM((rank, groups * 16), BF16),
        pltpu.VMEM((tokens, depth), BF16),
        dma((7,)),
        dma((2, nz // 2, 4)), dma((2, ny // 2, 4)), dma((2, ny // 2, 2)), dma((ny // 2,)),
        dma((8,)), dma((4,)), dma((4,)), dma((4,)),
    ]
    return pl.pallas_call(
        functools.partial(kernel, nx, ny, nz),
        out_shape=jax.ShapeDtypeStruct((tokens, cols), BF16),
        in_specs=[hbm] * 7,
        out_specs=vmem,
        scratch_shapes=scratch,
        compiler_params=pltpu.CompilerParams(
            collective_id=0, has_side_effects=True, vmem_limit_bytes=56 * 1024 * 1024
        ),
    )(act, weight, down, up, home, served, var)


def solution(mesh):
    nx = 4
    ny, nz = mesh.shape["grp"] // nx, mesh.shape["tp"] // 2
    in_specs = (
        P("grp", "tp"),
        P(None, "tp"),
        P(None, ("tp", "grp"), None),
        P(None, "grp", "tp"),
        P(),
        P(),
        P("grp", None),
    )
    return jax.shard_map(
        functools.partial(on_device, nx, ny, nz),
        mesh=mesh, in_specs=in_specs, out_specs=P("grp", "tp"), check_vma=False,
    )
```

```python
import functools

import jax
import jax.numpy as jnp
from jax import lax
from jax.experimental import pallas as pl
from jax.experimental.pallas import tpu as pltpu
from jax.sharding import PartitionSpec as P

PIECES = 2
VPG = 4
SLOTS = PIECES * VPG
MESH = pl.DeviceIdType.MESH
F32 = jnp.float32
BF16 = jnp.bfloat16


class Ring:
    def __init__(self, buf, pieces, peers, send, recv):
        self.buf, self.pieces, self.peers = buf, pieces, peers
        self.send, self.recv = send, recv
        self.n = buf.shape[0]
        self.half = self.n // 2
        self.size = buf.shape[1] // pieces

    def events(self):
        for hop in range(1, self.half):
            for index in range(self.pieces):
                yield hop, index
        for index in range(self.pieces // 2):
            yield self.half, index

    def cut(self, way, index):
        piece = index if way == 0 else self.pieces - 1 - index
        return pl.ds(piece * self.size, self.size)

    def slot(self, way, hop):
        return hop % self.n if way == 0 else (self.n - hop) % self.n

    def copy(self, way, hop, index):
        cut = self.cut(way, index)
        return pltpu.make_async_remote_copy(
            src_ref=self.buf.at[self.slot(way, hop - 1), cut],
            dst_ref=self.buf.at[self.slot(way, hop), cut],
            send_sem=self.send,
            recv_sem=self.recv.at[way, hop - 1, index],
            device_id=self.peers[way],
            device_id_type=MESH,
        )

    def start(self):
        for index in range(self.pieces):
            for way in range(2):
                self.copy(way, 1, index).start()

    def advance(self, hop, index):
        for way in range(2):
            self.copy(way, hop, index).wait_recv()
            if hop + 1 < self.half or (hop + 1 == self.half and index < self.pieces // 2):
                self.copy(way, hop + 1, index).start()


def loop(first, end, body):
    def step(k, carry):
        body(k)
        return carry

    lax.fori_loop(first, end, step, 0)


def kernel(
    nx, ny, nz,
    act, weight, down, up, home, served, var, out,
    abuf, wmine, wother, ybuf, ubuf, sel, xsend, xrelay, xrecv, usend, urecv, uother,
    acc, sums, sums_in, whole, parts, parts_in, shrunk, swap_in, table, homes, lists, var_row, var_wide,
    chooser, opener,
    permuted, early, local_sem, z_recv, y_recv, u_recv, relay_recv, sent, got, pair_send, pair_recv,
):
    grp, tp = lax.axis_index("grp"), lax.axis_index("tp")
    x, y = grp // ny, lax.rem(grp, ny)
    z, core = tp // 2, lax.rem(tp, 2)
    tokens = out.shape[0]
    cols = out.shape[1]
    groups = nx * ny
    far = 1 - 2 * core

    def at_x(step):
        return (lax.rem(x + step + nx, nx) * ny + y, tp)

    def at_y(step):
        return (x * ny + lax.rem(y + step + ny, ny), tp)

    def at_z(step):
        return (grp, lax.rem(z + step + nz, nz) * 2 + core)

    other = (grp, z * 2 + 1 - core)

    barrier = pltpu.get_barrier_semaphore()

    def greet(partner):
        pl.semaphore_signal(barrier, inc=1, device_id=partner, device_id_type=MESH)

    greet(other)
    greet(at_y(1))
    greet(at_y(-1))
    loop(1, nx, lambda e: greet(at_x(e)))
    loop(1, nz, lambda e: greet(at_z(e)))

    local = [
        pltpu.make_async_copy(home, homes, local_sem.at[4]),
        pltpu.make_async_copy(served, lists, local_sem.at[5]),
        pltpu.make_async_copy(down, ybuf.at[0], local_sem.at[1]),
        pltpu.make_async_copy(act, abuf.at[0], local_sem.at[0]),
        pltpu.make_async_copy(up, ubuf.at[0], local_sem.at[2]),
        pltpu.make_async_copy(var, var_row, local_sem.at[6]),
        pltpu.make_async_copy(weight.at[:, core], wmine, local_sem.at[3]),
    ]
    for copy in local:
        copy.start()

    local[0].wait()
    local[1].wait()

    def fill(k, carry):
        owner = lax.rem(x + k // SLOTS, nx) * ny + y
        j = lax.rem(k, SLOTS)
        table[k] = homes[lists[j // PIECES, owner] * PIECES + lax.rem(j, PIECES)]
        return carry

    lax.fori_loop(0, nx * SLOTS, fill, 0)
    up_rows = up.shape[0] * up.shape[1]
    rank = xrecv.shape[-1]
    depth = act.shape[1]
    share = tokens // nz

    def set_up_choice():
        shape = chooser.shape
        line = lax.broadcasted_iota(jnp.int32, shape, 0)

        def pick(k, rows):
            return jnp.where((line >> 2) == k, table[k], rows)

        rows = lax.fori_loop(0, nx * SLOTS, pick, jnp.zeros(shape, jnp.int32), unroll=4)
        wanted = rows * 4 + (line & 3)
        chooser[...] = (wanted == lax.broadcasted_iota(jnp.int32, shape, 1)).astype(F32).astype(BF16)

    def sources(e):
        width = ny * 16
        place = lax.broadcasted_iota(jnp.int32, (1, width), 1) >> 4
        behind_y = jnp.where((place & 1) == 1, (place + 1) >> 1, ny - (place >> 1))
        return pl.ds(e * width, width), lax.rem(x + nx - e, nx) * ny + ((y - behind_y) & (ny - 1))

    def set_up():
        width = min(128, depth)
        for at in range(0, depth, width):
            column = lax.broadcasted_iota(jnp.int32, (1, width), 1) + at
            place = column >> 6
            e = (column >> 4) & (nx - 1)
            behind_y = jnp.where((place & 1) == 1, (place + 1) >> 1, ny - (place >> 1))
            from_group = ((x - e) & (nx - 1)) * ny + ((y - behind_y) & (ny - 1))
            row = lax.broadcasted_iota(jnp.int32, (depth, width), 0)
            hit = row == from_group * 16 + (column & 15)
            moved = jnp.dot(abuf[0], hit.astype(F32).astype(BF16), preferred_element_type=F32)
            permuted[:, at:at + width] = moved.astype(BF16)

    def set_up_last():
        for e in range(nx):
            columns, from_group = sources(e)
            width = ny * 16
            row = lax.broadcasted_iota(jnp.int32, (rank, width), 0)
            column = lax.broadcasted_iota(jnp.int32, (rank, width), 1)
            hit = (row == from_group * 4 + (column & 3)) & (((column >> 2) & 1) == core)
            opener[:, columns] = hit.astype(F32).astype(BF16)

    def set_up_tokens():
        local[5].wait()
        for i in range(0, tokens, cols):
            size = min(cols, tokens - i)
            row = jnp.broadcast_to(var_row[:, pl.ds(i, size)], (cols, size))
            var_wide[pl.ds(i, size), :] = row.T

    pl.semaphore_wait(barrier, nx + nz + 1)

    zring = Ring(abuf, 4, (at_z(1), at_z(-1)), sent.at[0], z_recv)
    yring = Ring(ybuf, 4, (at_y(1), at_y(-1)), sent.at[1], y_recv)
    uring = Ring(ubuf, 2, (at_y(1), at_y(-1)), sent.at[6], u_recv)

    def pair(index, src, dst):
        return pltpu.make_async_remote_copy(
            src_ref=src, dst_ref=dst, send_sem=pair_send.at[index], recv_sem=pair_recv.at[index],
            device_id=other, device_id_type=MESH,
        )

    local[2].wait()
    yring.start()
    local[3].wait()
    zring.start()
    weights = pair(0, weight.at[:, 1 - core], wother)

    def behind(d):
        return lax.rem(y - d + ny, ny)

    def remote(src, dst, send, recv, peer):
        return pltpu.make_async_remote_copy(
            src_ref=src, dst_ref=dst, send_sem=send, recv_sem=recv, device_id=peer, device_id_type=MESH
        )

    def all_sent(kind, ref):
        remote(ref, ref, sent.at[kind], got.at[0], other).wait_send()

    def all_got(kind, ref):
        remote(ref, ref, sent.at[0], got.at[kind], other).wait_recv()

    groups_of_places = [(0, 1)] + [(2 * k - 1, 2) for k in range(1, ny // 2)] + [(ny - 1, 1)]

    def chunk(place):
        return (place + 1) // 2 if place % 2 else (ny - place // 2) % ny

    def turn(number):
        return 1 if number < len(groups_of_places) - 2 else 4

    def hand(e, number):
        places = pl.ds(*groups_of_places[number])
        if e == 2 and number != len(groups_of_places) - 1:
            return remote(xsend.at[2, places], xrelay.at[places], sent.at[2], relay_recv.at[number], at_x(far))
        return remote(xsend.at[e, places], xrecv.at[places, e], sent.at[2], got.at[turn(number)], at_x(e))

    def choose(number):
        first, count = groups_of_places[number]
        chunks = [chunk(first + k) for k in range(count)]
        for k in range(count):
            sel[k] = ybuf[chunks[k]]
        for e in (2, 1, 3, 0):

            def take(j):
                slot = table[e * SLOTS + j]
                for k in range(count):
                    if e == 0:
                        xrecv[first + k, 0, j] = sel[k, slot]
                    else:
                        xsend[e, first + k, j] = sel[k, slot]

            for j in range(SLOTS):
                take(j)
            if e:
                hand(e, number).start()

    def choose_up():
        ups = [ubuf[chunk(place)].reshape(up_rows, cols) for place in range(ny)]
        chosen = jnp.dot(chooser[...], jnp.concatenate(ups, axis=1), preferred_element_type=F32).astype(BF16)
        for place in range(ny):
            rows = chosen[:, place * cols:(place + 1) * cols].reshape(nx, 2, 16, cols)
            for e in range(nx):
                usend[e, place] = rows[e]

    def hand_up(e):
        return remote(usend.at[e], urecv.at[e], sent.at[7], got.at[0], at_x(e))

    def relay(number):
        if number != len(groups_of_places) - 1:
            hand(2, number).wait_recv()
            places = pl.ds(*groups_of_places[number])
            remote(xrelay.at[places], xrecv.at[places, 2], sent.at[3], got.at[turn(number)], at_x(far)).start()

    def multiply(slot):
        place = lax.rem(z - slot + nz, nz)
        both = jnp.concatenate([wmine[place], wother[place]], axis=1)
        return jnp.dot(abuf[slot], both, preferred_element_type=F32)

    def multiply_pair(hop):
        z_step(max(0, len(waiting) - sum(event[0] > hop for event in z_events)))

        def add(k):
            acc[...] += multiply(hop + k * (nz - 2 * hop))

        loop(0, 2, add)

    z_events, y_events = (list(ring.events()) for ring in (zring, yring))
    choose(0)
    set_up_choice()
    set_up()

    def u_step(hop):
        for event in uring.events():
            if event[0] == hop and hop > 0:
                uring.advance(*event)

    waiting = list(z_events)

    def z_step(count):
        for event in waiting[:count]:
            zring.advance(*event)
        del waiting[:count]

    for number, (hop, index) in enumerate(y_events):
        yring.advance(hop, index)
        if number + 1 == len(y_events) or y_events[number + 1][0] > hop:
            choose(hop)
            relay(hop - 1)
            z_step(1)
            if hop == 1:
                weights.start()
            if hop == min(2, yring.half):
                local[4].wait()
                uring.start()
            u_step(hop - 2)
        elif index == 1:
            z_step(1)
    z_step(2)
    set_up_tokens()

    cut = groups_of_places[-2][0] if ny > 2 else 0
    who = jnp.concatenate([var_wide[:, pl.ds(0, rank)]] * PIECES, axis=1)

    def shrink(first, end):
        mine = permuted[:, first * nx * 16:end * nx * 16]
        total = jnp.zeros((tokens, PIECES * rank), F32)
        for v in range(VPG):
            slots = [xrecv[first:end, :, v * PIECES + p].reshape(-1, rank) for p in range(PIECES)]
            product = jnp.dot(mine, jnp.concatenate(slots, axis=1), preferred_element_type=F32)
            total = jnp.where(who == v, product, total)
        return total

    if cut:
        all_got(1, xrecv.at[pl.ds(0, cut), pl.ds(1, nx - 1)])
        early[...] = shrink(0, cut)
    all_got(4, xrecv.at[pl.ds(cut, ny - cut), pl.ds(1, nx - 1)])
    total = shrink(cut, ny)
    if cut:
        total += early[...]
    for p in range(PIECES):
        sums[p] = total[:, p * rank:(p + 1) * rank]
    first = pair(1, sums.at[1 - core], sums_in)
    first.start()
    z_step(1)
    if uring.half > 1:
        u_step(uring.half - 1)
    first.wait_recv()
    total = sums[core] + sums_in[...]
    whole[...] = total.reshape(nz, share, rank)
    parts[...] = total.astype(BF16).reshape(nz, share, rank)

    def scatter(e):
        return remote(parts.at[lax.rem(z + e, nz)], parts_in.at[e - 1], sent.at[4], got.at[2], at_z(e))

    def spread(e):
        return remote(shrunk.at[z], shrunk.at[z], sent.at[5], got.at[3], at_z(e))

    loop(1, nz, lambda e: scatter(e).start())
    z_step(1)
    u_step(uring.half)
    choose_up()
    loop(1, nx, lambda e: hand_up(e).start())
    urecv[0] = usend[0]
    set_up_last()
    all_got(2, parts_in)
    shrunk[z] = (whole[z] + jnp.sum(parts_in[...].astype(F32), axis=0)).astype(BF16)
    loop(1, nz, lambda e: spread(e).start())
    z_step(1)
    local[6].wait()
    weights.wait_recv()
    acc[...] = multiply(0)
    multiply_pair(1)
    all_got(0, urecv.at[pl.ds(1, nx - 1)])
    ups = pair(2, urecv, uother)
    ups.start()
    for hop in range(2, min(3, nz // 2)):
        multiply_pair(hop)
    ups.wait_recv()

    all_got(3, shrunk.at[pl.ds(0, nz - 1)])
    wide = groups * 16
    opened = jnp.dot(shrunk[...].reshape(tokens, rank), opener[...], preferred_element_type=F32)
    who = jnp.concatenate([var_wide[:, pl.ds(0, min(cols, wide))]] * max(wide // cols, 1), axis=1)
    which = (lax.broadcasted_iota(jnp.int32, (1, wide), 1) >> 3) & 1
    for h in range(2):
        part = jnp.where(who == which + 2 * h, opened, 0.0).astype(BF16)
        both = jnp.concatenate([side[:, :, h].reshape(wide, cols) for side in (urecv, uother)], axis=1)
        acc[...] += jnp.dot(part, both, preferred_element_type=F32)

    for hop in range(3, nz // 2):
        multiply_pair(hop)
    all_sent(1, ybuf.at[pl.ds(0, ny - 1)])
    all_sent(2, xsend.at[pl.ds(1, nx - 1)])
    all_sent(3, xrelay)
    all_sent(4, parts_in)
    all_sent(5, shrunk.at[pl.ds(0, nz - 1)])
    all_sent(6, ubuf.at[pl.ds(0, ny - 1)])
    all_sent(7, usend.at[pl.ds(1, nx - 1)])
    weights.wait_send()
    first.wait_send()
    ups.wait_send()
    z_step(len(waiting))
    acc[...] += multiply(nz // 2)
    last = pair(3, acc.at[:, pl.ds(cols, cols)], swap_in)
    last.start()
    all_sent(0, abuf.at[pl.ds(0, nz - 1)])
    last.wait_recv()
    out[...] = (acc[:, pl.ds(0, cols)] + swap_in[...]).astype(BF16)
    last.wait_send()


def on_device(nx, ny, nz, act, weight, down, up, home, served, var):
    tokens, depth = act.shape
    cols = weight.shape[1]
    blocks, rank = down.shape[0], down.shape[2]
    groups = nx * ny
    served, var = served.T, var.T
    up = up.reshape(blocks * 4 // 16, 16, cols)
    weight = weight.reshape(nz, 2, depth, cols)
    hbm = pl.BlockSpec(memory_space=pl.ANY)
    vmem = pl.BlockSpec(memory_space=pltpu.VMEM)
    dma = pltpu.SemaphoreType.DMA
    share = tokens // nz
    scratch = [
        pltpu.VMEM((nz, tokens, depth), BF16),
        pltpu.VMEM((nz, depth, cols), BF16),
        pltpu.VMEM((nz, depth, cols), BF16),
        pltpu.VMEM((ny,) + down.shape, BF16),
        pltpu.VMEM((ny,) + up.shape, BF16),
        pltpu.VMEM((2,) + down.shape, BF16),
        pltpu.VMEM((nx, ny, SLOTS, 16, rank), BF16),
        pltpu.VMEM((ny - 1, SLOTS, 16, rank), BF16),
        pltpu.VMEM((ny, nx, SLOTS, 16, rank), BF16),
        pltpu.VMEM((nx, ny, 2, 16, cols), BF16),
        pltpu.VMEM((nx, ny, 2, 16, cols), BF16),
        pltpu.VMEM((nx, ny, 2, 16, cols), BF16),
        pltpu.VMEM((tokens, 2 * cols), F32),
        pltpu.VMEM((PIECES, tokens, rank), F32),
        pltpu.VMEM((tokens, rank), F32),
        pltpu.VMEM((nz, share, rank), F32),
        pltpu.VMEM((nz, share, rank), BF16),
        pltpu.VMEM((nz - 1, share, rank), BF16),
        pltpu.VMEM((nz, share, rank), BF16),
        pltpu.VMEM((tokens, cols), F32),
        pltpu.SMEM((nx * SLOTS,), jnp.int32),
        pltpu.SMEM(home.shape, jnp.int32),
        pltpu.SMEM(served.shape, jnp.int32),
        pltpu.VMEM(var.shape, jnp.int32),
        pltpu.VMEM((tokens, cols), jnp.int32),
        pltpu.VMEM((nx * SLOTS * 4, blocks * 4), BF16),
        pltpu.VMEM((rank, groups * 16), BF16),
        pltpu.VMEM((tokens, depth), BF16),
        pltpu.VMEM((tokens, PIECES * rank), F32),
        dma((7,)),
        dma((2, nz // 2, 4)), dma((2, ny // 2, 4)), dma((2, ny // 2, 2)), dma((ny // 2,)),
        dma((8,)), dma((5,)), dma((4,)), dma((4,)),
    ]
    return pl.pallas_call(
        functools.partial(kernel, nx, ny, nz),
        out_shape=jax.ShapeDtypeStruct((tokens, cols), BF16),
        in_specs=[hbm] * 7,
        out_specs=vmem,
        scratch_shapes=scratch,
        compiler_params=pltpu.CompilerParams(
            collective_id=0, has_side_effects=True, vmem_limit_bytes=56 * 1024 * 1024
        ),
    )(act, weight, down, up, home, served, var)


def solution(mesh):
    nx = 4
    ny, nz = mesh.shape["grp"] // nx, mesh.shape["tp"] // 2
    in_specs = (
        P("grp", "tp"),
        P(None, "tp"),
        P(None, ("tp", "grp"), None),
        P(None, "grp", "tp"),
        P(),
        P(),
        P("grp", None),
    )
    return jax.shard_map(
        functools.partial(on_device, nx, ny, nz),
        mesh=mesh, in_specs=in_specs, out_specs=P("grp", "tp"), check_vma=False,
    )
```

```python
import functools

import jax
import jax.numpy as jnp
from jax import lax
from jax.experimental import pallas as pl
from jax.experimental.pallas import tpu as pltpu
from jax.sharding import PartitionSpec as P

PIECES = 2
VPG = 4
SLOTS = PIECES * VPG
MESH = pl.DeviceIdType.MESH
F32 = jnp.float32
BF16 = jnp.bfloat16


class Ring:
    def __init__(self, own, buf, pieces, peers, send, recv):
        self.own, self.buf, self.pieces, self.peers = own, buf, pieces, peers
        self.send, self.recv = send, recv
        self.n = buf.shape[0]
        self.half = self.n // 2
        self.size = buf.shape[1] // pieces

    def events(self):
        for hop in range(1, self.half):
            for index in range(self.pieces):
                yield hop, index
        for index in range(self.pieces // 2):
            yield self.half, index

    def cut(self, way, index):
        piece = index if way == 0 else self.pieces - 1 - index
        return pl.ds(piece * self.size, self.size)

    def slot(self, way, hop):
        return hop % self.n if way == 0 else (self.n - hop) % self.n

    def copy(self, way, hop, index):
        cut = self.cut(way, index)
        return pltpu.make_async_remote_copy(
            src_ref=self.own.at[cut] if hop == 1 else self.buf.at[self.slot(way, hop - 1), cut],
            dst_ref=self.buf.at[self.slot(way, hop), cut],
            send_sem=self.send,
            recv_sem=self.recv.at[way, hop - 1, index],
            device_id=self.peers[way],
            device_id_type=MESH,
        )

    def start(self):
        for index in range(self.pieces):
            for way in range(2):
                self.copy(way, 1, index).start()

    def advance(self, hop, index):
        for way in range(2):
            self.copy(way, hop, index).wait_recv()
            if hop + 1 < self.half or (hop + 1 == self.half and index < self.pieces // 2):
                self.copy(way, hop + 1, index).start()


def loop(first, end, body):
    def step(k, carry):
        body(k)
        return carry

    lax.fori_loop(first, end, step, 0)


def kernel(
    nx, ny, nz,
    act, weight, down, up, home, served, var, out,
    abuf, wmine, wother, ybuf, ubuf, sel, xsend, xrelay, xrecv, usend, urecv, uother,
    acc, sums, sums_in, whole, parts, parts_in, shrunk, swap_in, table, homes, lists, var_row, var_wide,
    chooser, opener,
    permuted, early, local_sem, z_recv, y_recv, u_recv, relay_recv, sent, got, pair_send, pair_recv,
):
    grp, tp = lax.axis_index("grp"), lax.axis_index("tp")
    x, y = grp // ny, lax.rem(grp, ny)
    z, core = tp // 2, lax.rem(tp, 2)
    tokens = out.shape[0]
    cols = out.shape[1]
    groups = nx * ny
    far = 1 - 2 * core

    def at_x(step):
        return (lax.rem(x + step + nx, nx) * ny + y, tp)

    def at_y(step):
        return (x * ny + lax.rem(y + step + ny, ny), tp)

    def at_z(step):
        return (grp, lax.rem(z + step + nz, nz) * 2 + core)

    other = (grp, z * 2 + 1 - core)

    barrier = pltpu.get_barrier_semaphore()

    def greet(partner):
        pl.semaphore_signal(barrier, inc=1, device_id=partner, device_id_type=MESH)

    greet(other)
    greet(at_y(1))
    greet(at_y(-1))
    loop(1, nx, lambda e: greet(at_x(e)))
    loop(1, nz, lambda e: greet(at_z(e)))

    local = [
        pltpu.make_async_copy(home, homes, local_sem.at[4]),
        pltpu.make_async_copy(served, lists, local_sem.at[5]),
        pltpu.make_async_copy(down, ybuf.at[0], local_sem.at[1]),
        pltpu.make_async_copy(act, abuf.at[0], local_sem.at[0]),
        pltpu.make_async_copy(up, ubuf.at[0], local_sem.at[2]),
        pltpu.make_async_copy(var, var_row, local_sem.at[6]),
        pltpu.make_async_copy(weight.at[:, core], wmine, local_sem.at[3]),
    ]
    for copy in local:
        copy.start()

    up_rows = up.shape[0] * up.shape[1]
    rank = xrecv.shape[-1]
    depth = act.shape[1]
    share = tokens // nz

    def set_up_choice():
        shape = chooser.shape
        line = lax.broadcasted_iota(jnp.int32, shape, 0)

        def pick(k, rows):
            return jnp.where((line >> 2) == k, table[k], rows)

        rows = lax.fori_loop(0, nx * SLOTS, pick, jnp.zeros(shape, jnp.int32), unroll=4)
        wanted = rows * 4 + (line & 3)
        chooser[...] = (wanted == lax.broadcasted_iota(jnp.int32, shape, 1)).astype(F32).astype(BF16)

    def sources(e):
        width = ny * 16
        place = lax.broadcasted_iota(jnp.int32, (1, width), 1) >> 4
        behind_y = jnp.where((place & 1) == 1, (place + 1) >> 1, ny - (place >> 1))
        return pl.ds(e * width, width), lax.rem(x + nx - e, nx) * ny + ((y - behind_y) & (ny - 1))

    def set_up():
        width = min(128, depth)
        for at in range(0, depth, width):
            column = lax.broadcasted_iota(jnp.int32, (1, width), 1) + at
            place = column >> 6
            e = (column >> 4) & (nx - 1)
            behind_y = jnp.where((place & 1) == 1, (place + 1) >> 1, ny - (place >> 1))
            from_group = ((x - e) & (nx - 1)) * ny + ((y - behind_y) & (ny - 1))
            row = lax.broadcasted_iota(jnp.int32, (depth, width), 0)
            hit = row == from_group * 16 + (column & 15)
            moved = jnp.dot(abuf[0], hit.astype(F32).astype(BF16), preferred_element_type=F32)
            permuted[:, at:at + width] = moved.astype(BF16)

    def set_up_last():
        for e in range(nx):
            columns, from_group = sources(e)
            width = ny * 16
            row = lax.broadcasted_iota(jnp.int32, (rank, width), 0)
            column = lax.broadcasted_iota(jnp.int32, (rank, width), 1)
            hit = (row == from_group * 4 + (column & 3)) & (((column >> 2) & 1) == core)
            opener[:, columns] = hit.astype(F32).astype(BF16)

    def set_up_tokens():
        local[5].wait()
        for i in range(0, tokens, cols):
            size = min(cols, tokens - i)
            row = jnp.broadcast_to(var_row[:, pl.ds(i, size)], (cols, size))
            var_wide[pl.ds(i, size), :] = row.T

    pl.semaphore_wait(barrier, nx + nz + 1)

    zring = Ring(act, abuf, 4, (at_z(1), at_z(-1)), sent.at[0], z_recv)
    yring = Ring(down, ybuf, 4, (at_y(1), at_y(-1)), sent.at[1], y_recv)
    uring = Ring(up, ubuf, 2, (at_y(1), at_y(-1)), sent.at[6], u_recv)

    def pair(index, src, dst):
        return pltpu.make_async_remote_copy(
            src_ref=src, dst_ref=dst, send_sem=pair_send.at[index], recv_sem=pair_recv.at[index],
            device_id=other, device_id_type=MESH,
        )

    yring.start()
    zring.start()
    local[0].wait()
    local[1].wait()

    def fill(k, carry):
        owner = lax.rem(x + k // SLOTS, nx) * ny + y
        j = lax.rem(k, SLOTS)
        table[k] = homes[lists[j // PIECES, owner] * PIECES + lax.rem(j, PIECES)]
        return carry

    lax.fori_loop(0, nx * SLOTS, fill, 0)
    weights = pair(0, weight.at[:, 1 - core], wother)

    def behind(d):
        return lax.rem(y - d + ny, ny)

    def remote(src, dst, send, recv, peer):
        return pltpu.make_async_remote_copy(
            src_ref=src, dst_ref=dst, send_sem=send, recv_sem=recv, device_id=peer, device_id_type=MESH
        )

    def all_sent(kind, ref):
        remote(ref, ref, sent.at[kind], got.at[0], other).wait_send()

    def all_got(kind, ref):
        remote(ref, ref, sent.at[0], got.at[kind], other).wait_recv()

    groups_of_places = [(0, 1)] + [(2 * k - 1, 2) for k in range(1, ny // 2)] + [(ny - 1, 1)]

    def chunk(place):
        return (place + 1) // 2 if place % 2 else (ny - place // 2) % ny

    def turn(number):
        return 1 if number < len(groups_of_places) - 2 else 4

    def hand(e, number):
        places = pl.ds(*groups_of_places[number])
        if e == 2 and number != len(groups_of_places) - 1:
            return remote(xsend.at[2, places], xrelay.at[places], sent.at[2], relay_recv.at[number], at_x(far))
        return remote(xsend.at[e, places], xrecv.at[places, e], sent.at[2], got.at[turn(number)], at_x(e))

    def choose(number):
        first, count = groups_of_places[number]
        chunks = [chunk(first + k) for k in range(count)]
        for k in range(count):
            sel[k] = ybuf[chunks[k]]
        for e in (2, 1, 3, 0):

            def take(j):
                slot = table[e * SLOTS + j]
                for k in range(count):
                    if e == 0:
                        xrecv[first + k, 0, j] = sel[k, slot]
                    else:
                        xsend[e, first + k, j] = sel[k, slot]

            for j in range(SLOTS):
                take(j)
            if e:
                hand(e, number).start()

    def choose_up():
        ups = [ubuf[chunk(place)].reshape(up_rows, cols) for place in range(ny)]
        chosen = jnp.dot(chooser[...], jnp.concatenate(ups, axis=1), preferred_element_type=F32).astype(BF16)
        for place in range(ny):
            rows = chosen[:, place * cols:(place + 1) * cols].reshape(nx, 2, 16, cols)
            for e in range(nx):
                usend[e, place] = rows[e]

    def hand_up(e):
        return remote(usend.at[e], urecv.at[e], sent.at[7], got.at[0], at_x(e))

    def relay(number):
        if number != len(groups_of_places) - 1:
            hand(2, number).wait_recv()
            places = pl.ds(*groups_of_places[number])
            remote(xrelay.at[places], xrecv.at[places, 2], sent.at[3], got.at[turn(number)], at_x(far)).start()

    def multiply(slot):
        place = lax.rem(z - slot + nz, nz)
        both = jnp.concatenate([wmine[place], wother[place]], axis=1)
        return jnp.dot(abuf[slot], both, preferred_element_type=F32)

    def multiply_pair(hop):
        z_step(max(0, len(waiting) - sum(event[0] > hop for event in z_events)))

        def add(k):
            acc[...] += multiply(hop + k * (nz - 2 * hop))

        loop(0, 2, add)

    z_events, y_events = (list(ring.events()) for ring in (zring, yring))
    local[2].wait()
    choose(0)
    set_up_choice()
    local[3].wait()
    set_up()

    def u_step(hop):
        for event in uring.events():
            if event[0] == hop and hop > 0:
                uring.advance(*event)

    waiting = list(z_events)

    def z_step(count):
        for event in waiting[:count]:
            zring.advance(*event)
        del waiting[:count]

    for number, (hop, index) in enumerate(y_events):
        yring.advance(hop, index)
        if number + 1 == len(y_events) or y_events[number + 1][0] > hop:
            choose(hop)
            relay(hop - 1)
            z_step(1)
            if hop == 1:
                weights.start()
            if hop == min(2, yring.half):
                uring.start()
            u_step(hop - 2)
        elif index == 1:
            z_step(1)
    z_step(2)
    set_up_tokens()

    cut = groups_of_places[-2][0] if ny > 2 else 0
    who = jnp.concatenate([var_wide[:, pl.ds(0, rank)]] * PIECES, axis=1)

    def shrink(first, end):
        mine = permuted[:, first * nx * 16:end * nx * 16]
        total = jnp.zeros((tokens, PIECES * rank), F32)
        for v in range(VPG):
            slots = [xrecv[first:end, :, v * PIECES + p].reshape(-1, rank) for p in range(PIECES)]
            product = jnp.dot(mine, jnp.concatenate(slots, axis=1), preferred_element_type=F32)
            total = jnp.where(who == v, product, total)
        return total

    if cut:
        all_got(1, xrecv.at[pl.ds(0, cut), pl.ds(1, nx - 1)])
        early[...] = shrink(0, cut)
    z_step(1)
    all_got(4, xrecv.at[pl.ds(cut, ny - cut), pl.ds(1, nx - 1)])
    total = shrink(cut, ny)
    if cut:
        total += early[...]
    for p in range(PIECES):
        sums[p] = total[:, p * rank:(p + 1) * rank]
    first = pair(1, sums.at[1 - core], sums_in)
    first.start()
    if uring.half > 1:
        u_step(uring.half - 1)
    first.wait_recv()
    total = sums[core] + sums_in[...]
    whole[...] = total.reshape(nz, share, rank)
    parts[...] = total.astype(BF16).reshape(nz, share, rank)

    def scatter(e):
        return remote(parts.at[lax.rem(z + e, nz)], parts_in.at[e - 1], sent.at[4], got.at[2], at_z(e))

    def spread(e):
        return remote(shrunk.at[z], shrunk.at[z], sent.at[5], got.at[3], at_z(e))

    loop(1, nz, lambda e: scatter(e).start())
    z_step(1)
    u_step(uring.half)
    local[4].wait()
    choose_up()
    loop(1, nx, lambda e: hand_up(e).start())
    urecv[0] = usend[0]
    set_up_last()
    all_got(2, parts_in)
    shrunk[z] = (whole[z] + jnp.sum(parts_in[...].astype(F32), axis=0)).astype(BF16)
    loop(1, nz, lambda e: spread(e).start())
    z_step(1)
    local[6].wait()
    weights.wait_recv()
    acc[...] = multiply(0)
    multiply_pair(1)
    all_got(0, urecv.at[pl.ds(1, nx - 1)])
    ups = pair(2, urecv, uother)
    ups.start()
    for hop in range(2, min(3, nz // 2)):
        multiply_pair(hop)
    ups.wait_recv()

    all_got(3, shrunk.at[pl.ds(0, nz - 1)])
    wide = groups * 16
    opened = jnp.dot(shrunk[...].reshape(tokens, rank), opener[...], preferred_element_type=F32)
    who = jnp.concatenate([var_wide[:, pl.ds(0, min(cols, wide))]] * max(wide // cols, 1), axis=1)
    which = (lax.broadcasted_iota(jnp.int32, (1, wide), 1) >> 3) & 1
    for h in range(2):
        part = jnp.where(who == which + 2 * h, opened, 0.0).astype(BF16)
        both = jnp.concatenate([side[:, :, h].reshape(wide, cols) for side in (urecv, uother)], axis=1)
        acc[...] += jnp.dot(part, both, preferred_element_type=F32)

    for hop in range(3, nz // 2):
        multiply_pair(hop)
    all_sent(1, ybuf.at[pl.ds(0, ny - 1)])
    all_sent(2, xsend.at[pl.ds(1, nx - 1)])
    all_sent(3, xrelay)
    all_sent(4, parts_in)
    all_sent(5, shrunk.at[pl.ds(0, nz - 1)])
    all_sent(6, ubuf.at[pl.ds(0, ny - 1)])
    all_sent(7, usend.at[pl.ds(1, nx - 1)])
    weights.wait_send()
    first.wait_send()
    ups.wait_send()
    z_step(len(waiting))
    acc[...] += multiply(nz // 2)
    last = pair(3, acc.at[:, pl.ds(cols, cols)], swap_in)
    last.start()
    all_sent(0, abuf.at[pl.ds(0, nz - 1)])
    last.wait_recv()
    out[...] = (acc[:, pl.ds(0, cols)] + swap_in[...]).astype(BF16)
    last.wait_send()


def on_device(nx, ny, nz, act, weight, down, up, home, served, var):
    tokens, depth = act.shape
    cols = weight.shape[1]
    blocks, rank = down.shape[0], down.shape[2]
    groups = nx * ny
    served, var = served.T, var.T
    up = up.reshape(blocks * 4 // 16, 16, cols)
    weight = weight.reshape(nz, 2, depth, cols)
    hbm = pl.BlockSpec(memory_space=pl.ANY)
    vmem = pl.BlockSpec(memory_space=pltpu.VMEM)
    dma = pltpu.SemaphoreType.DMA
    share = tokens // nz
    scratch = [
        pltpu.VMEM((nz, tokens, depth), BF16),
        pltpu.VMEM((nz, depth, cols), BF16),
        pltpu.VMEM((nz, depth, cols), BF16),
        pltpu.VMEM((ny,) + down.shape, BF16),
        pltpu.VMEM((ny,) + up.shape, BF16),
        pltpu.VMEM((2,) + down.shape, BF16),
        pltpu.VMEM((nx, ny, SLOTS, 16, rank), BF16),
        pltpu.VMEM((ny - 1, SLOTS, 16, rank), BF16),
        pltpu.VMEM((ny, nx, SLOTS, 16, rank), BF16),
        pltpu.VMEM((nx, ny, 2, 16, cols), BF16),
        pltpu.VMEM((nx, ny, 2, 16, cols), BF16),
        pltpu.VMEM((nx, ny, 2, 16, cols), BF16),
        pltpu.VMEM((tokens, 2 * cols), F32),
        pltpu.VMEM((PIECES, tokens, rank), F32),
        pltpu.VMEM((tokens, rank), F32),
        pltpu.VMEM((nz, share, rank), F32),
        pltpu.VMEM((nz, share, rank), BF16),
        pltpu.VMEM((nz - 1, share, rank), BF16),
        pltpu.VMEM((nz, share, rank), BF16),
        pltpu.VMEM((tokens, cols), F32),
        pltpu.SMEM((nx * SLOTS,), jnp.int32),
        pltpu.SMEM(home.shape, jnp.int32),
        pltpu.SMEM(served.shape, jnp.int32),
        pltpu.VMEM(var.shape, jnp.int32),
        pltpu.VMEM((tokens, cols), jnp.int32),
        pltpu.VMEM((nx * SLOTS * 4, blocks * 4), BF16),
        pltpu.VMEM((rank, groups * 16), BF16),
        pltpu.VMEM((tokens, depth), BF16),
        pltpu.VMEM((tokens, PIECES * rank), F32),
        dma((7,)),
        dma((2, nz // 2, 4)), dma((2, ny // 2, 4)), dma((2, ny // 2, 2)), dma((ny // 2,)),
        dma((8,)), dma((5,)), dma((4,)), dma((4,)),
    ]
    return pl.pallas_call(
        functools.partial(kernel, nx, ny, nz),
        out_shape=jax.ShapeDtypeStruct((tokens, cols), BF16),
        in_specs=[hbm] * 7,
        out_specs=vmem,
        scratch_shapes=scratch,
        compiler_params=pltpu.CompilerParams(
            collective_id=0, has_side_effects=True, vmem_limit_bytes=56 * 1024 * 1024
        ),
    )(act, weight, down, up, home, served, var)


def solution(mesh):
    nx = 4
    ny, nz = mesh.shape["grp"] // nx, mesh.shape["tp"] // 2
    in_specs = (
        P("grp", "tp"),
        P(None, "tp"),
        P(None, ("tp", "grp"), None),
        P(None, "grp", "tp"),
        P(),
        P(),
        P("grp", None),
    )
    return jax.shard_map(
        functools.partial(on_device, nx, ny, nz),
        mesh=mesh, in_specs=in_specs, out_specs=P("grp", "tp"), check_vma=False,
    )
```

```python
import functools

import jax
import jax.numpy as jnp
from jax import lax
from jax.experimental import pallas as pl
from jax.experimental.pallas import tpu as pltpu
from jax.sharding import PartitionSpec as P

PIECES = 2
VPG = 4
SLOTS = PIECES * VPG
MESH = pl.DeviceIdType.MESH
F32 = jnp.float32
BF16 = jnp.bfloat16


class Ring:
    def __init__(self, own, buf, pieces, peers, send, recv):
        self.own, self.buf, self.pieces, self.peers = own, buf, pieces, peers
        self.send, self.recv = send, recv
        self.n = buf.shape[0]
        self.half = self.n // 2
        self.size = buf.shape[1] // pieces

    def events(self):
        for hop in range(1, self.half):
            for index in range(self.pieces):
                yield hop, index
        for index in range(self.pieces // 2):
            yield self.half, index

    def cut(self, way, index):
        piece = index if way == 0 else self.pieces - 1 - index
        return pl.ds(piece * self.size, self.size)

    def slot(self, way, hop):
        return hop % self.n if way == 0 else (self.n - hop) % self.n

    def copy(self, way, hop, index):
        cut = self.cut(way, index)
        return pltpu.make_async_remote_copy(
            src_ref=self.own.at[cut] if hop == 1 else self.buf.at[self.slot(way, hop - 1), cut],
            dst_ref=self.buf.at[self.slot(way, hop), cut],
            send_sem=self.send,
            recv_sem=self.recv.at[way, hop - 1, index],
            device_id=self.peers[way],
            device_id_type=MESH,
        )

    def start(self):
        for index in range(self.pieces):
            for way in range(2):
                self.copy(way, 1, index).start()

    def advance(self, hop, index):
        for way in range(2):
            self.copy(way, hop, index).wait_recv()
            if hop + 1 < self.half or (hop + 1 == self.half and index < self.pieces // 2):
                self.copy(way, hop + 1, index).start()


def loop(first, end, body):
    def step(k, carry):
        body(k)
        return carry

    lax.fori_loop(first, end, step, 0)


def kernel(
    nx, ny, nz,
    act, weight, down, up, home, served, var, out,
    abuf, wmine, wother, ybuf, ubuf, sel, xsend, xrelay, xrecv, usend, urecv, uother,
    acc, sums, sums_in, whole, parts, parts_in, shrunk, swap_in, table, homes, lists, var_row, var_wide,
    chooser, opener,
    permuted, early, local_sem, z_recv, y_recv, u_recv, relay_recv, sent, got, pair_send, pair_recv,
):
    grp, tp = lax.axis_index("grp"), lax.axis_index("tp")
    x, y = grp // ny, lax.rem(grp, ny)
    z, core = tp // 2, lax.rem(tp, 2)
    tokens = out.shape[0]
    cols = out.shape[1]
    groups = nx * ny
    far = 1 - 2 * core

    def at_x(step):
        return (lax.rem(x + step + nx, nx) * ny + y, tp)

    def at_y(step):
        return (x * ny + lax.rem(y + step + ny, ny), tp)

    def at_z(step):
        return (grp, lax.rem(z + step + nz, nz) * 2 + core)

    other = (grp, z * 2 + 1 - core)

    barrier = pltpu.get_barrier_semaphore()

    def greet(partner):
        pl.semaphore_signal(barrier, inc=1, device_id=partner, device_id_type=MESH)

    greet(other)
    greet(at_y(1))
    greet(at_y(-1))
    loop(1, nx, lambda e: greet(at_x(e)))
    loop(1, nz, lambda e: greet(at_z(e)))

    local = [
        pltpu.make_async_copy(home, homes, local_sem.at[4]),
        pltpu.make_async_copy(served, lists, local_sem.at[5]),
        pltpu.make_async_copy(down, ybuf.at[0], local_sem.at[1]),
        pltpu.make_async_copy(act, abuf.at[0], local_sem.at[0]),
        pltpu.make_async_copy(up, ubuf.at[0], local_sem.at[2]),
        pltpu.make_async_copy(var, var_row, local_sem.at[6]),
        pltpu.make_async_copy(weight.at[:, core], wmine, local_sem.at[3]),
    ]
    for copy in local[:-1]:
        copy.start()

    up_rows = up.shape[0] * up.shape[1]
    rank = xrecv.shape[-1]
    depth = act.shape[1]
    share = tokens // nz

    def set_up_choice():
        shape = chooser.shape
        line = lax.broadcasted_iota(jnp.int32, shape, 0)

        def pick(k, rows):
            return jnp.where((line >> 2) == k, table[k], rows)

        rows = lax.fori_loop(0, nx * SLOTS, pick, jnp.zeros(shape, jnp.int32), unroll=4)
        wanted = rows * 4 + (line & 3)
        chooser[...] = (wanted == lax.broadcasted_iota(jnp.int32, shape, 1)).astype(F32).astype(BF16)

    def sources(e):
        width = ny * 16
        place = lax.broadcasted_iota(jnp.int32, (1, width), 1) >> 4
        behind_y = jnp.where((place & 1) == 1, (place + 1) >> 1, ny - (place >> 1))
        return pl.ds(e * width, width), lax.rem(x + nx - e, nx) * ny + ((y - behind_y) & (ny - 1))

    def set_up():
        width = min(128, depth)
        for at in range(0, depth, width):
            column = lax.broadcasted_iota(jnp.int32, (1, width), 1) + at
            place = column >> 6
            e = (column >> 4) & (nx - 1)
            behind_y = jnp.where((place & 1) == 1, (place + 1) >> 1, ny - (place >> 1))
            from_group = ((x - e) & (nx - 1)) * ny + ((y - behind_y) & (ny - 1))
            row = lax.broadcasted_iota(jnp.int32, (depth, width), 0)
            hit = row == from_group * 16 + (column & 15)
            moved = jnp.dot(abuf[0], hit.astype(F32).astype(BF16), preferred_element_type=F32)
            permuted[:, at:at + width] = moved.astype(BF16)

    def set_up_last():
        for e in range(nx):
            columns, from_group = sources(e)
            width = ny * 16
            row = lax.broadcasted_iota(jnp.int32, (rank, width), 0)
            column = lax.broadcasted_iota(jnp.int32, (rank, width), 1)
            hit = (row == from_group * 4 + (column & 3)) & (((column >> 2) & 1) == core)
            opener[:, columns] = hit.astype(F32).astype(BF16)

    def set_up_tokens():
        local[5].wait()
        for i in range(0, tokens, cols):
            size = min(cols, tokens - i)
            row = jnp.broadcast_to(var_row[:, pl.ds(i, size)], (cols, size))
            var_wide[pl.ds(i, size), :] = row.T

    pl.semaphore_wait(barrier, nx + nz + 1)

    zring = Ring(act, abuf, 4, (at_z(1), at_z(-1)), sent.at[0], z_recv)
    yring = Ring(down, ybuf, 4, (at_y(1), at_y(-1)), sent.at[1], y_recv)
    uring = Ring(up, ubuf, 2, (at_y(1), at_y(-1)), sent.at[6], u_recv)

    def pair(index, src, dst):
        return pltpu.make_async_remote_copy(
            src_ref=src, dst_ref=dst, send_sem=pair_send.at[index], recv_sem=pair_recv.at[index],
            device_id=other, device_id_type=MESH,
        )

    yring.start()
    zring.start()
    local[0].wait()
    local[1].wait()

    def fill(k, carry):
        owner = lax.rem(x + k // SLOTS, nx) * ny + y
        j = lax.rem(k, SLOTS)
        table[k] = homes[lists[j // PIECES, owner] * PIECES + lax.rem(j, PIECES)]
        return carry

    lax.fori_loop(0, nx * SLOTS, fill, 0)
    weights = pair(0, weight.at[:, 1 - core], wother)

    def behind(d):
        return lax.rem(y - d + ny, ny)

    def remote(src, dst, send, recv, peer):
        return pltpu.make_async_remote_copy(
            src_ref=src, dst_ref=dst, send_sem=send, recv_sem=recv, device_id=peer, device_id_type=MESH
        )

    def all_sent(kind, ref):
        remote(ref, ref, sent.at[kind], got.at[0], other).wait_send()

    def all_got(kind, ref):
        remote(ref, ref, sent.at[0], got.at[kind], other).wait_recv()

    groups_of_places = [(0, 1)] + [(2 * k - 1, 2) for k in range(1, ny // 2)] + [(ny - 1, 1)]

    def chunk(place):
        return (place + 1) // 2 if place % 2 else (ny - place // 2) % ny

    def turn(number):
        return 1 if number < len(groups_of_places) - 2 else 4

    def hand(e, number):
        places = pl.ds(*groups_of_places[number])
        if e == 2 and number != len(groups_of_places) - 1:
            return remote(xsend.at[2, places], xrelay.at[places], sent.at[2], relay_recv.at[number], at_x(far))
        return remote(xsend.at[e, places], xrecv.at[places, e], sent.at[2], got.at[turn(number)], at_x(e))

    def choose(number):
        first, count = groups_of_places[number]
        chunks = [chunk(first + k) for k in range(count)]
        for k in range(count):
            sel[k] = ybuf[chunks[k]]
        for e in (2, 1, 3, 0):

            def take(j):
                slot = table[e * SLOTS + j]
                for k in range(count):
                    if e == 0:
                        xrecv[first + k, 0, j] = sel[k, slot]
                    else:
                        xsend[e, first + k, j] = sel[k, slot]

            for j in range(SLOTS):
                take(j)
            if e:
                hand(e, number).start()

    def choose_up():
        ups = [ubuf[chunk(place)].reshape(up_rows, cols) for place in range(ny)]
        chosen = jnp.dot(chooser[...], jnp.concatenate(ups, axis=1), preferred_element_type=F32).astype(BF16)
        for place in range(ny):
            rows = chosen[:, place * cols:(place + 1) * cols].reshape(nx, 2, 16, cols)
            for e in range(nx):
                usend[e, place] = rows[e]

    def hand_up(e):
        return remote(usend.at[e], urecv.at[e], sent.at[7], got.at[0], at_x(e))

    def relay(number):
        if number != len(groups_of_places) - 1:
            hand(2, number).wait_recv()
            places = pl.ds(*groups_of_places[number])
            remote(xrelay.at[places], xrecv.at[places, 2], sent.at[3], got.at[turn(number)], at_x(far)).start()

    def multiply(slot):
        place = lax.rem(z - slot + nz, nz)
        both = jnp.concatenate([wmine[place], wother[place]], axis=1)
        return jnp.dot(abuf[slot], both, preferred_element_type=F32)

    def multiply_pair(hop):
        z_step(max(0, len(waiting) - sum(event[0] > hop for event in z_events)))

        def add(k):
            acc[...] += multiply(hop + k * (nz - 2 * hop))

        loop(0, 2, add)

    z_events, y_events = (list(ring.events()) for ring in (zring, yring))
    local[2].wait()
    choose(0)
    set_up_choice()
    local[3].wait()
    set_up()

    def u_step(hop):
        for event in uring.events():
            if event[0] == hop and hop > 0:
                uring.advance(*event)

    waiting = list(z_events)

    def z_step(count):
        for event in waiting[:count]:
            zring.advance(*event)
        del waiting[:count]

    for number, (hop, index) in enumerate(y_events):
        yring.advance(hop, index)
        if number + 1 == len(y_events) or y_events[number + 1][0] > hop:
            choose(hop)
            relay(hop - 1)
            z_step(1)
            if hop == min(2, yring.half):
                uring.start()
            u_step(hop - 2)
        elif index == 1:
            z_step(1)
    weights.start()
    local[6].start()
    z_step(2)
    set_up_tokens()

    cut = groups_of_places[-2][0] if ny > 2 else 0
    who = jnp.concatenate([var_wide[:, pl.ds(0, rank)]] * PIECES, axis=1)

    def shrink(first, end):
        mine = permuted[:, first * nx * 16:end * nx * 16]
        total = jnp.zeros((tokens, PIECES * rank), F32)
        for v in range(VPG):
            slots = [xrecv[first:end, :, v * PIECES + p].reshape(-1, rank) for p in range(PIECES)]
            product = jnp.dot(mine, jnp.concatenate(slots, axis=1), preferred_element_type=F32)
            total = jnp.where(who == v, product, total)
        return total

    if cut:
        all_got(1, xrecv.at[pl.ds(0, cut), pl.ds(1, nx - 1)])
        early[...] = shrink(0, cut)
    z_step(1)
    all_got(4, xrecv.at[pl.ds(cut, ny - cut), pl.ds(1, nx - 1)])
    total = shrink(cut, ny)
    if cut:
        total += early[...]
    for p in range(PIECES):
        sums[p] = total[:, p * rank:(p + 1) * rank]
    first = pair(1, sums.at[1 - core], sums_in)
    first.start()
    if uring.half > 1:
        u_step(uring.half - 1)
    first.wait_recv()
    total = sums[core] + sums_in[...]
    whole[...] = total.reshape(nz, share, rank)
    parts[...] = total.astype(BF16).reshape(nz, share, rank)

    def scatter(e):
        return remote(parts.at[lax.rem(z + e, nz)], parts_in.at[e - 1], sent.at[4], got.at[2], at_z(e))

    def spread(e):
        return remote(shrunk.at[z], shrunk.at[z], sent.at[5], got.at[3], at_z(e))

    loop(1, nz, lambda e: scatter(e).start())
    z_step(1)
    u_step(uring.half)
    local[4].wait()
    choose_up()
    loop(1, nx, lambda e: hand_up(e).start())
    urecv[0] = usend[0]
    set_up_last()
    all_got(2, parts_in)
    shrunk[z] = (whole[z] + jnp.sum(parts_in[...].astype(F32), axis=0)).astype(BF16)
    loop(1, nz, lambda e: spread(e).start())
    z_step(1)
    local[6].wait()
    weights.wait_recv()
    acc[...] = multiply(0)
    multiply_pair(1)
    all_got(0, urecv.at[pl.ds(1, nx - 1)])
    ups = pair(2, urecv, uother)
    ups.start()
    for hop in range(2, min(3, nz // 2)):
        multiply_pair(hop)
    ups.wait_recv()

    all_got(3, shrunk.at[pl.ds(0, nz - 1)])
    wide = groups * 16
    opened = jnp.dot(shrunk[...].reshape(tokens, rank), opener[...], preferred_element_type=F32)
    who = jnp.concatenate([var_wide[:, pl.ds(0, min(cols, wide))]] * max(wide // cols, 1), axis=1)
    which = (lax.broadcasted_iota(jnp.int32, (1, wide), 1) >> 3) & 1
    for h in range(2):
        part = jnp.where(who == which + 2 * h, opened, 0.0).astype(BF16)
        both = jnp.concatenate([side[:, :, h].reshape(wide, cols) for side in (urecv, uother)], axis=1)
        acc[...] += jnp.dot(part, both, preferred_element_type=F32)

    for hop in range(3, nz // 2):
        multiply_pair(hop)
    all_sent(1, ybuf.at[pl.ds(0, ny - 1)])
    all_sent(2, xsend.at[pl.ds(1, nx - 1)])
    all_sent(3, xrelay)
    all_sent(4, parts_in)
    all_sent(5, shrunk.at[pl.ds(0, nz - 1)])
    all_sent(6, ubuf.at[pl.ds(0, ny - 1)])
    all_sent(7, usend.at[pl.ds(1, nx - 1)])
    weights.wait_send()
    first.wait_send()
    ups.wait_send()
    z_step(len(waiting))
    acc[...] += multiply(nz // 2)
    last = pair(3, acc.at[:, pl.ds(cols, cols)], swap_in)
    last.start()
    all_sent(0, abuf.at[pl.ds(0, nz - 1)])
    last.wait_recv()
    out[...] = (acc[:, pl.ds(0, cols)] + swap_in[...]).astype(BF16)
    last.wait_send()


def on_device(nx, ny, nz, act, weight, down, up, home, served, var):
    tokens, depth = act.shape
    cols = weight.shape[1]
    blocks, rank = down.shape[0], down.shape[2]
    groups = nx * ny
    served, var = served.T, var.T
    up = up.reshape(blocks * 4 // 16, 16, cols)
    weight = weight.reshape(nz, 2, depth, cols)
    hbm = pl.BlockSpec(memory_space=pl.ANY)
    vmem = pl.BlockSpec(memory_space=pltpu.VMEM)
    dma = pltpu.SemaphoreType.DMA
    share = tokens // nz
    scratch = [
        pltpu.VMEM((nz, tokens, depth), BF16),
        pltpu.VMEM((nz, depth, cols), BF16),
        pltpu.VMEM((nz, depth, cols), BF16),
        pltpu.VMEM((ny,) + down.shape, BF16),
        pltpu.VMEM((ny,) + up.shape, BF16),
        pltpu.VMEM((2,) + down.shape, BF16),
        pltpu.VMEM((nx, ny, SLOTS, 16, rank), BF16),
        pltpu.VMEM((ny - 1, SLOTS, 16, rank), BF16),
        pltpu.VMEM((ny, nx, SLOTS, 16, rank), BF16),
        pltpu.VMEM((nx, ny, 2, 16, cols), BF16),
        pltpu.VMEM((nx, ny, 2, 16, cols), BF16),
        pltpu.VMEM((nx, ny, 2, 16, cols), BF16),
        pltpu.VMEM((tokens, 2 * cols), F32),
        pltpu.VMEM((PIECES, tokens, rank), F32),
        pltpu.VMEM((tokens, rank), F32),
        pltpu.VMEM((nz, share, rank), F32),
        pltpu.VMEM((nz, share, rank), BF16),
        pltpu.VMEM((nz - 1, share, rank), BF16),
        pltpu.VMEM((nz, share, rank), BF16),
        pltpu.VMEM((tokens, cols), F32),
        pltpu.SMEM((nx * SLOTS,), jnp.int32),
        pltpu.SMEM(home.shape, jnp.int32),
        pltpu.SMEM(served.shape, jnp.int32),
        pltpu.VMEM(var.shape, jnp.int32),
        pltpu.VMEM((tokens, cols), jnp.int32),
        pltpu.VMEM((nx * SLOTS * 4, blocks * 4), BF16),
        pltpu.VMEM((rank, groups * 16), BF16),
        pltpu.VMEM((tokens, depth), BF16),
        pltpu.VMEM((tokens, PIECES * rank), F32),
        dma((7,)),
        dma((2, nz // 2, 4)), dma((2, ny // 2, 4)), dma((2, ny // 2, 2)), dma((ny // 2,)),
        dma((8,)), dma((5,)), dma((4,)), dma((4,)),
    ]
    return pl.pallas_call(
        functools.partial(kernel, nx, ny, nz),
        out_shape=jax.ShapeDtypeStruct((tokens, cols), BF16),
        in_specs=[hbm] * 7,
        out_specs=vmem,
        scratch_shapes=scratch,
        compiler_params=pltpu.CompilerParams(
            collective_id=0, has_side_effects=True, vmem_limit_bytes=56 * 1024 * 1024
        ),
    )(act, weight, down, up, home, served, var)


def solution(mesh):
    nx = 4
    ny, nz = mesh.shape["grp"] // nx, mesh.shape["tp"] // 2
    in_specs = (
        P("grp", "tp"),
        P(None, "tp"),
        P(None, ("tp", "grp"), None),
        P(None, "grp", "tp"),
        P(),
        P(),
        P("grp", None),
    )
    return jax.shard_map(
        functools.partial(on_device, nx, ny, nz),
        mesh=mesh, in_specs=in_specs, out_specs=P("grp", "tp"), check_vma=False,
    )
```

```python
import functools

import jax
import jax.numpy as jnp
from jax import lax
from jax.experimental import pallas as pl
from jax.experimental.pallas import tpu as pltpu
from jax.sharding import PartitionSpec as P

PIECES = 2
VPG = 4
SLOTS = PIECES * VPG
MESH = pl.DeviceIdType.MESH
F32 = jnp.float32
BF16 = jnp.bfloat16


class Ring:
    def __init__(self, own, buf, pieces, peers, send, recv):
        self.own, self.buf, self.pieces, self.peers = own, buf, pieces, peers
        self.send, self.recv = send, recv
        self.n = buf.shape[0]
        self.half = self.n // 2
        self.size = buf.shape[1] // pieces

    def events(self):
        for hop in range(1, self.half):
            for index in range(self.pieces):
                yield hop, index
        for index in range(self.pieces // 2):
            yield self.half, index

    def cut(self, way, index):
        piece = index if way == 0 else self.pieces - 1 - index
        return pl.ds(piece * self.size, self.size)

    def slot(self, way, hop):
        return hop % self.n if way == 0 else (self.n - hop) % self.n

    def copy(self, way, hop, index):
        cut = self.cut(way, index)
        return pltpu.make_async_remote_copy(
            src_ref=self.own.at[cut] if hop == 1 else self.buf.at[self.slot(way, hop - 1), cut],
            dst_ref=self.buf.at[self.slot(way, hop), cut],
            send_sem=self.send,
            recv_sem=self.recv.at[way, hop - 1, index],
            device_id=self.peers[way],
            device_id_type=MESH,
        )

    def start(self):
        for index in range(self.pieces):
            for way in range(2):
                self.copy(way, 1, index).start()

    def advance(self, hop, index):
        for way in range(2):
            self.copy(way, hop, index).wait_recv()
            if hop + 1 < self.half or (hop + 1 == self.half and index < self.pieces // 2):
                self.copy(way, hop + 1, index).start()


def loop(first, end, body):
    def step(k, carry):
        body(k)
        return carry

    lax.fori_loop(first, end, step, 0)


def kernel(
    nx, ny, nz,
    act, weight, down, up, home, served, var, out,
    abuf, wmine, wother, ybuf, ubuf, sel, xsend, xrelay, xrecv, usend, urecv, uother,
    acc, sums, sums_in, whole, parts, parts_in, shrunk, swap_in, table, homes, lists, var_row, var_wide,
    chooser, opener,
    permuted, early, local_sem, z_recv, y_recv, u_recv, relay_recv, sent, got, pair_send, pair_recv,
):
    grp, tp = lax.axis_index("grp"), lax.axis_index("tp")
    x, y = grp // ny, lax.rem(grp, ny)
    z, core = tp // 2, lax.rem(tp, 2)
    tokens = out.shape[0]
    cols = out.shape[1]
    groups = nx * ny
    far = 1 - 2 * core

    def at_x(step):
        return (lax.rem(x + step + nx, nx) * ny + y, tp)

    def at_y(step):
        return (x * ny + lax.rem(y + step + ny, ny), tp)

    def at_z(step):
        return (grp, lax.rem(z + step + nz, nz) * 2 + core)

    other = (grp, z * 2 + 1 - core)

    barrier = pltpu.get_barrier_semaphore()

    def greet(partner):
        pl.semaphore_signal(barrier, inc=1, device_id=partner, device_id_type=MESH)

    greet(other)
    greet(at_y(1))
    greet(at_y(-1))
    loop(1, nx, lambda e: greet(at_x(e)))
    loop(1, nz, lambda e: greet(at_z(e)))

    local = [
        pltpu.make_async_copy(home, homes, local_sem.at[4]),
        pltpu.make_async_copy(served, lists, local_sem.at[5]),
        pltpu.make_async_copy(down, ybuf.at[0], local_sem.at[1]),
        pltpu.make_async_copy(act, abuf.at[0], local_sem.at[0]),
        pltpu.make_async_copy(up, ubuf.at[0], local_sem.at[2]),
        pltpu.make_async_copy(var, var_row, local_sem.at[6]),
        pltpu.make_async_copy(weight.at[:, core], wmine, local_sem.at[3]),
    ]
    for copy in local[:-1]:
        copy.start()

    up_rows = up.shape[0] * up.shape[1]
    rank = xrecv.shape[-1]
    depth = act.shape[1]
    share = tokens // nz

    def set_up_choice():
        shape = chooser.shape
        line = lax.broadcasted_iota(jnp.int32, shape, 0)

        def pick(k, rows):
            return jnp.where((line >> 2) == k, table[k], rows)

        rows = lax.fori_loop(0, nx * SLOTS, pick, jnp.zeros(shape, jnp.int32), unroll=4)
        wanted = rows * 4 + (line & 3)
        chooser[...] = (wanted == lax.broadcasted_iota(jnp.int32, shape, 1)).astype(F32).astype(BF16)

    def sources(e):
        width = ny * 16
        place = lax.broadcasted_iota(jnp.int32, (1, width), 1) >> 4
        behind_y = jnp.where((place & 1) == 1, (place + 1) >> 1, ny - (place >> 1))
        return pl.ds(e * width, width), lax.rem(x + nx - e, nx) * ny + ((y - behind_y) & (ny - 1))

    def set_up():
        width = min(128, depth)
        for at in range(0, depth, width):
            column = lax.broadcasted_iota(jnp.int32, (1, width), 1) + at
            place = column >> 6
            e = (column >> 4) & (nx - 1)
            behind_y = jnp.where((place & 1) == 1, (place + 1) >> 1, ny - (place >> 1))
            from_group = ((x - e) & (nx - 1)) * ny + ((y - behind_y) & (ny - 1))
            row = lax.broadcasted_iota(jnp.int32, (depth, width), 0)
            hit = row == from_group * 16 + (column & 15)
            moved = jnp.dot(abuf[0], hit.astype(F32).astype(BF16), preferred_element_type=F32)
            permuted[:, at:at + width] = moved.astype(BF16)

    def set_up_last():
        for e in range(nx):
            columns, from_group = sources(e)
            width = ny * 16
            row = lax.broadcasted_iota(jnp.int32, (rank, width), 0)
            column = lax.broadcasted_iota(jnp.int32, (rank, width), 1)
            hit = (row == from_group * 4 + (column & 3)) & (((column >> 2) & 1) == core)
            opener[:, columns] = hit.astype(F32).astype(BF16)

    def set_up_tokens():
        local[5].wait()
        for i in range(0, tokens, cols):
            size = min(cols, tokens - i)
            row = jnp.broadcast_to(var_row[:, pl.ds(i, size)], (cols, size))
            var_wide[pl.ds(i, size), :] = row.T

    pl.semaphore_wait(barrier, nx + nz + 1)

    zring = Ring(act, abuf, 4, (at_z(1), at_z(-1)), sent.at[0], z_recv)
    yring = Ring(down, ybuf, 4, (at_y(1), at_y(-1)), sent.at[1], y_recv)
    uring = Ring(up, ubuf, 2, (at_y(1), at_y(-1)), sent.at[6], u_recv)

    def pair(index, src, dst):
        return pltpu.make_async_remote_copy(
            src_ref=src, dst_ref=dst, send_sem=pair_send.at[index], recv_sem=pair_recv.at[index],
            device_id=other, device_id_type=MESH,
        )

    yring.start()
    zring.start()
    local[0].wait()
    local[1].wait()

    def fill(k, carry):
        owner = lax.rem(x + k // SLOTS, nx) * ny + y
        j = lax.rem(k, SLOTS)
        table[k] = homes[lists[j // PIECES, owner] * PIECES + lax.rem(j, PIECES)]
        return carry

    lax.fori_loop(0, nx * SLOTS, fill, 0)
    weights = pair(0, weight.at[:, 1 - core], wother)

    def behind(d):
        return lax.rem(y - d + ny, ny)

    def remote(src, dst, send, recv, peer):
        return pltpu.make_async_remote_copy(
            src_ref=src, dst_ref=dst, send_sem=send, recv_sem=recv, device_id=peer, device_id_type=MESH
        )

    def all_sent(kind, ref):
        remote(ref, ref, sent.at[kind], got.at[0], other).wait_send()

    def all_got(kind, ref):
        remote(ref, ref, sent.at[0], got.at[kind], other).wait_recv()

    groups_of_places = [(0, 1)] + [(2 * k - 1, 2) for k in range(1, ny // 2)] + [(ny - 1, 1)]

    def chunk(place):
        return (place + 1) // 2 if place % 2 else (ny - place // 2) % ny

    def turn(number):
        return 1 if number < len(groups_of_places) - 2 else 4

    def hand(e, number):
        places = pl.ds(*groups_of_places[number])
        if e == 2 and number != len(groups_of_places) - 1:
            return remote(xsend.at[2, places], xrelay.at[places], sent.at[2], relay_recv.at[number], at_x(far))
        return remote(xsend.at[e, places], xrecv.at[places, e], sent.at[2], got.at[turn(number)], at_x(e))

    def choose(number):
        first, count = groups_of_places[number]
        chunks = [chunk(first + k) for k in range(count)]
        for k in range(count):
            sel[k] = ybuf[chunks[k]]
        for e in (2, 1, 3, 0):

            def take(j):
                slot = table[e * SLOTS + j]
                for k in range(count):
                    if e == 0:
                        xrecv[first + k, 0, j] = sel[k, slot]
                    else:
                        xsend[e, first + k, j] = sel[k, slot]

            for j in range(SLOTS):
                take(j)
            if e:
                hand(e, number).start()

    def choose_up():
        ups = [ubuf[chunk(place)].reshape(up_rows, cols) for place in range(ny)]
        chosen = jnp.dot(chooser[...], jnp.concatenate(ups, axis=1), preferred_element_type=F32).astype(BF16)
        for place in range(ny):
            rows = chosen[:, place * cols:(place + 1) * cols].reshape(nx, 2, 16, cols)
            for e in range(nx):
                usend[e, place] = rows[e]

    def hand_up(e):
        return remote(usend.at[e], urecv.at[e], sent.at[7], got.at[0], at_x(e))

    def relay(number):
        if number != len(groups_of_places) - 1:
            hand(2, number).wait_recv()
            places = pl.ds(*groups_of_places[number])
            remote(xrelay.at[places], xrecv.at[places, 2], sent.at[3], got.at[turn(number)], at_x(far)).start()

    def multiply(slot):
        place = lax.rem(z - slot + nz, nz)
        both = jnp.concatenate([wmine[place], wother[place]], axis=1)
        return jnp.dot(abuf[slot], both, preferred_element_type=F32)

    def multiply_pair(hop):
        z_step(max(0, len(waiting) - sum(event[0] > hop for event in z_events)))

        def add(k):
            acc[...] += multiply(hop + k * (nz - 2 * hop))

        loop(0, 2, add)

    z_events, y_events = (list(ring.events()) for ring in (zring, yring))
    local[2].wait()
    choose(0)
    set_up_choice()
    local[3].wait()
    set_up()

    def u_step(hop):
        for event in uring.events():
            if event[0] == hop and hop > 0:
                uring.advance(*event)

    waiting = list(z_events)

    def z_step(count):
        for event in waiting[:count]:
            zring.advance(*event)
        del waiting[:count]

    for number, (hop, index) in enumerate(y_events):
        yring.advance(hop, index)
        if number + 1 == len(y_events) or y_events[number + 1][0] > hop:
            choose(hop)
            relay(hop - 1)
            z_step(1)
            if hop == min(2, yring.half):
                uring.start()
            u_step(hop - 2)
        elif index == 1:
            z_step(1)
    weights.start()
    local[6].start()
    z_step(2)
    set_up_tokens()

    cut = groups_of_places[-2][0] if ny > 2 else 0
    who = jnp.concatenate([var_wide[:, pl.ds(0, rank)]] * PIECES, axis=1)

    def shrink(first, end):
        mine = permuted[:, first * nx * 16:end * nx * 16]
        total = jnp.zeros((tokens, PIECES * rank), F32)
        for v in range(VPG):
            slots = [xrecv[first:end, :, v * PIECES + p].reshape(-1, rank) for p in range(PIECES)]
            product = jnp.dot(mine, jnp.concatenate(slots, axis=1), preferred_element_type=F32)
            total = jnp.where(who == v, product, total)
        return total

    if cut:
        all_got(1, xrecv.at[pl.ds(0, cut), pl.ds(1, nx - 1)])
        early[...] = shrink(0, cut)
    z_step(1)
    u_step(uring.half - 1)
    all_got(4, xrecv.at[pl.ds(cut, ny - cut), pl.ds(1, nx - 1)])
    total = shrink(cut, ny)
    if cut:
        total += early[...]
    for p in range(PIECES):
        sums[p] = total[:, p * rank:(p + 1) * rank]
    first = pair(1, sums.at[1 - core], sums_in)
    first.start()
    u_step(uring.half)
    local[4].wait()
    choose_up()
    loop(1, nx, lambda e: hand_up(e).start())
    urecv[0] = usend[0]
    first.wait_recv()
    total = sums[core] + sums_in[...]
    whole[...] = total.reshape(nz, share, rank)
    parts[...] = total.astype(BF16).reshape(nz, share, rank)

    def scatter(e):
        return remote(parts.at[lax.rem(z + e, nz)], parts_in.at[e - 1], sent.at[4], got.at[2], at_z(e))

    def spread(e):
        return remote(shrunk.at[z], shrunk.at[z], sent.at[5], got.at[3], at_z(e))

    loop(1, nz, lambda e: scatter(e).start())
    z_step(1)
    set_up_last()
    all_got(2, parts_in)
    shrunk[z] = (whole[z] + jnp.sum(parts_in[...].astype(F32), axis=0)).astype(BF16)
    loop(1, nz, lambda e: spread(e).start())
    z_step(1)
    local[6].wait()
    weights.wait_recv()
    acc[...] = multiply(0)
    multiply_pair(1)
    all_got(0, urecv.at[pl.ds(1, nx - 1)])
    ups = pair(2, urecv, uother)
    ups.start()
    for hop in range(2, min(3, nz // 2)):
        multiply_pair(hop)
    ups.wait_recv()

    all_got(3, shrunk.at[pl.ds(0, nz - 1)])
    wide = groups * 16
    opened = jnp.dot(shrunk[...].reshape(tokens, rank), opener[...], preferred_element_type=F32)
    who = jnp.concatenate([var_wide[:, pl.ds(0, min(cols, wide))]] * max(wide // cols, 1), axis=1)
    which = (lax.broadcasted_iota(jnp.int32, (1, wide), 1) >> 3) & 1
    for h in range(2):
        part = jnp.where(who == which + 2 * h, opened, 0.0).astype(BF16)
        both = jnp.concatenate([side[:, :, h].reshape(wide, cols) for side in (urecv, uother)], axis=1)
        acc[...] += jnp.dot(part, both, preferred_element_type=F32)

    for hop in range(3, nz // 2):
        multiply_pair(hop)
    all_sent(1, ybuf.at[pl.ds(0, ny - 1)])
    all_sent(2, xsend.at[pl.ds(1, nx - 1)])
    all_sent(3, xrelay)
    all_sent(4, parts_in)
    all_sent(5, shrunk.at[pl.ds(0, nz - 1)])
    all_sent(6, ubuf.at[pl.ds(0, ny - 1)])
    all_sent(7, usend.at[pl.ds(1, nx - 1)])
    weights.wait_send()
    first.wait_send()
    ups.wait_send()
    z_step(len(waiting))
    acc[...] += multiply(nz // 2)
    last = pair(3, acc.at[:, pl.ds(cols, cols)], swap_in)
    last.start()
    all_sent(0, abuf.at[pl.ds(0, nz - 1)])
    last.wait_recv()
    out[...] = (acc[:, pl.ds(0, cols)] + swap_in[...]).astype(BF16)
    last.wait_send()


def on_device(nx, ny, nz, act, weight, down, up, home, served, var):
    tokens, depth = act.shape
    cols = weight.shape[1]
    blocks, rank = down.shape[0], down.shape[2]
    groups = nx * ny
    served, var = served.T, var.T
    up = up.reshape(blocks * 4 // 16, 16, cols)
    weight = weight.reshape(nz, 2, depth, cols)
    hbm = pl.BlockSpec(memory_space=pl.ANY)
    vmem = pl.BlockSpec(memory_space=pltpu.VMEM)
    dma = pltpu.SemaphoreType.DMA
    share = tokens // nz
    scratch = [
        pltpu.VMEM((nz, tokens, depth), BF16),
        pltpu.VMEM((nz, depth, cols), BF16),
        pltpu.VMEM((nz, depth, cols), BF16),
        pltpu.VMEM((ny,) + down.shape, BF16),
        pltpu.VMEM((ny,) + up.shape, BF16),
        pltpu.VMEM((2,) + down.shape, BF16),
        pltpu.VMEM((nx, ny, SLOTS, 16, rank), BF16),
        pltpu.VMEM((ny - 1, SLOTS, 16, rank), BF16),
        pltpu.VMEM((ny, nx, SLOTS, 16, rank), BF16),
        pltpu.VMEM((nx, ny, 2, 16, cols), BF16),
        pltpu.VMEM((nx, ny, 2, 16, cols), BF16),
        pltpu.VMEM((nx, ny, 2, 16, cols), BF16),
        pltpu.VMEM((tokens, 2 * cols), F32),
        pltpu.VMEM((PIECES, tokens, rank), F32),
        pltpu.VMEM((tokens, rank), F32),
        pltpu.VMEM((nz, share, rank), F32),
        pltpu.VMEM((nz, share, rank), BF16),
        pltpu.VMEM((nz - 1, share, rank), BF16),
        pltpu.VMEM((nz, share, rank), BF16),
        pltpu.VMEM((tokens, cols), F32),
        pltpu.SMEM((nx * SLOTS,), jnp.int32),
        pltpu.SMEM(home.shape, jnp.int32),
        pltpu.SMEM(served.shape, jnp.int32),
        pltpu.VMEM(var.shape, jnp.int32),
        pltpu.VMEM((tokens, cols), jnp.int32),
        pltpu.VMEM((nx * SLOTS * 4, blocks * 4), BF16),
        pltpu.VMEM((rank, groups * 16), BF16),
        pltpu.VMEM((tokens, depth), BF16),
        pltpu.VMEM((tokens, PIECES * rank), F32),
        dma((7,)),
        dma((2, nz // 2, 4)), dma((2, ny // 2, 4)), dma((2, ny // 2, 2)), dma((ny // 2,)),
        dma((8,)), dma((5,)), dma((4,)), dma((4,)),
    ]
    return pl.pallas_call(
        functools.partial(kernel, nx, ny, nz),
        out_shape=jax.ShapeDtypeStruct((tokens, cols), BF16),
        in_specs=[hbm] * 7,
        out_specs=vmem,
        scratch_shapes=scratch,
        compiler_params=pltpu.CompilerParams(
            collective_id=0, has_side_effects=True, vmem_limit_bytes=56 * 1024 * 1024
        ),
    )(act, weight, down, up, home, served, var)


def solution(mesh):
    nx = 4
    ny, nz = mesh.shape["grp"] // nx, mesh.shape["tp"] // 2
    in_specs = (
        P("grp", "tp"),
        P(None, "tp"),
        P(None, ("tp", "grp"), None),
        P(None, "grp", "tp"),
        P(),
        P(),
        P("grp", None),
    )
    return jax.shard_map(
        functools.partial(on_device, nx, ny, nz),
        mesh=mesh, in_specs=in_specs, out_specs=P("grp", "tp"), check_vma=False,
    )
```
